256 devices in a mesh: rep: 32 (over x_lo, z, core), tp: 8 (over y, x_hi).
Axes of the slice: x: 4 (x_hi: 2, x_lo: 2; x = x_hi * 2 + x_lo), y: 4, z: 8, core: 2. Of those that a mesh axis runs over, the one named last changes fastest.
Arguments:
- kv_cache: bfloat16 [512, 8, 256, 256], P('rep', 'tp'), may hold values from -160 to 160
- lengths: int32 [512], P('rep'), may hold values from 2 to 256, as said below
- departing: int32 [32, 13], P('rep'), may hold values from 0 to 15, as said below
- destination: int32 [32, 13], P('rep'), may hold values from 0 to 31, as said below
- queries: bfloat16 [2, 512, 64, 128], P(None, 'rep', 'tp'), may hold values from -160 to 160
- new_kv: bfloat16 [2, 512, 8, 256], P(None, 'rep', 'tp'), may hold values from -160 to 160
- codes: bfloat16 [2560, 128, 128], P(('tp', 'rep')), may hold values from -6 to 6
- scales: float32 [2560], P(('tp', 'rep')), may hold values from 0.02 to 0.25
- block_slot: int32 [2560], P(('tp', 'rep')), may hold values from 0 to 2559, as said below
Outputs:
- projected: bfloat16 [2, 512, 5120], P(None, 'rep', 'tp')
The draws below stay inside these ranges and needn't reach their ends.
Inputs may be any that keep to these rules, and one draw needn't show every extreme that they name: `lengths`: every slot holds at least two positions, and some slot holds exactly 256. `departing`: each row names 13 different slots. `destination`: in each round every replica is named exactly once and never by itself; no row names a replica twice. `block_slot`: a permutation; the entries at positions of one tp index are exactly that index's consecutive range of 320 block numbers.
All inputs are finite; a program needn't handle non-finite values.
Results may differ from the reference program's by a relative error of at most 0.02.
Values may be sent and summed in bfloat16 or wider, within the bound.
No kernel may reach another device: no remote copies, remote signals or barrier semaphores. Data moves between devices by JAX's collectives and lax.ppermute only.
A program may use at most 64 MiB of HBM per device.

```python
import math
import jax
import jax.numpy as jnp
from jax import lax

D = 5120
H = 64
KVH = 8
HD = 128
STEPS = 2
REQ_DEV = 16
CTX = 256
MOVE = 13
REQS = 512
BLOCKS = 2560
BLK_TP = 320
N_REP = 32
N_TP = 8


def migration_lists(key):
    key = jax.random.fold_in(key, 7)
    first, second, third = jax.random.split(key, 3)
    order = jax.random.permutation(first, N_REP)
    rank = jnp.argsort(order)
    offsets = jax.random.permutation(second, N_REP - 1)[:MOVE] + 1
    heading = order[(rank[:, None] + offsets[None, :]) % N_REP]
    row_keys = jax.random.split(third, N_REP)
    leaving = jax.vmap(lambda row_key: jax.random.permutation(row_key, REQ_DEV)[:MOVE])(row_keys)
    return (leaving.astype(jnp.int32), heading.astype(jnp.int32))


def attention_parts(key):
    key = jax.random.fold_in(key, 41)
    first = jax.random.fold_in(key, 0)
    steer = jax.random.normal(first, (STEPS, REQS, KVH, HD), jnp.float32)
    return steer


def draw_departing(key, part):
    shared = migration_lists(key)
    return shared[0]


def draw_destination(key, part):
    shared = migration_lists(key)
    return shared[1]


def draw_lengths(key, part):
    key = jax.random.fold_in(key, 3)
    first, second, third = jax.random.split(key, 3)
    shifts = jax.random.randint(first, (N_REP,), 0, 4)
    caps = jnp.right_shift(jnp.full((N_REP,), CTX, jnp.int32), shifts)
    raw = jax.random.randint(second, (N_REP, REQ_DEV), 0, 1 << 20)
    result = 2 + raw % (caps[:, None] - 1)
    pick = jax.random.randint(third, (), 0, N_REP * REQ_DEV)
    return result.reshape(-1).at[pick].set(CTX).astype(jnp.int32)


def draw_block_slot(key, part):
    key = jax.random.fold_in(key, 17)
    group_keys = jax.random.split(key, N_TP)
    perms = jax.vmap(lambda group_key: jax.random.permutation(group_key, BLK_TP))(group_keys)
    offsets = jnp.arange(N_TP, dtype=jnp.int32)[:, None] * BLK_TP
    return (perms + offsets).reshape(-1).astype(jnp.int32)


def draw_kv_cache(key, part):
    key = jax.random.fold_in(key, 9)
    shape = (REQS, KVH, CTX, 2 * HD)
    base = jax.random.normal(key, shape, jnp.float32)
    return base.astype(jnp.bfloat16)


def draw_queries(key, part):
    steer = attention_parts(key)
    key = jax.random.fold_in(key, 5)
    shape = (STEPS, REQS, H, HD)
    shared = jnp.repeat(steer, H // KVH, axis=2)
    own = jax.random.normal(key, shape, jnp.float32)
    base = 1.2 * shared + 0.9 * own
    return base.astype(jnp.bfloat16)


def draw_new_kv(key, part):
    steer = attention_parts(key)
    key = jax.random.fold_in(key, 13)
    first, second = jax.random.split(key)
    shape = (STEPS, REQS, KVH, HD)
    noise_keys = jax.random.normal(first, shape, jnp.float32)
    noise_values = jax.random.normal(second, shape, jnp.float32)
    keys = 0.35 * steer + 0.94 * noise_keys
    return jnp.concatenate([keys, noise_values], axis=-1).astype(jnp.bfloat16)


def shard_levels(own_key, extent, pieces, least, top_value):
    gain, own = 1.0, jax.random.fold_in(own_key, 6)
    for dim, blocks in pieces:
        heights = jnp.exp(jax.random.uniform(jax.random.fold_in(own, dim), (blocks,), jnp.float32, least / len(pieces), top_value / len(pieces)))
        gain = gain * jnp.repeat(heights, extent[dim] // blocks).reshape([-1 if axis == dim else 1 for axis in range(len(extent))])
    return gain


def centred(rng, shape, scale, reach, pieces=(), held_as=jnp.bfloat16):
    values = scale * jax.random.normal(rng, shape, jnp.float32)
    if pieces:
        values = values * shard_levels(rng, shape, pieces, -0.22, 0.18)
    return jnp.clip(values, -reach, reach).astype(held_as)


def setup_inputs(seed: int = 0) -> dict:
    streams_of = jax.random.split(jax.random.key(seed), 10)
    return {
        "kv_cache": draw_kv_cache(jax.random.fold_in(streams_of[9], 71), 0),
        "lengths": draw_lengths(jax.random.fold_in(streams_of[9], 71), 0),
        "departing": draw_departing(jax.random.fold_in(streams_of[9], 71), 0),
        "destination": draw_destination(jax.random.fold_in(streams_of[9], 71), 0),
        "queries": draw_queries(jax.random.fold_in(streams_of[9], 71), 0),
        "new_kv": draw_new_kv(jax.random.fold_in(streams_of[9], 71), 0),
        "codes": centred(streams_of[6], (BLOCKS, HD, HD), 1.0, 6.0, ((0, 256),)),
        "scales": jnp.clip(jnp.exp(math.log(0.25) - 2.5257287 * jax.random.uniform(streams_of[7], (BLOCKS,), jnp.float32) ** shard_levels(streams_of[7], (BLOCKS,), ((0, 256),), -0.2, 0.2)), 0.02, 0.25),
        "block_slot": draw_block_slot(jax.random.fold_in(streams_of[9], 71), 0),
    }


def slot_attention(cache, length, query, fresh):
    steps, heads, width = query.shape
    groups = cache.shape[0]
    grouped = query.reshape(steps, groups, heads // groups, width).astype(jnp.float32)
    keys = cache[:, :, :width].astype(jnp.float32)
    values = cache[:, :, width:].astype(jnp.float32)
    scale_factor = 1.0 / math.sqrt(width)
    scores = jnp.einsum('sgqd,gpd->sgqp', grouped, keys) * scale_factor
    valid = jnp.arange(cache.shape[1], dtype=jnp.int32) < length
    scores = jnp.where(valid, scores, -jnp.inf)
    top = lax.optimization_barrier(jnp.max(scores, axis=-1))
    expo = jnp.where(valid, jnp.exp(scores - top[..., None]), 0.0)
    total = lax.optimization_barrier(jnp.sum(expo, axis=-1))
    rounded = lax.optimization_barrier(expo.astype(jnp.bfloat16)).astype(jnp.float32)
    carried = jnp.einsum('sgqp,gpd->sgqd', rounded, values)
    fresh_keys = fresh[:, :, :width].astype(jnp.float32)
    fresh_values = fresh[:, :, width:].astype(jnp.float32)
    extra = jnp.einsum('sgqd,ugd->sgqu', grouped, fresh_keys) * scale_factor
    allowed = (jnp.arange(steps)[None, :] <= jnp.arange(steps)[:, None])[:, None, None, :]
    extra = jnp.where(allowed, extra, -jnp.inf)
    peak = jnp.maximum(top, lax.optimization_barrier(jnp.max(extra, axis=-1)))
    factor = jnp.exp(top - peak)
    weights = jnp.where(allowed, jnp.exp(extra - peak[..., None]), 0.0)
    denom = total * factor + lax.optimization_barrier(jnp.sum(weights, axis=-1))
    numer = carried * factor[..., None] + jnp.einsum('sgqu,ugd->sgqd', weights, fresh_values)
    return (numer / denom[..., None]).astype(jnp.bfloat16).reshape(steps, heads * width)

def reference(kv_cache, lengths, departing, destination, queries, new_kv, codes, scales, block_slot):
    rounds = jnp.arange(departing.shape[1], dtype=jnp.int32)[None, :]
    arrive = destination * REQ_DEV + departing[destination, rounds]
    leave = jnp.arange(N_REP, dtype=jnp.int32)[:, None] * REQ_DEV + departing
    root = jnp.arange(REQS, dtype=jnp.int32).at[arrive.reshape(-1).astype(jnp.int32)].set(leave.reshape(-1).astype(jnp.int32))

    def one_slot(item):
        index, query, fresh = item
        return slot_attention(kv_cache[index], lengths[index], query, fresh)
    attended = lax.map(one_slot, (root, jnp.swapaxes(queries, 0, 1), jnp.swapaxes(new_kv, 0, 1)))
    blocks = (codes.astype(jnp.float32) * scales[:, None, None]).astype(jnp.bfloat16)
    placed = jnp.zeros_like(blocks).at[block_slot.astype(jnp.int32)].set(blocks)
    matrix = placed.reshape(H, D // HD, HD, HD).transpose(0, 2, 1, 3).reshape(H * HD, D)
    rows = jnp.swapaxes(attended, 0, 1).reshape(STEPS * REQS, H * HD)
    result = jnp.dot(rows, matrix, preferred_element_type=jnp.float32)
    return result.astype(jnp.bfloat16).reshape(STEPS, REQS, D)
```

```python
import math

import jax
import jax.numpy as jnp
from jax import lax
from jax.experimental import pallas as pl
from jax.experimental.pallas import tpu as pltpu
from jax.sharding import Mesh, PartitionSpec as P

BF16, F32, I32 = jnp.bfloat16, jnp.float32, jnp.int32

XL, Z, CORE, TP = 2, 8, 2, 8
REP = XL * Z * CORE

HD = 128
SLOTS = 16
STEPS = 2
HEADS = 8
CTX = 256
MOVE = 13
STAY = SLOTS - MOVE
COLS = 40
OUT_COLS = COLS // TP
OWN = 10
ROWS = SLOTS * STEPS
PACK = STEPS * HEADS + 2 * STEPS

ROUND, HEAD, COL, SCALE, DEP, DEST = 0, 1, 11, 21, 32, 48

VMEM_LIMIT = 40 * 1024 * 1024


def smem():
    return pl.BlockSpec(memory_space=pltpu.SMEM)


def vmem():
    return pl.BlockSpec(memory_space=pltpu.VMEM)


def call(body, out_shape, in_specs, scratch=(), **kw):
    single = not isinstance(out_shape, (list, tuple))
    return pl.pallas_call(
        body,
        out_shape=out_shape,
        in_specs=in_specs,
        out_specs=vmem() if single else [vmem()] * len(out_shape),
        scratch_shapes=list(scratch),
        compiler_params=pltpu.CompilerParams(vmem_limit_bytes=VMEM_LIMIT),
        **kw,
    )


def notice_body(place, dep, dest, ids, scales, queries, fresh, notice, packs):
    row = lax.broadcasted_iota(I32, (REP, HD), 0)
    lane = lax.broadcasted_iota(I32, (REP, HD), 1)
    base = place[0]
    out = jnp.full((REP, HD), -1.0, F32)
    for k in range(MOVE):
        out = jnp.where((lane == ROUND) & (row == dest[0, k]), float(k), out)
        out = jnp.where(lane == DEP + k, dep[0, k].astype(F32), out)
        out = jnp.where(lane == DEST + k, dest[0, k].astype(F32), out)
    for n in range(OWN):
        place_n = ids[n] - base
        head = lax.div(place_n, COLS)
        out = jnp.where(lane == HEAD + n, head.astype(F32), out)
        out = jnp.where(lane == COL + n, (place_n - head * COLS).astype(F32), out)
        out = jnp.where(lane == SCALE + n, scales[n], out)
    notice[:, 0, :] = out
    for s in range(SLOTS):
        packs[s] = jnp.concatenate(
            [queries[t, s] for t in range(STEPS)]
            + [fresh[t, s, :, j * HD : (j + 1) * HD] for t in range(STEPS) for j in range(2)],
            axis=0,
        )


def pull_body(notices, dep, packs, out):
    def one(peer, carry):
        turn = notices[peer, 0, ROUND].astype(I32)
        slot = dep[0, jnp.maximum(turn, 0)]
        out[peer] = packs[slot]
        return carry

    lax.fori_loop(0, REP, one, 0, unroll=4)


def attend_body(lengths, dep, dest, pulled, packs, cache, out, work, scores, held):
    scale = 1.0 / math.sqrt(HD)
    per = STEPS * HEADS
    for s in range(SLOTS):
        held[s] = packs[s]

    def fetch(k, c):
        held[dep[0, k]] = pulled[dest[0, k]]
        return c

    lax.fori_loop(0, MOVE, fetch, 0, unroll=True)
    for s in range(SLOTS):
        q = held[s][:per]
        sc = lax.dot_general(
            q, cache[s, 0, :, :HD], (((1,), (1,)), ((), ())), preferred_element_type=F32
        )
        pos = lax.broadcasted_iota(I32, (per, CTX), 1)
        scores[s] = jnp.where(pos < lengths[s], sc * scale, -jnp.inf)
    step = lax.broadcasted_iota(I32, (per, 1), 0) // HEADS
    for s in range(SLOTS):
        sc = scores[s]
        top = jnp.max(sc, axis=1, keepdims=True)
        expo = jnp.exp(sc - top)
        total = jnp.sum(expo, axis=1, keepdims=True)
        carried = jnp.dot(expo.astype(BF16), cache[s, 0, :, HD:], preferred_element_type=F32)
        pack = held[s].astype(F32)
        q = pack[:per]
        peak = top
        extra = []
        for u in range(STEPS):
            f = jnp.sum(q * pack[per + 2 * u : per + 2 * u + 1], axis=1, keepdims=True) * scale
            f = jnp.where(step >= u, f, -jnp.inf)
            extra.append(f)
            peak = jnp.maximum(peak, f)
        factor = jnp.exp(top - peak)
        denom = total * factor
        numer = carried * factor
        for u in range(STEPS):
            w = jnp.exp(extra[u] - peak)
            denom = denom + w
            numer = numer + w * pack[per + 2 * u + 1 : per + 2 * u + 2]
        work[pl.ds(s * per, per), :] = numer / denom
    for h in range(HEADS):
        for t in range(STEPS):
            out[h, t * SLOTS : (t + 1) * SLOTS, :] = work[
                pl.ds(t * HEADS + h, SLOTS, stride=per), :
            ].astype(BF16)


def project_body(place, notices, mine, other, *rest):
    arrays, out, rows, total = rest[:-3], rest[-3], rest[-2], rest[-1]
    xl, z, core = place[1], place[2], place[3]
    rows[:, :ROWS, :] = mine[...]
    rows[:, ROWS:, :] = other[...]
    total[...] = jnp.zeros_like(total)
    away = 1 - 2 * core

    def run(blocks, first, z_src, core_src):
        src = (xl * Z + z_src) * CORE + core_src
        for lo in range(0, OWN, 5):
            products = []
            for n in range(lo, lo + 5):
                h = notices[src, 0, HEAD + n].astype(I32)
                products.append(
                    jnp.dot(rows[h], blocks[first + n], preferred_element_type=F32)
                    * notices[src, 0, SCALE + n]
                )
            for n in range(lo, lo + 5):
                c = notices[src, 0, COL + n].astype(I32)
                total[c] += products[n - lo]

    run(arrays[0], 0, z, core)
    run(arrays[1], 0, z, 1 - core)
    for step in range(1, Z // 2):
        from_z = lax.rem(z - away * step + Z, Z)
        sib_z = lax.rem(z + away * step + Z, Z)
        a, b = arrays[2 * step], arrays[2 * step + 1]
        run(a, 0, from_z, core)
        run(a, OWN, from_z, 1 - core)
        run(b, 0, sib_z, 1 - core)
        run(b, OWN, sib_z, core)
    far = lax.rem(z + Z // 2, Z)
    run(arrays[Z], 0, far, core)
    run(arrays[Z + 1], 0, far, 1 - core)
    out[...] = total[...].astype(BF16)


def sum_body(place, notices, parts, send, stay, keep, total):
    rep, pair = place[4], place[5]
    for c in range(OUT_COLS):
        acc = parts[0, c].astype(F32)
        for t in range(1, TP):
            acc = acc + parts[t, c].astype(F32)
        total[:, c * HD : (c + 1) * HD] = acc.astype(BF16)
    row = lax.broadcasted_iota(I32, (REP * 8, 1), 0)
    goal, part = lax.div(row, 8), lax.rem(row, 8)
    side, step = lax.div(part, STEPS), lax.rem(part, STEPS)
    want = jnp.full((REP * 8, 1), -1, I32)
    for s, owner in ((0, rep), (1, pair)):
        for k in range(MOVE):
            slot = notices[owner, 0, DEP + k].astype(I32)
            dest = notices[owner, 0, DEST + k].astype(I32)
            want = jnp.where((goal == dest) & (side == s), slot, want)
    want = jnp.where(want >= 0, side * ROWS + step * SLOTS + want, -1)
    col = lax.broadcasted_iota(I32, (REP * 8, XL * ROWS), 1)
    pick = jnp.where(col == want, 1.0, 0.0).astype(BF16)
    packed = jnp.dot(pick, total[...], preferred_element_type=F32)
    send[...] = packed.reshape(REP, 8, OUT_COLS * HD)[:, : 2 * STEPS, :].astype(BF16)
    keep[...] = total[:ROWS, :]
    stay[...] = total[ROWS:, :]


def finish_body(place, notices, dep, moved, keep, stay, out, arrived):
    arrived[:, : 2 * STEPS, :] = moved[...].astype(F32)
    arrived[:, 2 * STEPS :, :] = jnp.zeros_like(arrived[:, 2 * STEPS :, :])
    rows = arrived[...].reshape(REP * 8, OUT_COLS * HD).astype(BF16)
    lane = lax.broadcasted_iota(I32, (1, REP * 8), 1)
    peer, part = lax.div(lane, 8), lax.rem(lane, 8)
    side, step = lax.div(part, STEPS), lax.rem(part, STEPS)
    peer = lax.rem(peer + side * (REP // XL), REP)
    slot = jnp.full((1, REP * 8), -1, I32)
    for p in range(REP):
        turn = notices[p, 0, ROUND].astype(I32)
        mine = jnp.where(turn >= 0, dep[0, jnp.maximum(turn, 0)], -1)
        slot = jnp.where(peer == p, mine, slot)
    slot = jnp.where((slot >= 0) & (part < 2 * STEPS), slot + step * SLOTS, -1)
    row = lax.broadcasted_iota(I32, (ROWS, REP * 8), 0)
    pick = jnp.where(row == slot, 1.0, 0.0).astype(BF16)
    came = jnp.dot(pick, rows, preferred_element_type=F32)
    here = lax.rem(lax.broadcasted_iota(I32, (ROWS, 1), 0), SLOTS)
    left = jnp.zeros((ROWS, 1), jnp.bool_)
    for k in range(MOVE):
        left = left | (here == dep[0, k])
    both = keep[...].astype(F32) + stay[...].astype(F32)
    result = jnp.where(left, came, both).astype(BF16)
    for t in range(STEPS):
        out[t] = result[t * SLOTS : (t + 1) * SLOTS]


def shards(kv_cache, lengths, departing, destination, queries, new_kv, codes, scales, block_slot):
    rep_axes, tp_axes = ("xl", "z", "core"), ("y", "xh")
    xl, z, core = (lax.axis_index(a) for a in rep_axes)
    rep = lax.axis_index(rep_axes)
    base = lax.axis_index(tp_axes) * (HEADS * COLS)
    place = jnp.stack([base, xl, z, core, rep, (rep + REP // XL) % REP]).astype(I32)

    def exchange(x, axes):
        return lax.all_to_all(x, axes, split_axis=0, concat_axis=0, tiled=True)

    def swap(x, axis):
        return lax.ppermute(x, axis, [(0, 1), (1, 0)])

    ring = [
        (i * CORE + c, ((i + (1 - 2 * c)) % Z) * CORE + c) for i in range(Z) for c in range(CORE)
    ]

    sib = swap(codes, "core")
    notice, packs = call(
        notice_body,
        [
            jax.ShapeDtypeStruct((REP, 1, HD), F32),
            jax.ShapeDtypeStruct((SLOTS, PACK, HD), BF16),
        ],
        [smem()] * 5 + [vmem()] * 2,
    )(place, departing, destination, block_slot, scales, queries, new_kv)
    pair = jnp.concatenate([codes, sib], axis=0)

    one = lax.ppermute(pair, ("z", "core"), ring)
    notices = exchange(notice, rep_axes)

    one, notices = lax.optimization_barrier((one, notices))
    two = lax.ppermute(one, ("z", "core"), ring)
    one_sib = swap(one, "core")
    to_pull = call(
        pull_body,
        jax.ShapeDtypeStruct((REP, PACK, HD), BF16),
        [smem(), smem(), vmem()],
    )(notices, departing, packs)
    pulled = exchange(to_pull, rep_axes)

    two, pulled = lax.optimization_barrier((two, pulled))
    three = lax.ppermute(two, ("z", "core"), ring)
    two_sib = swap(two, "core")
    mine = call(
        attend_body,
        jax.ShapeDtypeStruct((HEADS, ROWS, HD), BF16),
        [smem()] * 3 + [vmem()] * 3,
        [
            pltpu.VMEM((SLOTS * STEPS * HEADS, HD), F32),
            pltpu.VMEM((SLOTS, STEPS * HEADS, CTX), F32),
            pltpu.VMEM((SLOTS, PACK, HD), BF16),
        ],
    )(lengths, departing, destination, pulled, packs, kv_cache)
    three, mine = lax.optimization_barrier((three, mine))
    four = lax.ppermute(three[:OWN], ("z", "core"), ring)
    three_sib = swap(three, "core")
    other = swap(mine, "xl")
    four_sib = swap(four, "core")
    arrays = [codes, sib, one, one_sib, two, two_sib, three, three_sib, four, four_sib]
    parts = call(
        project_body,
        jax.ShapeDtypeStruct((COLS, XL * ROWS, HD), BF16),
        [smem()] * 2 + [vmem()] * (2 + len(arrays)),
        [
            pltpu.VMEM((HEADS, XL * ROWS, HD), BF16),
            pltpu.VMEM((COLS, XL * ROWS, HD), F32),
        ],
    )(place, notices, mine, other, *arrays)
    parts = exchange(parts, tp_axes).reshape(TP, OUT_COLS, XL * ROWS, HD)
    send, stay, keep = call(
        sum_body,
        [
            jax.ShapeDtypeStruct((REP, 2 * STEPS, OUT_COLS * HD), BF16),
            jax.ShapeDtypeStruct((ROWS, OUT_COLS * HD), BF16),
            jax.ShapeDtypeStruct((ROWS, OUT_COLS * HD), BF16),
        ],
        [smem()] * 2 + [vmem()],
        [pltpu.VMEM((XL * ROWS, OUT_COLS * HD), BF16)],
    )(place, notices, parts)
    stay = swap(stay, "xl")
    moved = exchange(send, rep_axes)
    return call(
        finish_body,
        jax.ShapeDtypeStruct((STEPS, SLOTS, OUT_COLS * HD), BF16),
        [smem()] * 3 + [vmem()] * 3,
        [pltpu.VMEM((REP, 8, OUT_COLS * HD), F32)],
    )(place, notices, departing, moved, keep, stay)


def solution(mesh):
    rep, tp = ("xl", "z", "core"), ("y", "xh")
    parts = Mesh(mesh.devices.reshape(XL, Z, CORE, 4, 2), rep + tp)
    placed = (
        P(rep, tp, None, None),
        P(rep),
        P(rep, None),
        P(rep, None),
        P(None, rep, tp, None),
        P(None, rep, tp, None),
        P(tp + rep, None, None),
        P(tp + rep),
        P(tp + rep),
    )
    return jax.shard_map(
        shards, mesh=parts, in_specs=placed, out_specs=P(None, rep, tp), check_vma=False
    )
```

```python
import math

import jax
import jax.numpy as jnp
from jax import lax
from jax.experimental import pallas as pl
from jax.experimental.pallas import tpu as pltpu
from jax.sharding import Mesh, PartitionSpec as P

BF16, F32, I32 = jnp.bfloat16, jnp.float32, jnp.int32

XL, Z, CORE, TP = 2, 8, 2, 8
REP = XL * Z * CORE

HD = 128
SLOTS = 16
STEPS = 2
HEADS = 8
CTX = 256
MOVE = 13
STAY = SLOTS - MOVE
COLS = 40
OUT_COLS = COLS // TP
OWN = 10
ROWS = SLOTS * STEPS
PACK = STEPS * HEADS + 2 * STEPS

ROUND, PAIR_ROUND, ME, HEAD, COL, SCALE, DEP, DEST, LEN = 0, 1, 2, 3, 13, 23, 33, 46, 59

VMEM_LIMIT = 40 * 1024 * 1024


def smem():
    return pl.BlockSpec(memory_space=pltpu.SMEM)


def vmem():
    return pl.BlockSpec(memory_space=pltpu.VMEM)


def hbm():
    return pl.BlockSpec(memory_space=pltpu.HBM)


def call(body, out_shape, in_specs, scratch=(), **kw):
    single = not isinstance(out_shape, (list, tuple))
    return pl.pallas_call(
        body,
        out_shape=out_shape,
        in_specs=in_specs,
        out_specs=vmem() if single else [vmem()] * len(out_shape),
        scratch_shapes=list(scratch),
        compiler_params=pltpu.CompilerParams(vmem_limit_bytes=VMEM_LIMIT),
        **kw,
    )


def copy_in(pairs, sems):
    copies = [pltpu.make_async_copy(a, b, sems.at[i]) for i, (a, b) in enumerate(pairs)]
    for c in copies:
        c.start()
    for c in copies:
        c.wait()


def notice_body(place, *refs):
    given, (notice, packs), held, sems = refs[:7], refs[7:9], refs[9:16], refs[16]
    copy_in(zip(given, held), sems)
    dep, dest, lengths, ids, scales, queries, fresh = held
    row = lax.broadcasted_iota(I32, (REP, HD), 0)
    lane = lax.broadcasted_iota(I32, (REP, HD), 1)
    base = place[0]
    pair_row = lax.rem(row + REP // XL, REP)
    out = jnp.where(lane == ME, row, -1).astype(F32)
    for k in range(MOVE):
        out = jnp.where((lane == ROUND) & (row == dest[0, k]), float(k), out)
        out = jnp.where((lane == PAIR_ROUND) & (pair_row == dest[0, k]), float(k), out)
        out = jnp.where(lane == DEP + k, dep[0, k].astype(F32), out)
        out = jnp.where(lane == DEST + k, dest[0, k].astype(F32), out)
    for n in range(OWN):
        place_n = ids[n] - base
        head = lax.div(place_n, COLS)
        out = jnp.where(lane == HEAD + n, head.astype(F32), out)
        out = jnp.where(lane == COL + n, (place_n - head * COLS).astype(F32), out)
        out = jnp.where(lane == SCALE + n, scales[n], out)
    for s in range(SLOTS):
        out = jnp.where(lane == LEN + s, lengths[s].astype(F32), out)
    notice[:, 0, :] = out
    for s in range(SLOTS):
        packs[s] = jnp.concatenate(
            [queries[t, s] for t in range(STEPS)]
            + [fresh[t, s : s + 1, j * HD : (j + 1) * HD] for t in range(STEPS) for j in range(2)],
            axis=0,
        )


def join_body(first, second, out, sems):
    copy_in([(first, out.at[:OWN]), (second, out.at[OWN:])], sems)


def at(notices, rep, lane):
    return notices[rep, 0, lane].astype(I32)


def pull_body(notices, packs, out):
    me = at(notices, 0, ME)

    def one(peer, carry):
        turn = at(notices, peer, ROUND)
        out[peer] = packs[at(notices, me, DEP + jnp.maximum(turn, 0))]
        return carry

    lax.fori_loop(0, REP, one, 0, unroll=4)


def attend_body(notices, pulled, packs, cache, send, out, scores, held):
    scale = 1.0 / math.sqrt(HD)
    per = STEPS * HEADS
    me = at(notices, 0, ME)
    for s in range(SLOTS):
        held[s] = packs[s]
    for k in range(MOVE):
        held[at(notices, me, DEP + k)] = pulled[at(notices, me, DEST + k)]
    pos = lax.broadcasted_iota(I32, (per, CTX), 1)
    for s in range(SLOTS):
        q = held[s][:per]
        sc = lax.dot_general(
            q, cache[s, 0, :, :HD], (((1,), (1,)), ((), ())), preferred_element_type=F32
        )
        scores[s] = jnp.where(pos < at(notices, me, LEN + s), sc * scale, -jnp.inf)
    step = lax.broadcasted_iota(I32, (per, 1), 0) // HEADS
    for s in range(SLOTS):
        sc = scores[s]
        top = jnp.max(sc, axis=1, keepdims=True)
        expo = jnp.exp(sc - top)
        total = jnp.sum(expo, axis=1, keepdims=True)
        carried = jnp.dot(expo.astype(BF16), cache[s, 0, :, HD:], preferred_element_type=F32)
        pack = held[s].astype(F32)
        q = pack[:per]
        peak = top
        extra = []
        for u in range(STEPS):
            f = jnp.sum(q * pack[per + 2 * u : per + 2 * u + 1], axis=1, keepdims=True) * scale
            f = jnp.where(step >= u, f, -jnp.inf)
            extra.append(f)
            peak = jnp.maximum(peak, f)
        factor = jnp.exp(top - peak)
        denom = total * factor
        numer = carried * factor
        for u in range(STEPS):
            w = jnp.exp(extra[u] - peak)
            denom = denom + w
            numer = numer + w * pack[per + 2 * u + 1 : per + 2 * u + 2]
        out[s] = (numer / denom).astype(BF16)
    for k in range(MOVE):
        goal = at(notices, me, DEST + k)
        rows = out[at(notices, me, DEP + k)]
        send[goal, :per, :] = rows
        send[lax.rem(goal + REP // XL, REP), per:, :] = rows


def project_body(notices, came, mine, other, *rest):
    arrays, out, slots, rows, total = rest[:-4], rest[-4], rest[-3], rest[-2], rest[-1]
    per = STEPS * HEADS
    me = at(notices, 0, ME)
    pair = lax.rem(me + REP // XL, REP)
    xl, z, core = lax.div(me, Z * CORE), lax.rem(lax.div(me, CORE), Z), lax.rem(me, CORE)
    first, second = xl * SLOTS, (1 - xl) * SLOTS
    for s in range(SLOTS):
        slots[pl.ds(pl.multiple_of((first + s) * per, per), per), :] = mine[s].astype(F32)
        slots[pl.ds(pl.multiple_of((second + s) * per, per), per), :] = other[s].astype(F32)

    def place_rows(peer, carry):
        for lane, owner, start, lo in ((ROUND, me, first, 0), (PAIR_ROUND, pair, second, per)):
            turn = at(notices, peer, lane)
            slot = start + at(notices, owner, DEP + jnp.maximum(turn, 0))
            goal = jnp.where(turn >= 0, slot, XL * SLOTS)
            slots[pl.ds(pl.multiple_of(goal * per, per), per), :] = came[
                peer, lo : lo + per, :
            ].astype(F32)
        return carry

    lax.fori_loop(0, REP, place_rows, 0, unroll=4)
    for h in range(HEADS):
        for side in range(XL):
            for t in range(STEPS):
                lo = side * ROWS + t * SLOTS
                rows[h, lo : lo + SLOTS, :] = slots[
                    pl.ds(side * SLOTS * per + t * HEADS + h, SLOTS, stride=per), :
                ].astype(BF16)
    total[...] = jnp.zeros_like(total)
    away = 1 - 2 * core

    def run(blocks, first, z_src, core_src):
        src = (xl * Z + z_src) * CORE + core_src
        for lo in range(0, OWN, 5):
            products = []
            for n in range(lo, lo + 5):
                products.append(
                    jnp.dot(
                        rows[at(notices, src, HEAD + n)],
                        blocks[first + n],
                        preferred_element_type=F32,
                    )
                    * notices[src, 0, SCALE + n]
                )
            for n in range(lo, lo + 5):
                total[at(notices, src, COL + n)] += products[n - lo]

    run(arrays[0], 0, z, core)
    run(arrays[0], OWN, z, 1 - core)
    for step in range(1, Z // 2):
        from_z = lax.rem(z - away * step + Z, Z)
        sib_z = lax.rem(z + away * step + Z, Z)
        a, b = arrays[2 * step - 1], arrays[2 * step]
        run(a, 0, from_z, core)
        run(a, OWN, from_z, 1 - core)
        run(b, 0, sib_z, 1 - core)
        run(b, OWN, sib_z, core)
    far = lax.rem(z + Z // 2, Z)
    run(arrays[Z - 1], 0, far, core)
    run(arrays[Z], 0, far, 1 - core)
    out[:COLS] = total[:, :ROWS, :].astype(BF16)
    out[COLS:] = total[:, ROWS:, :].astype(BF16)


def sum_body(parts, out):
    for c in range(OUT_COLS):
        acc = parts[0, c].astype(F32)
        for t in range(1, XL * TP):
            acc = acc + parts[t, c].astype(F32)
        acc = acc.astype(BF16)
        for t in range(STEPS):
            out[t, :, c * HD : (c + 1) * HD] = acc[t * SLOTS : (t + 1) * SLOTS, :]


def shards(kv_cache, lengths, departing, destination, queries, new_kv, codes, scales, block_slot):
    rep_axes, tp_axes = ("xl", "z", "core"), ("y", "xh")
    base = lax.axis_index(tp_axes) * (HEADS * COLS)
    per = STEPS * HEADS

    def in_hbm(x):
        return pltpu.with_memory_space_constraint(x, pltpu.HBM)

    def exchange(x, axes):
        return lax.all_to_all(x, axes, split_axis=0, concat_axis=0, tiled=True)

    def swap(x, axis):
        return lax.ppermute(x, axis, [(0, 1), (1, 0)])

    def around(x, hops):
        pairs = [
            (i * CORE + c, ((i + hops * (1 - 2 * c)) % Z) * CORE + c)
            for i in range(Z)
            for c in range(CORE)
        ]
        return lax.ppermute(x, ("z", "core"), pairs)

    sib = swap(codes, "core")
    given = [
        departing,
        destination,
        lengths,
        block_slot,
        scales,
        queries,
        new_kv.reshape(STEPS, SLOTS, 2 * HD),
    ]
    notice, packs = call(
        notice_body,
        [
            jax.ShapeDtypeStruct((REP, 1, HD), F32),
            jax.ShapeDtypeStruct((SLOTS, PACK, HD), BF16),
        ],
        [smem()] + [hbm()] * len(given),
        [pltpu.SMEM(a.shape, a.dtype) for a in given[:5]]
        + [pltpu.VMEM(a.shape, a.dtype) for a in given[5:]]
        + [pltpu.SemaphoreType.DMA((len(given),))],
    )(base.astype(I32)[None], *(in_hbm(a) for a in given))
    own = call(
        join_body,
        jax.ShapeDtypeStruct((CORE * OWN, HD, HD), BF16),
        [pl.BlockSpec(memory_space=pl.ANY)] * 2,
        [pltpu.SemaphoreType.DMA((2,))],
    )(in_hbm(codes), sib)

    one = around(own, 1)
    notices = exchange(notice, rep_axes)
    one, notices = lax.optimization_barrier((one, notices))

    two = around(one, 1)
    one_sib = swap(one, "core")
    to_pull = call(
        pull_body, jax.ShapeDtypeStruct((REP, PACK, HD), BF16), [smem(), vmem()]
    )(notices, packs)
    pulled = exchange(to_pull, rep_axes)
    two, pulled = lax.optimization_barrier((two, pulled))

    four = around(two[:OWN], 2)
    three = around(two, 1)
    two_sib = swap(two, "core")
    send, mine = call(
        attend_body,
        [
            jax.ShapeDtypeStruct((REP, 2 * per, HD), BF16),
            jax.ShapeDtypeStruct((SLOTS, per, HD), BF16),
        ],
        [smem()] + [vmem()] * 3,
        [pltpu.VMEM((SLOTS, per, CTX), F32), pltpu.VMEM((SLOTS, PACK, HD), BF16)],
    )(notices, pulled, packs, kv_cache)
    other = swap(mine, "xl")
    came = exchange(send, rep_axes)
    three, four, came, other = lax.optimization_barrier((three, four, came, other))
    arrays = [own, one, one_sib, two, two_sib, three, swap(three, "core"), four, swap(four, "core")]
    parts = call(
        project_body,
        jax.ShapeDtypeStruct((XL * COLS, ROWS, HD), BF16),
        [smem()] + [vmem()] * (3 + len(arrays)),
        [
            pltpu.VMEM(((XL * SLOTS + 1) * per, HD), F32),
            pltpu.VMEM((HEADS, XL * ROWS, HD), BF16),
            pltpu.VMEM((COLS, XL * ROWS, HD), F32),
        ],
    )(notices, came, mine, other, *arrays)
    parts = exchange(parts, ("xl",) + tp_axes).reshape(XL * TP, OUT_COLS, ROWS, HD)
    return call(
        sum_body, jax.ShapeDtypeStruct((STEPS, SLOTS, OUT_COLS * HD), BF16), [vmem()]
    )(parts)


def solution(mesh):
    rep, tp = ("xl", "z", "core"), ("y", "xh")
    parts = Mesh(mesh.devices.reshape(XL, Z, CORE, 4, 2), rep + tp)
    placed = (
        P(rep, tp, None, None),
        P(rep),
        P(rep, None),
        P(rep, None),
        P(None, rep, tp, None),
        P(None, rep, tp, None),
        P(tp + rep, None, None),
        P(tp + rep),
        P(tp + rep),
    )
    return jax.shard_map(
        shards, mesh=parts, in_specs=placed, out_specs=P(None, rep, tp), check_vma=False
    )
```

```python
import math

import jax
import jax.numpy as jnp
from jax import lax
from jax.experimental import pallas as pl
from jax.experimental.pallas import tpu as pltpu
from jax.sharding import Mesh, PartitionSpec as P

BF16, F32, I32 = jnp.bfloat16, jnp.float32, jnp.int32

XL, Z, CORE, TP = 2, 8, 2, 8
REP = XL * Z * CORE

HD = 128
SLOTS = 16
STEPS = 2
HEADS = 8
CTX = 256
MOVE = 13
STAY = SLOTS - MOVE
COLS = 40
OUT_COLS = COLS // TP
OWN = 10
ROWS = SLOTS * STEPS
PACK = STEPS * HEADS + 2 * STEPS

ROUND, PAIR_ROUND, ME, HEAD, COL, SCALE, DEP, DEST, LEN = 0, 1, 2, 3, 13, 23, 33, 46, 59

VMEM_LIMIT = 40 * 1024 * 1024


def smem():
    return pl.BlockSpec(memory_space=pltpu.SMEM)


def vmem():
    return pl.BlockSpec(memory_space=pltpu.VMEM)


def hbm():
    return pl.BlockSpec(memory_space=pltpu.HBM)


def call(body, out_shape, in_specs, scratch=(), **kw):
    single = not isinstance(out_shape, (list, tuple))
    return pl.pallas_call(
        body,
        out_shape=out_shape,
        in_specs=in_specs,
        out_specs=vmem() if single else [vmem()] * len(out_shape),
        scratch_shapes=list(scratch),
        compiler_params=pltpu.CompilerParams(vmem_limit_bytes=VMEM_LIMIT),
        **kw,
    )


def copy_in(pairs, sems):
    copies = [pltpu.make_async_copy(a, b, sems.at[i]) for i, (a, b) in enumerate(pairs)]
    for c in copies:
        c.start()
    for c in copies:
        c.wait()


def notice_body(place, *refs):
    given, (notice, packs), held, sems = refs[:7], refs[7:9], refs[9:16], refs[16]
    copy_in(zip(given, held), sems)
    dep, dest, lengths, ids, scales, queries, fresh = held
    row = lax.broadcasted_iota(I32, (REP, HD), 0)
    lane = lax.broadcasted_iota(I32, (REP, HD), 1)
    base = place[0]
    pair_row = lax.rem(row + REP // XL, REP)
    out = jnp.where(lane == ME, row, -1).astype(F32)
    for k in range(MOVE):
        out = jnp.where((lane == ROUND) & (row == dest[0, k]), float(k), out)
        out = jnp.where((lane == PAIR_ROUND) & (pair_row == dest[0, k]), float(k), out)
        out = jnp.where(lane == DEP + k, dep[0, k].astype(F32), out)
        out = jnp.where(lane == DEST + k, dest[0, k].astype(F32), out)
    for n in range(OWN):
        place_n = ids[n] - base
        head = lax.div(place_n, COLS)
        out = jnp.where(lane == HEAD + n, head.astype(F32), out)
        out = jnp.where(lane == COL + n, (place_n - head * COLS).astype(F32), out)
        out = jnp.where(lane == SCALE + n, scales[n], out)
    for s in range(SLOTS):
        out = jnp.where(lane == LEN + s, lengths[s].astype(F32), out)
    notice[:, 0, :] = out
    for s in range(SLOTS):
        packs[s] = jnp.concatenate(
            [queries[t, s] for t in range(STEPS)]
            + [fresh[t, s : s + 1, j * HD : (j + 1) * HD] for t in range(STEPS) for j in range(2)],
            axis=0,
        )


def join_body(first, second, out, sems):
    copy_in([(first, out.at[:OWN]), (second, out.at[OWN:])], sems)


def at(notices, rep, lane):
    return notices[rep, 0, lane].astype(I32)


def pull_body(notices, packs, out):
    me = at(notices, 0, ME)

    def one(peer, carry):
        turn = at(notices, peer, ROUND)
        out[peer] = packs[at(notices, me, DEP + jnp.maximum(turn, 0))]
        return carry

    lax.fori_loop(0, REP, one, 0, unroll=4)


def attend_body(notices, pulled, packs, cache, send, out, scores, held):
    scale = 1.0 / math.sqrt(HD)
    per = STEPS * HEADS
    me = at(notices, 0, ME)
    for s in range(SLOTS):
        held[s] = packs[s]
    for k in range(MOVE):
        held[at(notices, me, DEP + k)] = pulled[at(notices, me, DEST + k)]
    pos = lax.broadcasted_iota(I32, (per, CTX), 1)
    for s in range(SLOTS):
        q = held[s][:per]
        sc = lax.dot_general(
            q, cache[s, 0, :, :HD], (((1,), (1,)), ((), ())), preferred_element_type=F32
        )
        scores[s] = jnp.where(pos < at(notices, me, LEN + s), sc * scale, -jnp.inf)
    step = lax.broadcasted_iota(I32, (per, 1), 0) // HEADS
    for s in range(SLOTS):
        sc = scores[s]
        top = jnp.max(sc, axis=1, keepdims=True)
        expo = jnp.exp(sc - top)
        total = jnp.sum(expo, axis=1, keepdims=True)
        carried = jnp.dot(expo.astype(BF16), cache[s, 0, :, HD:], preferred_element_type=F32)
        pack = held[s].astype(F32)
        q = pack[:per]
        peak = top
        extra = []
        for u in range(STEPS):
            f = jnp.sum(q * pack[per + 2 * u : per + 2 * u + 1], axis=1, keepdims=True) * scale
            f = jnp.where(step >= u, f, -jnp.inf)
            extra.append(f)
            peak = jnp.maximum(peak, f)
        factor = jnp.exp(top - peak)
        denom = total * factor
        numer = carried * factor
        for u in range(STEPS):
            w = jnp.exp(extra[u] - peak)
            denom = denom + w
            numer = numer + w * pack[per + 2 * u + 1 : per + 2 * u + 2]
        out[s] = (numer / denom).astype(BF16)
    for k in range(MOVE):
        goal = at(notices, me, DEST + k)
        rows = out[at(notices, me, DEP + k)]
        send[goal, :per, :] = rows
        send[lax.rem(goal + REP // XL, REP), per:, :] = rows


def project_body(notices, came, mine, other, *rest):
    arrays, out, slots, rows, total = rest[:-4], rest[-4], rest[-3], rest[-2], rest[-1]
    per = STEPS * HEADS
    me = at(notices, 0, ME)
    pair = lax.rem(me + REP // XL, REP)
    xl, z, core = lax.div(me, Z * CORE), lax.rem(lax.div(me, CORE), Z), lax.rem(me, CORE)
    first, second = xl * SLOTS, (1 - xl) * SLOTS
    for s in range(SLOTS):
        slots[pl.ds(pl.multiple_of((first + s) * per, per), per), :] = mine[s].astype(F32)
        slots[pl.ds(pl.multiple_of((second + s) * per, per), per), :] = other[s].astype(F32)

    def place_rows(peer, carry):
        for lane, owner, start, lo in ((ROUND, me, first, 0), (PAIR_ROUND, pair, second, per)):
            turn = at(notices, peer, lane)
            slot = start + at(notices, owner, DEP + jnp.maximum(turn, 0))
            goal = jnp.where(turn >= 0, slot, XL * SLOTS)
            slots[pl.ds(pl.multiple_of(goal * per, per), per), :] = came[
                peer, lo : lo + per, :
            ].astype(F32)
        return carry

    lax.fori_loop(0, REP, place_rows, 0, unroll=4)
    for h in range(HEADS):
        for side in range(XL):
            for t in range(STEPS):
                lo = side * ROWS + t * SLOTS
                rows[h, lo : lo + SLOTS, :] = slots[
                    pl.ds(side * SLOTS * per + t * HEADS + h, SLOTS, stride=per), :
                ].astype(BF16)
    total[...] = jnp.zeros_like(total)

    def run(blocks, first, z_src, core_src):
        src = (xl * Z + z_src) * CORE + core_src
        for lo in range(0, OWN, 5):
            products = []
            for n in range(lo, lo + 5):
                products.append(
                    jnp.dot(
                        rows[at(notices, src, HEAD + n)],
                        blocks[first + n],
                        preferred_element_type=F32,
                    )
                    * notices[src, 0, SCALE + n]
                )
            for n in range(lo, lo + 5):
                total[at(notices, src, COL + n)] += products[n - lo]

    own, one, one_sib, two_a, two_a_sib, mid, mid_sib, last, last_sib = arrays
    run(own, 0, z, core)
    run(own, OWN, z, 1 - core)
    for line, a, b, c, d in (
        (core, one, two_a, mid, last),
        (1 - core, one_sib, two_a_sib, mid_sib, last_sib),
    ):
        away = 1 - 2 * line
        far = [lax.rem(z - away * step + Z, Z) for step in range(Z // 2 + 1)]
        run(a, 0, far[1], line)
        run(a, OWN, far[1], 1 - line)
        run(b, 0, far[2], line)
        run(c, 0, far[2], 1 - line)
        run(c, OWN, far[3], line)
        run(d, 0, far[3], 1 - line)
        run(d, OWN, far[4], line)
    out[:COLS] = total[:, :ROWS, :].astype(BF16)
    out[COLS:] = total[:, ROWS:, :].astype(BF16)


def sum_body(parts, out):
    for c in range(OUT_COLS):
        acc = parts[0, c].astype(F32)
        for t in range(1, XL * TP):
            acc = acc + parts[t, c].astype(F32)
        acc = acc.astype(BF16)
        for t in range(STEPS):
            out[t, :, c * HD : (c + 1) * HD] = acc[t * SLOTS : (t + 1) * SLOTS, :]


def shards(kv_cache, lengths, departing, destination, queries, new_kv, codes, scales, block_slot):
    rep_axes, tp_axes = ("xl", "z", "core"), ("y", "xh")
    base = lax.axis_index(tp_axes) * (HEADS * COLS)
    per = STEPS * HEADS

    def in_hbm(x):
        return pltpu.with_memory_space_constraint(x, pltpu.HBM)

    def exchange(x, axes):
        return lax.all_to_all(x, axes, split_axis=0, concat_axis=0, tiled=True)

    def swap(x, axis):
        return lax.ppermute(x, axis, [(0, 1), (1, 0)])

    def around(x, hops):
        pairs = [
            (i * CORE + c, ((i + hops * (1 - 2 * c)) % Z) * CORE + c)
            for i in range(Z)
            for c in range(CORE)
        ]
        return lax.ppermute(x, ("z", "core"), pairs)

    two_a = around(codes, 2)
    sib = swap(codes, "core")
    given = [
        departing,
        destination,
        lengths,
        block_slot,
        scales,
        queries,
        new_kv.reshape(STEPS, SLOTS, 2 * HD),
    ]
    notice, packs = call(
        notice_body,
        [
            jax.ShapeDtypeStruct((REP, 1, HD), F32),
            jax.ShapeDtypeStruct((SLOTS, PACK, HD), BF16),
        ],
        [smem()] + [hbm()] * len(given),
        [pltpu.SMEM(a.shape, a.dtype) for a in given[:5]]
        + [pltpu.VMEM(a.shape, a.dtype) for a in given[5:]]
        + [pltpu.SemaphoreType.DMA((len(given),))],
    )(base.astype(I32)[None], *(in_hbm(a) for a in given))
    sib, notice = lax.optimization_barrier((sib, notice))
    join = call(
        join_body,
        jax.ShapeDtypeStruct((CORE * OWN, HD, HD), BF16),
        [pl.BlockSpec(memory_space=pl.ANY)] * 2,
        [pltpu.SemaphoreType.DMA((2,))],
    )
    own = join(in_hbm(codes), sib)

    one = around(own, 1)
    notices = exchange(notice, rep_axes)
    one, two_a, notices = lax.optimization_barrier((one, two_a, notices))

    mid = around(join(one[OWN:], two_a), 1)
    one_sib, two_a_sib = swap(one, "core"), swap(two_a, "core")
    to_pull = call(
        pull_body, jax.ShapeDtypeStruct((REP, PACK, HD), BF16), [smem(), vmem()]
    )(notices, packs)
    pulled = exchange(to_pull, rep_axes)
    mid, pulled = lax.optimization_barrier((mid, pulled))

    last = around(mid, 1)
    mid_sib = swap(mid, "core")
    send, mine = call(
        attend_body,
        [
            jax.ShapeDtypeStruct((REP, 2 * per, HD), BF16),
            jax.ShapeDtypeStruct((SLOTS, per, HD), BF16),
        ],
        [smem()] + [vmem()] * 3,
        [pltpu.VMEM((SLOTS, per, CTX), F32), pltpu.VMEM((SLOTS, PACK, HD), BF16)],
    )(notices, pulled, packs, kv_cache)
    other = swap(mine, "xl")
    came = exchange(send, rep_axes)
    last, came, other = lax.optimization_barrier((last, came, other))
    arrays = [own, one, one_sib, two_a, two_a_sib, mid, mid_sib, last, swap(last, "core")]
    parts = call(
        project_body,
        jax.ShapeDtypeStruct((XL * COLS, ROWS, HD), BF16),
        [smem()] + [vmem()] * (3 + len(arrays)),
        [
            pltpu.VMEM(((XL * SLOTS + 1) * per, HD), F32),
            pltpu.VMEM((HEADS, XL * ROWS, HD), BF16),
            pltpu.VMEM((COLS, XL * ROWS, HD), F32),
        ],
    )(notices, came, mine, other, *arrays)
    parts = exchange(parts, ("xl",) + tp_axes).reshape(XL * TP, OUT_COLS, ROWS, HD)
    return call(
        sum_body, jax.ShapeDtypeStruct((STEPS, SLOTS, OUT_COLS * HD), BF16), [vmem()]
    )(parts)


def solution(mesh):
    rep, tp = ("xl", "z", "core"), ("y", "xh")
    parts = Mesh(mesh.devices.reshape(XL, Z, CORE, 4, 2), rep + tp)
    placed = (
        P(rep, tp, None, None),
        P(rep),
        P(rep, None),
        P(rep, None),
        P(None, rep, tp, None),
        P(None, rep, tp, None),
        P(tp + rep, None, None),
        P(tp + rep),
        P(tp + rep),
    )
    return jax.shard_map(
        shards, mesh=parts, in_specs=placed, out_specs=P(None, rep, tp), check_vma=False
    )
```

```python
import math

import jax
import jax.numpy as jnp
from jax import lax
from jax.experimental import pallas as pl
from jax.experimental.pallas import tpu as pltpu
from jax.sharding import Mesh, PartitionSpec as P

BF16, F32, I32 = jnp.bfloat16, jnp.float32, jnp.int32

XL, Z, CORE, TP = 2, 8, 2, 8
REP = XL * Z * CORE

HD = 128
SLOTS = 16
STEPS = 2
HEADS = 8
CTX = 256
MOVE = 13
STAY = SLOTS - MOVE
COLS = 40
OUT_COLS = COLS // TP
OWN = 10
ROWS = SLOTS * STEPS
PACK = STEPS * HEADS + 2 * STEPS

ROUND, PAIR_ROUND, ME, HEAD, COL, SCALE, DEP, DEST, LEN = 0, 1, 2, 3, 13, 23, 33, 46, 59

VMEM_LIMIT = 40 * 1024 * 1024


def smem():
    return pl.BlockSpec(memory_space=pltpu.SMEM)


def vmem():
    return pl.BlockSpec(memory_space=pltpu.VMEM)


def hbm():
    return pl.BlockSpec(memory_space=pltpu.HBM)


def call(body, out_shape, in_specs, scratch=(), **kw):
    single = not isinstance(out_shape, (list, tuple))
    return pl.pallas_call(
        body,
        out_shape=out_shape,
        in_specs=in_specs,
        out_specs=vmem() if single else [vmem()] * len(out_shape),
        scratch_shapes=list(scratch),
        compiler_params=pltpu.CompilerParams(vmem_limit_bytes=VMEM_LIMIT),
        **kw,
    )


def copy_in(pairs, sems):
    copies = [pltpu.make_async_copy(a, b, sems.at[i]) for i, (a, b) in enumerate(pairs)]
    for c in copies:
        c.start()
    for c in copies:
        c.wait()


def notice_body(place, *refs):
    given, (notice, packs), held, sems = refs[:7], refs[7:9], refs[9:16], refs[16]
    copy_in(zip(given, held), sems)
    dep, dest, lengths, ids, scales, queries, fresh = held
    row = lax.broadcasted_iota(I32, (REP, HD), 0)
    lane = lax.broadcasted_iota(I32, (REP, HD), 1)
    base = place[0]
    pair_row = lax.rem(row + REP // XL, REP)
    out = jnp.where(lane == ME, row, -1).astype(F32)
    for k in range(MOVE):
        out = jnp.where((lane == ROUND) & (row == dest[0, k]), float(k), out)
        out = jnp.where((lane == PAIR_ROUND) & (pair_row == dest[0, k]), float(k), out)
        out = jnp.where(lane == DEP + k, dep[0, k].astype(F32), out)
        out = jnp.where(lane == DEST + k, dest[0, k].astype(F32), out)
    for n in range(OWN):
        place_n = ids[n] - base
        head = lax.div(place_n, COLS)
        out = jnp.where(lane == HEAD + n, head.astype(F32), out)
        out = jnp.where(lane == COL + n, (place_n - head * COLS).astype(F32), out)
        out = jnp.where(lane == SCALE + n, scales[n], out)
    for s in range(SLOTS):
        out = jnp.where(lane == LEN + s, lengths[s].astype(F32), out)
    notice[:, 0, :] = out
    for s in range(SLOTS):
        packs[s] = jnp.concatenate(
            [queries[t, s] for t in range(STEPS)]
            + [fresh[t, s : s + 1, j * HD : (j + 1) * HD] for t in range(STEPS) for j in range(2)],
            axis=0,
        )


def join_body(first, second, out, sems):
    n = first.shape[0]
    copy_in([(first.at[n - OWN :], out.at[:OWN]), (second.at[:OWN], out.at[OWN:])], sems)


def at(notices, rep, lane):
    return notices[rep, 0, lane].astype(I32)


def pull_body(notices, packs, out):
    me = at(notices, 0, ME)

    def one(peer, carry):
        turn = at(notices, peer, ROUND)
        out[peer] = packs[at(notices, me, DEP + jnp.maximum(turn, 0))]
        return carry

    lax.fori_loop(0, REP, one, 0, unroll=4)


def attend_body(notices, pulled, packs, cache, send, out, scores, held):
    scale = 1.0 / math.sqrt(HD)
    per = STEPS * HEADS
    me = at(notices, 0, ME)
    for s in range(SLOTS):
        held[s] = packs[s]
    for k in range(MOVE):
        held[at(notices, me, DEP + k)] = pulled[at(notices, me, DEST + k)]
    pos = lax.broadcasted_iota(I32, (per, CTX), 1)
    for s in range(SLOTS):
        q = held[s][:per]
        sc = lax.dot_general(
            q, cache[s, 0, :, :HD], (((1,), (1,)), ((), ())), preferred_element_type=F32
        )
        scores[s] = jnp.where(pos < at(notices, me, LEN + s), sc * scale, -jnp.inf)
    step = lax.broadcasted_iota(I32, (per, 1), 0) // HEADS
    for s in range(SLOTS):
        sc = scores[s]
        top = jnp.max(sc, axis=1, keepdims=True)
        expo = jnp.exp(sc - top)
        total = jnp.sum(expo, axis=1, keepdims=True)
        carried = jnp.dot(expo.astype(BF16), cache[s, 0, :, HD:], preferred_element_type=F32)
        pack = held[s].astype(F32)
        q = pack[:per]
        peak = top
        extra = []
        for u in range(STEPS):
            f = jnp.sum(q * pack[per + 2 * u : per + 2 * u + 1], axis=1, keepdims=True) * scale
            f = jnp.where(step >= u, f, -jnp.inf)
            extra.append(f)
            peak = jnp.maximum(peak, f)
        factor = jnp.exp(top - peak)
        denom = total * factor
        numer = carried * factor
        for u in range(STEPS):
            w = jnp.exp(extra[u] - peak)
            denom = denom + w
            numer = numer + w * pack[per + 2 * u + 1 : per + 2 * u + 2]
        out[s] = (numer / denom).astype(BF16)
    for k in range(MOVE):
        goal = at(notices, me, DEST + k)
        rows = out[at(notices, me, DEP + k)]
        send[goal, :per, :] = rows
        send[lax.rem(goal + REP // XL, REP), per:, :] = rows


def project_body(notices, came, mine, other, *rest):
    arrays, out, slots, rows, total = rest[:-4], rest[-4], rest[-3], rest[-2], rest[-1]
    per = STEPS * HEADS
    me = at(notices, 0, ME)
    pair = lax.rem(me + REP // XL, REP)
    xl, z, core = lax.div(me, Z * CORE), lax.rem(lax.div(me, CORE), Z), lax.rem(me, CORE)
    first, second = xl * SLOTS, (1 - xl) * SLOTS
    for s in range(SLOTS):
        slots[pl.ds(pl.multiple_of((first + s) * per, per), per), :] = mine[s].astype(F32)
        slots[pl.ds(pl.multiple_of((second + s) * per, per), per), :] = other[s].astype(F32)

    def place_rows(peer, carry):
        for lane, owner, start, lo in ((ROUND, me, first, 0), (PAIR_ROUND, pair, second, per)):
            turn = at(notices, peer, lane)
            slot = start + at(notices, owner, DEP + jnp.maximum(turn, 0))
            goal = jnp.where(turn >= 0, slot, XL * SLOTS)
            slots[pl.ds(pl.multiple_of(goal * per, per), per), :] = came[
                peer, lo : lo + per, :
            ].astype(F32)
        return carry

    lax.fori_loop(0, REP, place_rows, 0, unroll=4)
    for h in range(HEADS):
        for side in range(XL):
            for t in range(STEPS):
                lo = side * ROWS + t * SLOTS
                rows[h, lo : lo + SLOTS, :] = slots[
                    pl.ds(side * SLOTS * per + t * HEADS + h, SLOTS, stride=per), :
                ].astype(BF16)
    total[...] = jnp.zeros_like(total)

    def run(blocks, first, z_src, core_src):
        src = (xl * Z + z_src) * CORE + core_src
        for lo in range(0, OWN, 5):
            products = []
            for n in range(lo, lo + 5):
                products.append(
                    jnp.dot(
                        rows[at(notices, src, HEAD + n)],
                        blocks[first + n],
                        preferred_element_type=F32,
                    )
                    * notices[src, 0, SCALE + n]
                )
            for n in range(lo, lo + 5):
                total[at(notices, src, COL + n)] += products[n - lo]

    own, one, one_sib, two, two_sib, three, three_sib, last, last_sib = arrays
    run(own, 0, z, core)
    run(own, OWN, z, 1 - core)
    for line, a, b, c, d in (
        (core, one, two, three, last),
        (1 - core, one_sib, two_sib, three_sib, last_sib),
    ):
        away = 1 - 2 * line
        far = [lax.rem(z - away * step + Z, Z) for step in range(Z // 2 + 1)]
        run(a, 0, far[1], line)
        run(a, OWN, far[1], 1 - line)
        run(b, 0, far[2], line)
        run(b, OWN, far[2], 1 - line)
        run(c, 0, far[3], line)
        run(d, 0, far[3], 1 - line)
        run(d, OWN, far[4], line)
    out[:COLS] = total[:, :ROWS, :].astype(BF16)
    out[COLS:] = total[:, ROWS:, :].astype(BF16)


def sum_body(parts, out):
    for c in range(OUT_COLS):
        acc = parts[0, c].astype(F32)
        for t in range(1, XL * TP):
            acc = acc + parts[t, c].astype(F32)
        acc = acc.astype(BF16)
        for t in range(STEPS):
            out[t, :, c * HD : (c + 1) * HD] = acc[t * SLOTS : (t + 1) * SLOTS, :]


def shards(kv_cache, lengths, departing, destination, queries, new_kv, codes, scales, block_slot):
    rep_axes, tp_axes = ("xl", "z", "core"), ("y", "xh")
    base = lax.axis_index(tp_axes) * (HEADS * COLS)
    per = STEPS * HEADS

    def in_hbm(x):
        return pltpu.with_memory_space_constraint(x, pltpu.HBM)

    def exchange(x, axes):
        return lax.all_to_all(x, axes, split_axis=0, concat_axis=0, tiled=True)

    def swap(x, axis):
        return lax.ppermute(x, axis, [(0, 1), (1, 0)])

    def around(x, hops):
        pairs = [
            (i * CORE + c, ((i + hops * (1 - 2 * c)) % Z) * CORE + c)
            for i in range(Z)
            for c in range(CORE)
        ]
        return lax.ppermute(x, ("z", "core"), pairs)

    sib = swap(codes, "core")
    given = [
        departing,
        destination,
        lengths,
        block_slot,
        scales,
        queries,
        new_kv.reshape(STEPS, SLOTS, 2 * HD),
    ]
    notice, packs = call(
        notice_body,
        [
            jax.ShapeDtypeStruct((REP, 1, HD), F32),
            jax.ShapeDtypeStruct((SLOTS, PACK, HD), BF16),
        ],
        [smem()] + [hbm()] * len(given),
        [pltpu.SMEM(a.shape, a.dtype) for a in given[:5]]
        + [pltpu.VMEM(a.shape, a.dtype) for a in given[5:]]
        + [pltpu.SemaphoreType.DMA((len(given),))],
    )(base.astype(I32)[None], *(in_hbm(a) for a in given))
    sib, notice = lax.optimization_barrier((sib, notice))
    join = call(
        join_body,
        jax.ShapeDtypeStruct((CORE * OWN, HD, HD), BF16),
        [pl.BlockSpec(memory_space=pl.ANY)] * 2,
        [pltpu.SemaphoreType.DMA((2,))],
    )
    own = join(in_hbm(codes), sib)

    one = around(own, 1)
    notices = exchange(notice, rep_axes)
    one, notices = lax.optimization_barrier((one, notices))

    two, three = around(one, 1), around(one[:OWN], 2)
    one_sib = swap(one, "core")
    to_pull = call(
        pull_body, jax.ShapeDtypeStruct((REP, PACK, HD), BF16), [smem(), vmem()]
    )(notices, packs)
    pulled = exchange(to_pull, rep_axes)
    two, three, pulled = lax.optimization_barrier((two, three, pulled))

    last = around(join(two, three), 1)
    two_sib, three_sib = swap(two, "core"), swap(three, "core")
    send, mine = call(
        attend_body,
        [
            jax.ShapeDtypeStruct((REP, 2 * per, HD), BF16),
            jax.ShapeDtypeStruct((SLOTS, per, HD), BF16),
        ],
        [smem()] + [vmem()] * 3,
        [pltpu.VMEM((SLOTS, per, CTX), F32), pltpu.VMEM((SLOTS, PACK, HD), BF16)],
    )(notices, pulled, packs, kv_cache)
    other = swap(mine, "xl")
    came = exchange(send, rep_axes)
    last, came, other = lax.optimization_barrier((last, came, other))
    arrays = [own, one, one_sib, two, two_sib, three, three_sib, last, swap(last, "core")]
    parts = call(
        project_body,
        jax.ShapeDtypeStruct((XL * COLS, ROWS, HD), BF16),
        [smem()] + [vmem()] * (3 + len(arrays)),
        [
            pltpu.VMEM(((XL * SLOTS + 1) * per, HD), F32),
            pltpu.VMEM((HEADS, XL * ROWS, HD), BF16),
            pltpu.VMEM((COLS, XL * ROWS, HD), F32),
        ],
    )(notices, came, mine, other, *arrays)
    parts = exchange(parts, ("xl",) + tp_axes).reshape(XL * TP, OUT_COLS, ROWS, HD)
    return call(
        sum_body, jax.ShapeDtypeStruct((STEPS, SLOTS, OUT_COLS * HD), BF16), [vmem()]
    )(parts)


def solution(mesh):
    rep, tp = ("xl", "z", "core"), ("y", "xh")
    parts = Mesh(mesh.devices.reshape(XL, Z, CORE, 4, 2), rep + tp)
    placed = (
        P(rep, tp, None, None),
        P(rep),
        P(rep, None),
        P(rep, None),
        P(None, rep, tp, None),
        P(None, rep, tp, None),
        P(tp + rep, None, None),
        P(tp + rep),
        P(tp + rep),
    )
    return jax.shard_map(
        shards, mesh=parts, in_specs=placed, out_specs=P(None, rep, tp), check_vma=False
    )
```

```python
import math

import jax
import jax.numpy as jnp
from jax import lax
from jax.experimental import pallas as pl
from jax.experimental.pallas import tpu as pltpu
from jax.sharding import Mesh, PartitionSpec as P

BF16, F32, I32 = jnp.bfloat16, jnp.float32, jnp.int32

XL, Z, CORE, TP = 2, 8, 2, 8
REP = XL * Z * CORE

HD = 128
SLOTS = 16
STEPS = 2
HEADS = 8
CTX = 256
MOVE = 13
STAY = SLOTS - MOVE
COLS = 40
OUT_COLS = COLS // TP
OWN = 10
ROWS = SLOTS * STEPS
PACK = STEPS * HEADS + 2 * STEPS

ROUND, PAIR_ROUND, ME, HEAD, COL, SCALE, DEP, DEST, LEN = 0, 1, 2, 3, 13, 23, 33, 46, 59

VMEM_LIMIT = 40 * 1024 * 1024


def smem():
    return pl.BlockSpec(memory_space=pltpu.SMEM)


def vmem():
    return pl.BlockSpec(memory_space=pltpu.VMEM)


def hbm():
    return pl.BlockSpec(memory_space=pltpu.HBM)


def call(body, out_shape, in_specs, scratch=(), **kw):
    single = not isinstance(out_shape, (list, tuple))
    return pl.pallas_call(
        body,
        out_shape=out_shape,
        in_specs=in_specs,
        out_specs=vmem() if single else [vmem()] * len(out_shape),
        scratch_shapes=list(scratch),
        compiler_params=pltpu.CompilerParams(vmem_limit_bytes=VMEM_LIMIT),
        **kw,
    )


def copy_in(pairs, sems):
    copies = [pltpu.make_async_copy(a, b, sems.at[i]) for i, (a, b) in enumerate(pairs)]
    for c in copies:
        c.start()
    for c in copies:
        c.wait()


def notice_body(place, *refs):
    given, (notice, packs), held, sems = refs[:7], refs[7:9], refs[9:16], refs[16]
    copy_in(zip(given, held), sems)
    dep, dest, lengths, ids, scales, queries, fresh = held
    row = lax.broadcasted_iota(I32, (REP, HD), 0)
    lane = lax.broadcasted_iota(I32, (REP, HD), 1)
    base = place[0]
    pair_row = lax.rem(row + REP // XL, REP)
    out = jnp.where(lane == ME, row, -1).astype(F32)
    for k in range(MOVE):
        out = jnp.where((lane == ROUND) & (row == dest[0, k]), float(k), out)
        out = jnp.where((lane == PAIR_ROUND) & (pair_row == dest[0, k]), float(k), out)
        out = jnp.where(lane == DEP + k, dep[0, k].astype(F32), out)
        out = jnp.where(lane == DEST + k, dest[0, k].astype(F32), out)
    for n in range(OWN):
        place_n = ids[n] - base
        head = lax.div(place_n, COLS)
        out = jnp.where(lane == HEAD + n, head.astype(F32), out)
        out = jnp.where(lane == COL + n, (place_n - head * COLS).astype(F32), out)
        out = jnp.where(lane == SCALE + n, scales[n], out)
    for s in range(SLOTS):
        out = jnp.where(lane == LEN + s, lengths[s].astype(F32), out)
    notice[:, 0, :] = out
    for s in range(SLOTS):
        packs[s] = jnp.concatenate(
            [queries[t, s] for t in range(STEPS)]
            + [fresh[t, s : s + 1, j * HD : (j + 1) * HD] for t in range(STEPS) for j in range(2)],
            axis=0,
        )


def at(notices, rep, lane):
    return notices[rep, 0, lane].astype(I32)


def pull_body(notices, packs, out):
    me = at(notices, 0, ME)

    def one(peer, carry):
        turn = at(notices, peer, ROUND)
        out[peer] = packs[at(notices, me, DEP + jnp.maximum(turn, 0))]
        return carry

    lax.fori_loop(0, REP, one, 0, unroll=4)


def attend_body(notices, pulled, packs, cache, send, out, scores, held):
    scale = 1.0 / math.sqrt(HD)
    per = STEPS * HEADS
    me = at(notices, 0, ME)
    for s in range(SLOTS):
        held[s] = packs[s]
    for k in range(MOVE):
        held[at(notices, me, DEP + k)] = pulled[at(notices, me, DEST + k)]
    pos = lax.broadcasted_iota(I32, (per, CTX), 1)
    for s in range(SLOTS):
        q = held[s][:per]
        sc = lax.dot_general(
            q, cache[s, 0, :, :HD], (((1,), (1,)), ((), ())), preferred_element_type=F32
        )
        scores[s] = jnp.where(pos < at(notices, me, LEN + s), sc * scale, -jnp.inf)
    step = lax.broadcasted_iota(I32, (per, 1), 0) // HEADS
    for s in range(SLOTS):
        sc = scores[s]
        top = jnp.max(sc, axis=1, keepdims=True)
        expo = jnp.exp(sc - top)
        total = jnp.sum(expo, axis=1, keepdims=True)
        carried = jnp.dot(expo.astype(BF16), cache[s, 0, :, HD:], preferred_element_type=F32)
        pack = held[s].astype(F32)
        q = pack[:per]
        peak = top
        extra = []
        for u in range(STEPS):
            f = jnp.sum(q * pack[per + 2 * u : per + 2 * u + 1], axis=1, keepdims=True) * scale
            f = jnp.where(step >= u, f, -jnp.inf)
            extra.append(f)
            peak = jnp.maximum(peak, f)
        factor = jnp.exp(top - peak)
        denom = total * factor
        numer = carried * factor
        for u in range(STEPS):
            w = jnp.exp(extra[u] - peak)
            denom = denom + w
            numer = numer + w * pack[per + 2 * u + 1 : per + 2 * u + 2]
        out[s] = (numer / denom).astype(BF16)
    for k in range(MOVE):
        goal = at(notices, me, DEST + k)
        rows = out[at(notices, me, DEP + k)]
        send[goal, :per, :] = rows
        send[lax.rem(goal + REP // XL, REP), per:, :] = rows


def project_body(notices, came, mine, other, *rest):
    arrays, out, slots, rows, total = rest[:-4], rest[-4], rest[-3], rest[-2], rest[-1]
    per = STEPS * HEADS
    me = at(notices, 0, ME)
    pair = lax.rem(me + REP // XL, REP)
    xl, z, core = lax.div(me, Z * CORE), lax.rem(lax.div(me, CORE), Z), lax.rem(me, CORE)
    first, second = xl * SLOTS, (1 - xl) * SLOTS
    for s in range(SLOTS):
        slots[pl.ds(pl.multiple_of((first + s) * per, per), per), :] = mine[s].astype(F32)
        slots[pl.ds(pl.multiple_of((second + s) * per, per), per), :] = other[s].astype(F32)

    def place_rows(peer, carry):
        for lane, owner, start, lo in ((ROUND, me, first, 0), (PAIR_ROUND, pair, second, per)):
            turn = at(notices, peer, lane)
            slot = start + at(notices, owner, DEP + jnp.maximum(turn, 0))
            goal = jnp.where(turn >= 0, slot, XL * SLOTS)
            slots[pl.ds(pl.multiple_of(goal * per, per), per), :] = came[
                peer, lo : lo + per, :
            ].astype(F32)
        return carry

    lax.fori_loop(0, REP, place_rows, 0, unroll=4)
    for h in range(HEADS):
        for side in range(XL):
            for t in range(STEPS):
                lo = side * ROWS + t * SLOTS
                rows[h, lo : lo + SLOTS, :] = slots[
                    pl.ds(side * SLOTS * per + t * HEADS + h, SLOTS, stride=per), :
                ].astype(BF16)
    total[...] = jnp.zeros_like(total)

    def run(blocks, first, z_src, core_src):
        src = (xl * Z + z_src) * CORE + core_src
        for lo in range(0, OWN, 5):
            products = []
            for n in range(lo, lo + 5):
                products.append(
                    jnp.dot(
                        rows[at(notices, src, HEAD + n)],
                        blocks[first + n],
                        preferred_element_type=F32,
                    )
                    * notices[src, 0, SCALE + n]
                )
            for n in range(lo, lo + 5):
                total[at(notices, src, COL + n)] += products[n - lo]

    half = Z // 2
    for line, same, cross in (
        (core, arrays[: half + 1], arrays[half + 1 : Z + 1]),
        (1 - core, (None, *arrays[Z + 1 : Z + half + 1]), (None, *arrays[Z + half + 1 :])),
    ):
        for step in range(half + 1):
            far = lax.rem(z - (1 - 2 * line) * step + Z, Z)
            if same[step] is not None:
                run(same[step], 0, far, line)
            if step < half and cross[step] is not None:
                run(cross[step], 0, far, 1 - line)
    out[:COLS] = total[:, :ROWS, :].astype(BF16)
    out[COLS:] = total[:, ROWS:, :].astype(BF16)


def sum_body(parts, out):
    for c in range(OUT_COLS):
        acc = parts[0, c].astype(F32)
        for t in range(1, XL * TP):
            acc = acc + parts[t, c].astype(F32)
        acc = acc.astype(BF16)
        for t in range(STEPS):
            out[t, :, c * HD : (c + 1) * HD] = acc[t * SLOTS : (t + 1) * SLOTS, :]


def shards(kv_cache, lengths, departing, destination, queries, new_kv, codes, scales, block_slot):
    rep_axes, tp_axes = ("xl", "z", "core"), ("y", "xh")
    base = lax.axis_index(tp_axes) * (HEADS * COLS)
    per = STEPS * HEADS

    def in_hbm(x):
        return pltpu.with_memory_space_constraint(x, pltpu.HBM)

    def exchange(x, axes):
        return lax.all_to_all(x, axes, split_axis=0, concat_axis=0, tiled=True)

    def swap(x, axis):
        return lax.ppermute(x, axis, [(0, 1), (1, 0)])

    def around(x, hops):
        pairs = [
            (i * CORE + c, ((i + hops * (1 - 2 * c)) % Z) * CORE + c)
            for i in range(Z)
            for c in range(CORE)
        ]
        return lax.ppermute(x, ("z", "core"), pairs)

    sib = swap(codes, "core")
    given = [
        departing,
        destination,
        lengths,
        block_slot,
        scales,
        queries,
        new_kv.reshape(STEPS, SLOTS, 2 * HD),
    ]
    notice, packs = call(
        notice_body,
        [
            jax.ShapeDtypeStruct((REP, 1, HD), F32),
            jax.ShapeDtypeStruct((SLOTS, PACK, HD), BF16),
        ],
        [smem()] + [hbm()] * len(given),
        [pltpu.SMEM(a.shape, a.dtype) for a in given[:5]]
        + [pltpu.VMEM(a.shape, a.dtype) for a in given[5:]]
        + [pltpu.SemaphoreType.DMA((len(given),))],
    )(base.astype(I32)[None], *(in_hbm(a) for a in given))
    near, near_x = around(codes, 1), around(sib, 1)
    notices = exchange(notice, rep_axes)
    near, notices = lax.optimization_barrier((near, notices))
    two, two_x = around(near, 1), around(near_x, 1)
    near_sib, near_x_sib = swap(near, "core"), swap(near_x, "core")
    to_pull = call(
        pull_body, jax.ShapeDtypeStruct((REP, PACK, HD), BF16), [smem(), vmem()]
    )(notices, packs)
    pulled = exchange(to_pull, rep_axes)
    three, three_x = around(two, 1), around(two_x, 1)
    two_sib, two_x_sib = swap(two, "core"), swap(two_x, "core")
    send, mine = call(
        attend_body,
        [
            jax.ShapeDtypeStruct((REP, 2 * per, HD), BF16),
            jax.ShapeDtypeStruct((SLOTS, per, HD), BF16),
        ],
        [smem()] + [vmem()] * 3,
        [pltpu.VMEM((SLOTS, per, CTX), F32), pltpu.VMEM((SLOTS, PACK, HD), BF16)],
    )(notices, pulled, packs, kv_cache)
    other = swap(mine, "xl")
    came = exchange(send, rep_axes)
    four = around(three, 1)
    three_sib, three_x_sib = swap(three, "core"), swap(three_x, "core")
    four_sib = around(three_x, 1)
    arrays = [codes, near, two, three, four, sib, near_x, two_x, three_x]
    arrays += [near_sib, two_sib, three_sib, four_sib, near_x_sib, two_x_sib, three_x_sib]
    parts = call(
        project_body,
        jax.ShapeDtypeStruct((XL * COLS, ROWS, HD), BF16),
        [smem()] + [vmem()] * (3 + len(arrays)),
        [
            pltpu.VMEM(((XL * SLOTS + 1) * per, HD), F32),
            pltpu.VMEM((HEADS, XL * ROWS, HD), BF16),
            pltpu.VMEM((COLS, XL * ROWS, HD), F32),
        ],
    )(notices, came, mine, other, *arrays)
    parts = exchange(parts, ("xl",) + tp_axes).reshape(XL * TP, OUT_COLS, ROWS, HD)
    return call(
        sum_body, jax.ShapeDtypeStruct((STEPS, SLOTS, OUT_COLS * HD), BF16), [vmem()]
    )(parts)


def solution(mesh):
    rep, tp = ("xl", "z", "core"), ("y", "xh")
    parts = Mesh(mesh.devices.reshape(XL, Z, CORE, 4, 2), rep + tp)
    placed = (
        P(rep, tp, None, None),
        P(rep),
        P(rep, None),
        P(rep, None),
        P(None, rep, tp, None),
        P(None, rep, tp, None),
        P(tp + rep, None, None),
        P(tp + rep),
        P(tp + rep),
    )
    return jax.shard_map(
        shards, mesh=parts, in_specs=placed, out_specs=P(None, rep, tp), check_vma=False
    )
```

```python
import math

import jax
import jax.numpy as jnp
from jax import lax
from jax.experimental import pallas as pl
from jax.experimental.pallas import tpu as pltpu
from jax.sharding import Mesh, PartitionSpec as P

BF16, F32, I32 = jnp.bfloat16, jnp.float32, jnp.int32

XL, Z, CORE, TP = 2, 8, 2, 8
REP = XL * Z * CORE

HD = 128
SLOTS = 16
STEPS = 2
HEADS = 8
CTX = 256
MOVE = 13
STAY = SLOTS - MOVE
COLS = 40
OUT_COLS = COLS // TP
OWN = 10
ROWS = SLOTS * STEPS
PACK = STEPS * HEADS + 2 * STEPS

ROUND, PAIR_ROUND, ME, HEAD, COL, SCALE, DEP, DEST, LEN = 0, 1, 2, 3, 13, 23, 33, 46, 59

VMEM_LIMIT = 16 * 1024 * 1024


def smem():
    return pl.BlockSpec(memory_space=pltpu.SMEM)


def vmem():
    return pl.BlockSpec(memory_space=pltpu.VMEM)


def hbm():
    return pl.BlockSpec(memory_space=pltpu.HBM)


def call(body, out_shape, in_specs, scratch=(), **kw):
    single = not isinstance(out_shape, (list, tuple))
    return pl.pallas_call(
        body,
        out_shape=out_shape,
        in_specs=in_specs,
        out_specs=vmem() if single else [vmem()] * len(out_shape),
        scratch_shapes=list(scratch),
        compiler_params=pltpu.CompilerParams(vmem_limit_bytes=VMEM_LIMIT),
        **kw,
    )


def copy_in(pairs, sems):
    copies = [pltpu.make_async_copy(a, b, sems.at[i]) for i, (a, b) in enumerate(pairs)]
    for c in copies:
        c.start()
    for c in copies:
        c.wait()


def notice_body(place, *refs):
    given, (notice, packs), held, sems = refs[:7], refs[7:9], refs[9:16], refs[16]
    copy_in(zip(given, held), sems)
    dep, dest, lengths, ids, scales, queries, fresh = held
    row = lax.broadcasted_iota(I32, (REP, HD), 0)
    lane = lax.broadcasted_iota(I32, (REP, HD), 1)
    base = place[0]
    pair_row = lax.rem(row + REP // XL, REP)
    out = jnp.where(lane == ME, row, -1).astype(F32)
    for k in range(MOVE):
        out = jnp.where((lane == ROUND) & (row == dest[0, k]), float(k), out)
        out = jnp.where((lane == PAIR_ROUND) & (pair_row == dest[0, k]), float(k), out)
        out = jnp.where(lane == DEP + k, dep[0, k].astype(F32), out)
        out = jnp.where(lane == DEST + k, dest[0, k].astype(F32), out)
    for n in range(OWN):
        place_n = ids[n] - base
        head = lax.div(place_n, COLS)
        out = jnp.where(lane == HEAD + n, head.astype(F32), out)
        out = jnp.where(lane == COL + n, (place_n - head * COLS).astype(F32), out)
        out = jnp.where(lane == SCALE + n, scales[n], out)
    for s in range(SLOTS):
        out = jnp.where(lane == LEN + s, lengths[s].astype(F32), out)
    notice[:, 0, :] = out
    for s in range(SLOTS):
        packs[s] = jnp.concatenate(
            [queries[t, s] for t in range(STEPS)]
            + [fresh[t, s : s + 1, j * HD : (j + 1) * HD] for t in range(STEPS) for j in range(2)],
            axis=0,
        )


def at(notices, rep, lane):
    return notices[rep, 0, lane].astype(I32)


def pull_body(notices, packs, out):
    me = at(notices, 0, ME)

    def one(peer, carry):
        turn = at(notices, peer, ROUND)
        out[peer] = packs[at(notices, me, DEP + jnp.maximum(turn, 0))]
        return carry

    lax.fori_loop(0, REP, one, 0, unroll=4)


def score(pack, keys, length):
    per = STEPS * HEADS
    sc = lax.dot_general(
        pack[:per], keys, (((1,), (1,)), ((), ())), preferred_element_type=F32
    )
    pos = lax.broadcasted_iota(I32, (per, CTX), 1)
    return jnp.where(pos < length, sc * (1.0 / math.sqrt(HD)), -jnp.inf)


def blend(pack, sc, values):
    per = STEPS * HEADS
    step = lax.broadcasted_iota(I32, (per, 1), 0) // HEADS
    top = jnp.max(sc, axis=1, keepdims=True)
    expo = jnp.exp(sc - top)
    total = jnp.sum(expo, axis=1, keepdims=True)
    carried = jnp.dot(expo.astype(BF16), values, preferred_element_type=F32)
    pack = pack.astype(F32)
    q = pack[:per]
    peak = top
    extra = []
    for u in range(STEPS):
        f = jnp.sum(q * pack[per + 2 * u : per + 2 * u + 1], axis=1, keepdims=True)
        f = jnp.where(step >= u, f * (1.0 / math.sqrt(HD)), -jnp.inf)
        extra.append(f)
        peak = jnp.maximum(peak, f)
    factor = jnp.exp(top - peak)
    denom = total * factor
    numer = carried * factor
    for u in range(STEPS):
        w = jnp.exp(extra[u] - peak)
        denom = denom + w
        numer = numer + w * pack[per + 2 * u + 1 : per + 2 * u + 2]
    return (numer / denom).astype(BF16)


def stay_body(dep, lengths, packs, cache, out, held, leaves, sems):
    for s in range(SLOTS):
        leaves[s] = 0
    for k in range(MOVE):
        leaves[dep[0, k]] = 1

    def copy(s):
        return pltpu.make_async_copy(cache.at[s], held.at[s], sems.at[s])

    def start(s, carry):
        @pl.when(leaves[s] == 0)
        def _():
            copy(s).start()

        return carry

    def one(s, carry):
        @pl.when(leaves[s] == 0)
        def _():
            copy(s).wait()
            pack = packs[s]
            sc = score(pack, held[s, 0, :, :HD], lengths[s])
            out[s] = blend(pack, sc, held[s, 0, :, HD:])

        return carry

    lax.fori_loop(0, SLOTS, start, 0)
    lax.fori_loop(0, SLOTS, one, 0)


def attend_body(notices, pulled, packs, cache, send, out, scores, held, near, sems):
    per = STEPS * HEADS
    copies = [pltpu.make_async_copy(cache.at[s], near.at[s], sems.at[s]) for s in range(SLOTS)]
    for c in copies:
        c.start()
    me = at(notices, 0, ME)
    for s in range(SLOTS):
        held[s] = packs[s]
    for k in range(MOVE):
        held[at(notices, me, DEP + k)] = pulled[at(notices, me, DEST + k)]
    for s in range(SLOTS):
        copies[s].wait()
        scores[s] = score(held[s], near[s, 0, :, :HD], at(notices, me, LEN + s))
    for s in range(SLOTS):
        out[s] = blend(held[s], scores[s], near[s, 0, :, HD:])
    for k in range(MOVE):
        goal = at(notices, me, DEST + k)
        rows = out[at(notices, me, DEP + k)]
        send[goal, :per, :] = rows
        send[lax.rem(goal + REP // XL, REP), per:, :] = rows


def project_body(notices, came, mine, other, *rest):
    arrays, out, slots, rows, total = rest[:-4], rest[-4], rest[-3], rest[-2], rest[-1]
    per = STEPS * HEADS
    me = at(notices, 0, ME)
    pair = lax.rem(me + REP // XL, REP)
    xl, z, core = lax.div(me, Z * CORE), lax.rem(lax.div(me, CORE), Z), lax.rem(me, CORE)
    first, second = xl * SLOTS, (1 - xl) * SLOTS
    for s in range(SLOTS):
        slots[pl.ds(pl.multiple_of((first + s) * per, per), per), :] = mine[s].astype(F32)
        slots[pl.ds(pl.multiple_of((second + s) * per, per), per), :] = other[s].astype(F32)

    def place_rows(peer, carry):
        for lane, owner, start, lo in ((ROUND, me, first, 0), (PAIR_ROUND, pair, second, per)):
            turn = at(notices, peer, lane)
            slot = start + at(notices, owner, DEP + jnp.maximum(turn, 0))
            goal = jnp.where(turn >= 0, slot, XL * SLOTS)
            slots[pl.ds(pl.multiple_of(goal * per, per), per), :] = came[
                peer, lo : lo + per, :
            ].astype(F32)
        return carry

    lax.fori_loop(0, REP, place_rows, 0, unroll=4)
    for h in range(HEADS):
        for side in range(XL):
            for t in range(STEPS):
                lo = side * ROWS + t * SLOTS
                rows[h, lo : lo + SLOTS, :] = slots[
                    pl.ds(side * SLOTS * per + t * HEADS + h, SLOTS, stride=per), :
                ].astype(BF16)
    total[...] = jnp.zeros_like(total)

    def run(blocks, first, z_src, core_src):
        src = (xl * Z + z_src) * CORE + core_src
        for lo in range(0, OWN, 5):
            products = []
            for n in range(lo, lo + 5):
                products.append(
                    jnp.dot(
                        rows[at(notices, src, HEAD + n)],
                        blocks[first + n],
                        preferred_element_type=F32,
                    )
                    * notices[src, 0, SCALE + n]
                )
            for n in range(lo, lo + 5):
                total[at(notices, src, COL + n)] += products[n - lo]

    half = Z // 2
    for line, same, cross in (
        (core, arrays[: half + 1], arrays[half + 1 : Z + 1]),
        (1 - core, (None, *arrays[Z + 1 : Z + half + 1]), (None, *arrays[Z + half + 1 :])),
    ):
        for step in range(half + 1):
            far = lax.rem(z - (1 - 2 * line) * step + Z, Z)
            if same[step] is not None:
                run(same[step], 0, far, line)
            if step < half and cross[step] is not None:
                run(cross[step], 0, far, 1 - line)
    out[:COLS] = total[:, :ROWS, :].astype(BF16)
    out[COLS:] = total[:, ROWS:, :].astype(BF16)


def sum_body(parts, out):
    for c in range(OUT_COLS):
        acc = parts[0, c].astype(F32)
        for t in range(1, XL * TP):
            acc = acc + parts[t, c].astype(F32)
        acc = acc.astype(BF16)
        for t in range(STEPS):
            out[t, :, c * HD : (c + 1) * HD] = acc[t * SLOTS : (t + 1) * SLOTS, :]


def shards(kv_cache, lengths, departing, destination, queries, new_kv, codes, scales, block_slot):
    rep_axes, tp_axes = ("xl", "z", "core"), ("y", "xh")
    base = lax.axis_index(tp_axes) * (HEADS * COLS)
    per = STEPS * HEADS

    def in_hbm(x):
        return pltpu.with_memory_space_constraint(x, pltpu.HBM)

    def exchange(x, axes):
        return lax.all_to_all(x, axes, split_axis=0, concat_axis=0, tiled=True)

    def swap(x, axis):
        return lax.ppermute(x, axis, [(0, 1), (1, 0)])

    def around(x, hops):
        pairs = [
            (i * CORE + c, ((i + hops * (1 - 2 * c)) % Z) * CORE + c)
            for i in range(Z)
            for c in range(CORE)
        ]
        return lax.ppermute(x, ("z", "core"), pairs)

    sib = swap(codes, "core")
    given = [
        departing,
        destination,
        lengths,
        block_slot,
        scales,
        queries,
        new_kv.reshape(STEPS, SLOTS, 2 * HD),
    ]
    notice, packs = call(
        notice_body,
        [
            jax.ShapeDtypeStruct((REP, 1, HD), F32),
            jax.ShapeDtypeStruct((SLOTS, PACK, HD), BF16),
        ],
        [smem()] + [hbm()] * len(given),
        [pltpu.SMEM(a.shape, a.dtype) for a in given[:5]]
        + [pltpu.VMEM(a.shape, a.dtype) for a in given[5:]]
        + [pltpu.SemaphoreType.DMA((len(given),))],
    )(base.astype(I32)[None], *(in_hbm(a) for a in given))
    cache = in_hbm(kv_cache)
    sib, notice = lax.optimization_barrier((sib, notice))
    near, near_x = around(codes, 1), around(sib, 1)
    notices = exchange(notice, rep_axes)
    near, notices = lax.optimization_barrier((near, notices))
    two, two_x = around(near, 1), around(near_x, 1)
    near_sib, near_x_sib = swap(near, "core"), swap(near_x, "core")
    stays = call(
        stay_body,
        jax.ShapeDtypeStruct((SLOTS, per, HD), BF16),
        [smem()] * 2 + [vmem(), hbm()],
        [
            pltpu.VMEM(kv_cache.shape, BF16),
            pltpu.SMEM((SLOTS,), I32),
            pltpu.SemaphoreType.DMA((SLOTS,)),
        ],
    )(departing, lengths, packs, cache)
    other = swap(stays, "xl")
    to_pull = call(
        pull_body, jax.ShapeDtypeStruct((REP, PACK, HD), BF16), [smem(), vmem()]
    )(notices, packs)
    pulled = exchange(to_pull, rep_axes)
    three, three_x = around(two, 1), around(two_x, 1)
    two_sib, two_x_sib = swap(two, "core"), swap(two_x, "core")
    send, mine = call(
        attend_body,
        [
            jax.ShapeDtypeStruct((REP, 2 * per, HD), BF16),
            jax.ShapeDtypeStruct((SLOTS, per, HD), BF16),
        ],
        [smem()] + [vmem()] * 2 + [hbm()],
        [
            pltpu.VMEM((SLOTS, per, CTX), F32),
            pltpu.VMEM((SLOTS, PACK, HD), BF16),
            pltpu.VMEM(kv_cache.shape, BF16),
            pltpu.SemaphoreType.DMA((SLOTS,)),
        ],
    )(notices, pulled, packs, cache)
    came = exchange(send, rep_axes)
    four = around(three, 1)
    three_sib, three_x_sib = swap(three, "core"), swap(three_x, "core")
    four_sib = around(three_x, 1)
    arrays = [codes, near, two, three, four, sib, near_x, two_x, three_x]
    arrays += [near_sib, two_sib, three_sib, four_sib, near_x_sib, two_x_sib, three_x_sib]
    parts = call(
        project_body,
        jax.ShapeDtypeStruct((XL * COLS, ROWS, HD), BF16),
        [smem()] + [vmem()] * (3 + len(arrays)),
        [
            pltpu.VMEM(((XL * SLOTS + 1) * per, HD), F32),
            pltpu.VMEM((HEADS, XL * ROWS, HD), BF16),
            pltpu.VMEM((COLS, XL * ROWS, HD), F32),
        ],
    )(notices, came, mine, other, *arrays)
    parts = exchange(parts, ("xl",) + tp_axes).reshape(XL * TP, OUT_COLS, ROWS, HD)
    return call(
        sum_body, jax.ShapeDtypeStruct((STEPS, SLOTS, OUT_COLS * HD), BF16), [vmem()]
    )(parts)


def solution(mesh):
    rep, tp = ("xl", "z", "core"), ("y", "xh")
    parts = Mesh(mesh.devices.reshape(XL, Z, CORE, 4, 2), rep + tp)
    placed = (
        P(rep, tp, None, None),
        P(rep),
        P(rep, None),
        P(rep, None),
        P(None, rep, tp, None),
        P(None, rep, tp, None),
        P(tp + rep, None, None),
        P(tp + rep),
        P(tp + rep),
    )
    return jax.shard_map(
        shards, mesh=parts, in_specs=placed, out_specs=P(None, rep, tp), check_vma=False
    )
```

```python
import math

import jax
import jax.numpy as jnp
from jax import lax
from jax.experimental import pallas as pl
from jax.experimental.pallas import tpu as pltpu
from jax.sharding import Mesh, PartitionSpec as P

BF16, F32, I32 = jnp.bfloat16, jnp.float32, jnp.int32

XL, Z, CORE, TP = 2, 8, 2, 8
REP = XL * Z * CORE

HD = 128
SLOTS = 16
STEPS = 2
HEADS = 8
CTX = 256
MOVE = 13
STAY = SLOTS - MOVE
COLS = 40
OUT_COLS = COLS // TP
OWN = 10
ROWS = SLOTS * STEPS
PACK = STEPS * HEADS + 2 * STEPS

ROUND, PAIR_ROUND, ME, HEAD, COL, SCALE, DEP, DEST, LEN = 0, 1, 2, 3, 13, 23, 33, 46, 59

VMEM_LIMIT = 16 * 1024 * 1024


def smem():
    return pl.BlockSpec(memory_space=pltpu.SMEM)


def vmem():
    return pl.BlockSpec(memory_space=pltpu.VMEM)


def hbm():
    return pl.BlockSpec(memory_space=pltpu.HBM)


def call(body, out_shape, in_specs, scratch=(), **kw):
    single = not isinstance(out_shape, (list, tuple))
    return pl.pallas_call(
        body,
        out_shape=out_shape,
        in_specs=in_specs,
        out_specs=vmem() if single else [vmem()] * len(out_shape),
        scratch_shapes=list(scratch),
        compiler_params=pltpu.CompilerParams(vmem_limit_bytes=VMEM_LIMIT),
        **kw,
    )


def copy_in(pairs, sems):
    copies = [pltpu.make_async_copy(a, b, sems.at[i]) for i, (a, b) in enumerate(pairs)]
    for c in copies:
        c.start()
    for c in copies:
        c.wait()


def notice_body(place, *refs):
    given, (notice, packs), held, sems = refs[:7], refs[7:9], refs[9:16], refs[16]
    copy_in(zip(given, held), sems)
    dep, dest, lengths, ids, scales, queries, fresh = held
    row = lax.broadcasted_iota(I32, (REP, HD), 0)
    lane = lax.broadcasted_iota(I32, (REP, HD), 1)
    base = place[0]
    pair_row = lax.rem(row + REP // XL, REP)
    out = jnp.where(lane == ME, row, -1).astype(F32)
    for k in range(MOVE):
        out = jnp.where((lane == ROUND) & (row == dest[0, k]), float(k), out)
        out = jnp.where((lane == PAIR_ROUND) & (pair_row == dest[0, k]), float(k), out)
        out = jnp.where(lane == DEP + k, dep[0, k].astype(F32), out)
        out = jnp.where(lane == DEST + k, dest[0, k].astype(F32), out)
    for n in range(OWN):
        place_n = ids[n] - base
        head = lax.div(place_n, COLS)
        out = jnp.where(lane == HEAD + n, head.astype(F32), out)
        out = jnp.where(lane == COL + n, (place_n - head * COLS).astype(F32), out)
        out = jnp.where(lane == SCALE + n, scales[n], out)
    for s in range(SLOTS):
        out = jnp.where(lane == LEN + s, lengths[s].astype(F32), out)
    notice[:, 0, :] = out
    for s in range(SLOTS):
        packs[s] = jnp.concatenate(
            [queries[t, s] for t in range(STEPS)]
            + [fresh[t, s : s + 1, j * HD : (j + 1) * HD] for t in range(STEPS) for j in range(2)],
            axis=0,
        )


def at(notices, rep, lane):
    return notices[rep, 0, lane].astype(I32)


def pull_body(notices, packs, out):
    me = at(notices, 0, ME)

    def one(peer, carry):
        turn = at(notices, peer, ROUND)
        out[peer] = packs[at(notices, me, DEP + jnp.maximum(turn, 0))]
        return carry

    lax.fori_loop(0, REP, one, 0, unroll=4)


def score(pack, keys, length):
    per = STEPS * HEADS
    sc = lax.dot_general(
        pack[:per], keys, (((1,), (1,)), ((), ())), preferred_element_type=F32
    )
    pos = lax.broadcasted_iota(I32, (per, CTX), 1)
    return jnp.where(pos < length, sc * (1.0 / math.sqrt(HD)), -jnp.inf)


def blend(pack, sc, values):
    per = STEPS * HEADS
    step = lax.broadcasted_iota(I32, (per, 1), 0) // HEADS
    top = jnp.max(sc, axis=1, keepdims=True)
    expo = jnp.exp(sc - top)
    total = jnp.sum(expo, axis=1, keepdims=True)
    carried = jnp.dot(expo.astype(BF16), values, preferred_element_type=F32)
    pack = pack.astype(F32)
    q = pack[:per]
    peak = top
    extra = []
    for u in range(STEPS):
        f = jnp.sum(q * pack[per + 2 * u : per + 2 * u + 1], axis=1, keepdims=True)
        f = jnp.where(step >= u, f * (1.0 / math.sqrt(HD)), -jnp.inf)
        extra.append(f)
        peak = jnp.maximum(peak, f)
    factor = jnp.exp(top - peak)
    denom = total * factor
    numer = carried * factor
    for u in range(STEPS):
        w = jnp.exp(extra[u] - peak)
        denom = denom + w
        numer = numer + w * pack[per + 2 * u + 1 : per + 2 * u + 2]
    return (numer / denom).astype(BF16)


def stay_body(dep_in, lengths_in, packs, cache, out, dep, lengths, held, leaves, sems):
    copy_in([(dep_in, dep), (lengths_in, lengths)], sems.at[SLOTS:])
    for s in range(SLOTS):
        leaves[s] = 0
    for k in range(MOVE):
        leaves[dep[0, k]] = 1

    def copy(s):
        return pltpu.make_async_copy(cache.at[s], held.at[s], sems.at[s])

    def start(s, carry):
        @pl.when(leaves[s] == 0)
        def _():
            copy(s).start()

        return carry

    def one(s, carry):
        @pl.when(leaves[s] == 0)
        def _():
            copy(s).wait()
            pack = packs[s]
            sc = score(pack, held[s, 0, :, :HD], lengths[s])
            out[s] = blend(pack, sc, held[s, 0, :, HD:])

        return carry

    lax.fori_loop(0, SLOTS, start, 0)
    lax.fori_loop(0, SLOTS, one, 0)


def attend_body(notices, pulled, packs, cache, send, out, scores, held):
    per = STEPS * HEADS
    me = at(notices, 0, ME)
    for s in range(SLOTS):
        held[s] = packs[s]
    for k in range(MOVE):
        held[at(notices, me, DEP + k)] = pulled[at(notices, me, DEST + k)]
    for s in range(SLOTS):
        scores[s] = score(held[s], cache[s, 0, :, :HD], at(notices, me, LEN + s))
    for s in range(SLOTS):
        out[s] = blend(held[s], scores[s], cache[s, 0, :, HD:])
    for k in range(MOVE):
        goal = at(notices, me, DEST + k)
        rows = out[at(notices, me, DEP + k)]
        send[goal, :per, :] = rows
        send[lax.rem(goal + REP // XL, REP), per:, :] = rows


def project_body(notices, came, mine, other, *rest):
    arrays, out, slots, rows, total = rest[:-4], rest[-4], rest[-3], rest[-2], rest[-1]
    per = STEPS * HEADS
    me = at(notices, 0, ME)
    pair = lax.rem(me + REP // XL, REP)
    xl, z, core = lax.div(me, Z * CORE), lax.rem(lax.div(me, CORE), Z), lax.rem(me, CORE)
    first, second = xl * SLOTS, (1 - xl) * SLOTS
    for s in range(SLOTS):
        slots[pl.ds(pl.multiple_of((first + s) * per, per), per), :] = mine[s].astype(F32)
        slots[pl.ds(pl.multiple_of((second + s) * per, per), per), :] = other[s].astype(F32)

    def place_rows(peer, carry):
        for lane, owner, start, lo in ((ROUND, me, first, 0), (PAIR_ROUND, pair, second, per)):
            turn = at(notices, peer, lane)
            slot = start + at(notices, owner, DEP + jnp.maximum(turn, 0))
            goal = jnp.where(turn >= 0, slot, XL * SLOTS)
            slots[pl.ds(pl.multiple_of(goal * per, per), per), :] = came[
                peer, lo : lo + per, :
            ].astype(F32)
        return carry

    lax.fori_loop(0, REP, place_rows, 0, unroll=4)
    for h in range(HEADS):
        for side in range(XL):
            for t in range(STEPS):
                lo = side * ROWS + t * SLOTS
                rows[h, lo : lo + SLOTS, :] = slots[
                    pl.ds(side * SLOTS * per + t * HEADS + h, SLOTS, stride=per), :
                ].astype(BF16)
    total[...] = jnp.zeros_like(total)

    def run(blocks, first, z_src, core_src):
        src = (xl * Z + z_src) * CORE + core_src
        for lo in range(0, OWN, 5):
            products = []
            for n in range(lo, lo + 5):
                products.append(
                    jnp.dot(
                        rows[at(notices, src, HEAD + n)],
                        blocks[first + n],
                        preferred_element_type=F32,
                    )
                    * notices[src, 0, SCALE + n]
                )
            for n in range(lo, lo + 5):
                total[at(notices, src, COL + n)] += products[n - lo]

    half = Z // 2
    for line, same, cross in (
        (core, arrays[: half + 1], arrays[half + 1 : Z + 1]),
        (1 - core, (None, *arrays[Z + 1 : Z + half + 1]), (None, *arrays[Z + half + 1 :])),
    ):
        for step in range(half + 1):
            far = lax.rem(z - (1 - 2 * line) * step + Z, Z)
            if same[step] is not None:
                run(same[step], 0, far, line)
            if step < half and cross[step] is not None:
                run(cross[step], 0, far, 1 - line)
    out[:COLS] = total[:, :ROWS, :].astype(BF16)
    out[COLS:] = total[:, ROWS:, :].astype(BF16)


def sum_body(parts, out):
    for c in range(OUT_COLS):
        acc = parts[0, c].astype(F32)
        for t in range(1, XL * TP):
            acc = acc + parts[t, c].astype(F32)
        acc = acc.astype(BF16)
        for t in range(STEPS):
            out[t, :, c * HD : (c + 1) * HD] = acc[t * SLOTS : (t + 1) * SLOTS, :]


def shards(kv_cache, lengths, departing, destination, queries, new_kv, codes, scales, block_slot):
    rep_axes, tp_axes = ("xl", "z", "core"), ("y", "xh")
    base = lax.axis_index(tp_axes) * (HEADS * COLS)
    per = STEPS * HEADS

    def in_hbm(x):
        return pltpu.with_memory_space_constraint(x, pltpu.HBM)

    def exchange(x, axes):
        return lax.all_to_all(x, axes, split_axis=0, concat_axis=0, tiled=True)

    def swap(x, axis):
        return lax.ppermute(x, axis, [(0, 1), (1, 0)])

    def around(x, hops):
        pairs = [
            (i * CORE + c, ((i + hops * (1 - 2 * c)) % Z) * CORE + c)
            for i in range(Z)
            for c in range(CORE)
        ]
        return lax.ppermute(x, ("z", "core"), pairs)

    sib = swap(codes, "core")
    given = [
        departing,
        destination,
        lengths,
        block_slot,
        scales,
        queries,
        new_kv.reshape(STEPS, SLOTS, 2 * HD),
    ]
    notice, packs = call(
        notice_body,
        [
            jax.ShapeDtypeStruct((REP, 1, HD), F32),
            jax.ShapeDtypeStruct((SLOTS, PACK, HD), BF16),
        ],
        [smem()] + [hbm()] * len(given),
        [pltpu.SMEM(a.shape, a.dtype) for a in given[:5]]
        + [pltpu.VMEM(a.shape, a.dtype) for a in given[5:]]
        + [pltpu.SemaphoreType.DMA((len(given),))],
    )(base.astype(I32)[None], *(in_hbm(a) for a in given))
    cache = in_hbm(kv_cache)
    sib, notice = lax.optimization_barrier((sib, notice))
    near, near_x = around(codes, 1), around(sib, 1)
    notices = exchange(notice, rep_axes)
    stays = call(
        stay_body,
        jax.ShapeDtypeStruct((SLOTS, per, HD), BF16),
        [hbm()] * 2 + [vmem(), hbm()],
        [
            pltpu.SMEM(departing.shape, I32),
            pltpu.SMEM(lengths.shape, I32),
            pltpu.VMEM(kv_cache.shape, BF16),
            pltpu.SMEM((SLOTS,), I32),
            pltpu.SemaphoreType.DMA((SLOTS + 2,)),
        ],
    )(in_hbm(departing), in_hbm(lengths), packs, cache)
    near, stays = lax.optimization_barrier((near, stays))
    near_x, notices = lax.optimization_barrier((near_x, notices))
    two, two_x = around(near, 1), around(near_x, 1)
    near_sib, near_x_sib = swap(near, "core"), swap(near_x, "core")
    other = swap(stays, "xl")
    to_pull = call(
        pull_body, jax.ShapeDtypeStruct((REP, PACK, HD), BF16), [smem(), vmem()]
    )(notices, packs)
    pulled = exchange(to_pull, rep_axes)
    three, three_x = around(two, 1), around(two_x, 1)
    two_sib, two_x_sib = swap(two, "core"), swap(two_x, "core")
    send, mine = call(
        attend_body,
        [
            jax.ShapeDtypeStruct((REP, 2 * per, HD), BF16),
            jax.ShapeDtypeStruct((SLOTS, per, HD), BF16),
        ],
        [smem()] + [vmem()] * 3,
        [pltpu.VMEM((SLOTS, per, CTX), F32), pltpu.VMEM((SLOTS, PACK, HD), BF16)],
    )(notices, pulled, packs, kv_cache)
    came = exchange(send, rep_axes)
    four = around(three, 1)
    three_sib, three_x_sib = swap(three, "core"), swap(three_x, "core")
    four_sib = around(three_x, 1)
    arrays = [codes, near, two, three, four, sib, near_x, two_x, three_x]
    arrays += [near_sib, two_sib, three_sib, four_sib, near_x_sib, two_x_sib, three_x_sib]
    parts = call(
        project_body,
        jax.ShapeDtypeStruct((XL * COLS, ROWS, HD), BF16),
        [smem()] + [vmem()] * (3 + len(arrays)),
        [
            pltpu.VMEM(((XL * SLOTS + 1) * per, HD), F32),
            pltpu.VMEM((HEADS, XL * ROWS, HD), BF16),
            pltpu.VMEM((COLS, XL * ROWS, HD), F32),
        ],
    )(notices, came, mine, other, *arrays)
    parts = exchange(parts, ("xl",) + tp_axes).reshape(XL * TP, OUT_COLS, ROWS, HD)
    return call(
        sum_body, jax.ShapeDtypeStruct((STEPS, SLOTS, OUT_COLS * HD), BF16), [vmem()]
    )(parts)


def solution(mesh):
    rep, tp = ("xl", "z", "core"), ("y", "xh")
    parts = Mesh(mesh.devices.reshape(XL, Z, CORE, 4, 2), rep + tp)
    placed = (
        P(rep, tp, None, None),
        P(rep),
        P(rep, None),
        P(rep, None),
        P(None, rep, tp, None),
        P(None, rep, tp, None),
        P(tp + rep, None, None),
        P(tp + rep),
        P(tp + rep),
    )
    return jax.shard_map(
        shards, mesh=parts, in_specs=placed, out_specs=P(None, rep, tp), check_vma=False
    )
```

```python
import math

import jax
import jax.numpy as jnp
from jax import lax
from jax.experimental import pallas as pl
from jax.experimental.pallas import tpu as pltpu
from jax.sharding import Mesh, PartitionSpec as P

BF16, F32, I32 = jnp.bfloat16, jnp.float32, jnp.int32

XL, Z, CORE, TP = 2, 8, 2, 8
REP = XL * Z * CORE

HD = 128
SLOTS = 16
STEPS = 2
HEADS = 8
CTX = 256
MOVE = 13
STAY = SLOTS - MOVE
COLS = 40
OUT_COLS = COLS // TP
OWN = 10
ROWS = SLOTS * STEPS
PACK = STEPS * HEADS + 2 * STEPS

ROUND, PAIR_ROUND, ME, HEAD, COL, SCALE, DEP, DEST, LEN = 0, 1, 2, 3, 13, 23, 33, 46, 59

VMEM_LIMIT = 16 * 1024 * 1024


def smem():
    return pl.BlockSpec(memory_space=pltpu.SMEM)


def vmem():
    return pl.BlockSpec(memory_space=pltpu.VMEM)


def hbm():
    return pl.BlockSpec(memory_space=pltpu.HBM)


def spec(shape):
    return vmem() if isinstance(shape, jax.ShapeDtypeStruct) else hbm()


def call(body, out_shape, in_specs, scratch=(), **kw):
    single = not isinstance(out_shape, (list, tuple))
    return pl.pallas_call(
        body,
        out_shape=out_shape,
        in_specs=in_specs,
        out_specs=spec(out_shape) if single else [spec(o) for o in out_shape],
        scratch_shapes=list(scratch),
        compiler_params=pltpu.CompilerParams(vmem_limit_bytes=VMEM_LIMIT),
        **kw,
    )


def copy_in(pairs, sems):
    copies = [pltpu.make_async_copy(a, b, sems.at[i]) for i, (a, b) in enumerate(pairs)]
    for c in copies:
        c.start()
    for c in copies:
        c.wait()


def notice_body(place, *refs):
    given, (notice, packs), held, sems = refs[:7], refs[7:9], refs[9:16], refs[16]
    copy_in(zip(given, held), sems)
    dep, dest, lengths, ids, scales, queries, fresh = held
    row = lax.broadcasted_iota(I32, (REP, HD), 0)
    lane = lax.broadcasted_iota(I32, (REP, HD), 1)
    base = place[0]
    pair_row = lax.rem(row + REP // XL, REP)
    out = jnp.where(lane == ME, row, -1).astype(F32)
    for k in range(MOVE):
        out = jnp.where((lane == ROUND) & (row == dest[0, k]), float(k), out)
        out = jnp.where((lane == PAIR_ROUND) & (pair_row == dest[0, k]), float(k), out)
        out = jnp.where(lane == DEP + k, dep[0, k].astype(F32), out)
        out = jnp.where(lane == DEST + k, dest[0, k].astype(F32), out)
    for n in range(OWN):
        place_n = ids[n] - base
        head = lax.div(place_n, COLS)
        out = jnp.where(lane == HEAD + n, head.astype(F32), out)
        out = jnp.where(lane == COL + n, (place_n - head * COLS).astype(F32), out)
        out = jnp.where(lane == SCALE + n, scales[n], out)
    for s in range(SLOTS):
        out = jnp.where(lane == LEN + s, lengths[s].astype(F32), out)
    notice[:, 0, :] = out
    for s in range(SLOTS):
        packs[s] = jnp.concatenate(
            [queries[t, s] for t in range(STEPS)]
            + [fresh[t, s : s + 1, j * HD : (j + 1) * HD] for t in range(STEPS) for j in range(2)],
            axis=0,
        )


def at(notices, rep, lane):
    return notices[rep, 0, lane].astype(I32)


def pull_body(notices, packs, out, sems):
    me = at(notices, 0, ME)

    def copy(peer):
        slot = at(notices, me, DEP + jnp.maximum(at(notices, peer, ROUND), 0))
        return pltpu.make_async_copy(packs.at[slot], out.at[peer], sems.at[peer])

    def start(peer, carry):
        copy(peer).start()
        return carry

    def wait(peer, carry):
        pltpu.make_async_copy(packs.at[0], out.at[peer], sems.at[peer]).wait()
        return carry

    lax.fori_loop(0, REP, start, 0, unroll=8)
    lax.fori_loop(0, REP, wait, 0, unroll=8)


def score(pack, keys, length):
    per = STEPS * HEADS
    sc = lax.dot_general(
        pack[:per], keys, (((1,), (1,)), ((), ())), preferred_element_type=F32
    )
    pos = lax.broadcasted_iota(I32, (per, CTX), 1)
    return jnp.where(pos < length, sc * (1.0 / math.sqrt(HD)), -jnp.inf)


def blend(pack, sc, values):
    per = STEPS * HEADS
    step = lax.broadcasted_iota(I32, (per, 1), 0) // HEADS
    top = jnp.max(sc, axis=1, keepdims=True)
    expo = jnp.exp(sc - top)
    total = jnp.sum(expo, axis=1, keepdims=True)
    carried = jnp.dot(expo.astype(BF16), values, preferred_element_type=F32)
    pack = pack.astype(F32)
    q = pack[:per]
    peak = top
    extra = []
    for u in range(STEPS):
        f = jnp.sum(q * pack[per + 2 * u : per + 2 * u + 1], axis=1, keepdims=True)
        f = jnp.where(step >= u, f * (1.0 / math.sqrt(HD)), -jnp.inf)
        extra.append(f)
        peak = jnp.maximum(peak, f)
    factor = jnp.exp(top - peak)
    denom = total * factor
    numer = carried * factor
    for u in range(STEPS):
        w = jnp.exp(extra[u] - peak)
        denom = denom + w
        numer = numer + w * pack[per + 2 * u + 1 : per + 2 * u + 2]
    return (numer / denom).astype(BF16)


def stay_body(dep_in, lengths_in, packs, cache, out, dep, lengths, held, leaves, sems):
    copy_in([(dep_in, dep), (lengths_in, lengths)], sems.at[SLOTS:])
    for s in range(SLOTS):
        leaves[s] = 0
    for k in range(MOVE):
        leaves[dep[0, k]] = 1

    def copy(s):
        return pltpu.make_async_copy(cache.at[s], held.at[s], sems.at[s])

    def start(s, carry):
        @pl.when(leaves[s] == 0)
        def _():
            copy(s).start()

        return carry

    def one(s, carry):
        @pl.when(leaves[s] == 0)
        def _():
            copy(s).wait()
            pack = packs[s]
            sc = score(pack, held[s, 0, :, :HD], lengths[s])
            out[s] = blend(pack, sc, held[s, 0, :, HD:])

        return carry

    lax.fori_loop(0, SLOTS, start, 0)
    lax.fori_loop(0, SLOTS, one, 0)


def attend_body(notices, pulled, packs, cache, send, out, scores, held, sems):
    per = STEPS * HEADS
    me = at(notices, 0, ME)
    for s in range(SLOTS):
        held[s] = packs[s]
    for k in range(MOVE):
        held[at(notices, me, DEP + k)] = pulled[at(notices, me, DEST + k)]
    for s in range(SLOTS):
        scores[s] = score(held[s], cache[s, 0, :, :HD], at(notices, me, LEN + s))
    for s in range(SLOTS):
        out[s] = blend(held[s], scores[s], cache[s, 0, :, HD:])
    copies = []
    for k in range(MOVE):
        goal = at(notices, me, DEST + k)
        rows = out.at[at(notices, me, DEP + k)]
        for side, to in enumerate((goal, lax.rem(goal + REP // XL, REP))):
            where = send.at[to, side * per : (side + 1) * per, :]
            copies.append(pltpu.make_async_copy(rows, where, sems.at[k, side]))
            copies[-1].start()
    for c in copies:
        c.wait()


def add_blocks(notices, rows, total, blocks, line, step, origin):
    me = at(notices, 0, ME)
    xl, z = lax.div(me, Z * CORE), lax.rem(lax.div(me, CORE), Z)
    far = lax.rem(z - (1 - 2 * line) * step + Z, Z)
    src = (xl * Z + far) * CORE + origin
    for lo in range(0, OWN, 5):
        products = []
        for n in range(lo, lo + 5):
            products.append(
                jnp.dot(
                    rows[at(notices, src, HEAD + n)], blocks[n], preferred_element_type=F32
                )
                * notices[src, 0, SCALE + n]
            )
        for n in range(lo, lo + 5):
            total[at(notices, src, COL + n)] += products[n - lo]


def project_body(notices, came, mine, other, *rest):
    arrays, rows, total, slots = rest[:-3], rest[-3], rest[-2], rest[-1]
    per = STEPS * HEADS
    me = at(notices, 0, ME)
    pair = lax.rem(me + REP // XL, REP)
    xl, core = lax.div(me, Z * CORE), lax.rem(me, CORE)
    first, second = xl * SLOTS, (1 - xl) * SLOTS
    for s in range(SLOTS):
        slots[pl.ds(pl.multiple_of((first + s) * per, per), per), :] = mine[s].astype(F32)
        slots[pl.ds(pl.multiple_of((second + s) * per, per), per), :] = other[s].astype(F32)

    def place_rows(peer, carry):
        for lane, owner, start, lo in ((ROUND, me, first, 0), (PAIR_ROUND, pair, second, per)):
            turn = at(notices, peer, lane)
            slot = start + at(notices, owner, DEP + jnp.maximum(turn, 0))
            goal = jnp.where(turn >= 0, slot, XL * SLOTS)
            slots[pl.ds(pl.multiple_of(goal * per, per), per), :] = came[
                peer, lo : lo + per, :
            ].astype(F32)
        return carry

    lax.fori_loop(0, REP, place_rows, 0, unroll=4)
    for h in range(HEADS):
        for side in range(XL):
            for t in range(STEPS):
                lo = side * ROWS + t * SLOTS
                rows[h, lo : lo + SLOTS, :] = slots[
                    pl.ds(side * SLOTS * per + t * HEADS + h, SLOTS, stride=per), :
                ].astype(BF16)
    total[...] = jnp.zeros_like(total)
    half = Z // 2
    steps = [(0, core, core), (0, core, 1 - core)]
    steps += [(i, core, core) for i in range(1, half)]
    steps += [(i, core, 1 - core) for i in range(1, half)]
    steps += [(i, 1 - core, 1 - core) for i in range(1, half)]
    steps += [(i, 1 - core, core) for i in range(1, half)]
    for blocks, (step, line, origin) in zip(arrays, steps):
        add_blocks(notices, rows, total, blocks, line, step, origin)


def last_body(notices, rows, so_far, four, four_x, out, total):
    core = lax.rem(at(notices, 0, ME), CORE)
    total[...] = so_far[...]
    add_blocks(notices, rows, total, four, core, Z // 2, core)
    add_blocks(notices, rows, total, four_x, core, Z // 2, 1 - core)
    out[:COLS] = total[:, :ROWS, :].astype(BF16)
    out[COLS:] = total[:, ROWS:, :].astype(BF16)


def sum_body(parts, out):
    for c in range(OUT_COLS):
        acc = parts[0, c].astype(F32)
        for t in range(1, XL * TP):
            acc = acc + parts[t, c].astype(F32)
        acc = acc.astype(BF16)
        for t in range(STEPS):
            out[t, :, c * HD : (c + 1) * HD] = acc[t * SLOTS : (t + 1) * SLOTS, :]


def shards(kv_cache, lengths, departing, destination, queries, new_kv, codes, scales, block_slot):
    rep_axes, tp_axes = ("xl", "z", "core"), ("y", "xh")
    base = lax.axis_index(tp_axes) * (HEADS * COLS)
    per = STEPS * HEADS

    def in_hbm(x):
        return pltpu.with_memory_space_constraint(x, pltpu.HBM)

    def exchange(x, axes):
        return lax.all_to_all(x, axes, split_axis=0, concat_axis=0, tiled=True)

    def swap(x, axis):
        return lax.ppermute(x, axis, [(0, 1), (1, 0)])

    def around(x, hops):
        pairs = [
            (i * CORE + c, ((i + hops * (1 - 2 * c)) % Z) * CORE + c)
            for i in range(Z)
            for c in range(CORE)
        ]
        return lax.ppermute(x, ("z", "core"), pairs)

    sib = swap(codes, "core")
    given = [
        departing,
        destination,
        lengths,
        block_slot,
        scales,
        queries,
        new_kv.reshape(STEPS, SLOTS, 2 * HD),
    ]
    notice, packs = call(
        notice_body,
        [
            jax.ShapeDtypeStruct((REP, 1, HD), F32),
            jax.ShapeDtypeStruct((SLOTS, PACK, HD), BF16),
        ],
        [smem()] + [hbm()] * len(given),
        [pltpu.SMEM(a.shape, a.dtype) for a in given[:5]]
        + [pltpu.VMEM(a.shape, a.dtype) for a in given[5:]]
        + [pltpu.SemaphoreType.DMA((len(given),))],
    )(base.astype(I32)[None], *(in_hbm(a) for a in given))
    cache = in_hbm(kv_cache)
    sib, notice = lax.optimization_barrier((sib, notice))
    near, near_x = around(codes, 1), around(sib, 1)
    notices = exchange(notice, rep_axes)
    stays = call(
        stay_body,
        jax.ShapeDtypeStruct((SLOTS, per, HD), BF16),
        [hbm()] * 2 + [vmem(), hbm()],
        [
            pltpu.SMEM(departing.shape, I32),
            pltpu.SMEM(lengths.shape, I32),
            pltpu.VMEM(kv_cache.shape, BF16),
            pltpu.SMEM((SLOTS,), I32),
            pltpu.SemaphoreType.DMA((SLOTS + 2,)),
        ],
    )(in_hbm(departing), in_hbm(lengths), packs, cache)
    near, stays = lax.optimization_barrier((near, stays))
    near_x, notices = lax.optimization_barrier((near_x, notices))
    two, two_x = around(near, 1), around(near_x, 1)
    other = swap(stays, "xl")
    to_pull = call(
        pull_body,
        pltpu.HBM((REP, PACK, HD), BF16),
        [smem(), vmem()],
        [pltpu.SemaphoreType.DMA((REP,))],
    )(notices, packs)
    pulled = exchange(to_pull, rep_axes)
    three, three_x = around(two, 1), around(two_x, 1)
    send, mine = call(
        attend_body,
        [
            pltpu.HBM((REP, 2 * per, HD), BF16),
            jax.ShapeDtypeStruct((SLOTS, per, HD), BF16),
        ],
        [smem()] + [vmem()] * 3,
        [
            pltpu.VMEM((SLOTS, per, CTX), F32),
            pltpu.VMEM((SLOTS, PACK, HD), BF16),
            pltpu.SemaphoreType.DMA((MOVE, 2)),
        ],
    )(notices, pulled, packs, kv_cache)
    came = exchange(send, rep_axes)
    four, four_x = around(three, 1), around(three_x, 1)
    rows, total = call(
        project_body,
        [
            jax.ShapeDtypeStruct((HEADS, XL * ROWS, HD), BF16),
            jax.ShapeDtypeStruct((COLS, XL * ROWS, HD), F32),
        ],
        [smem()] + [vmem()] * 17,
        [pltpu.VMEM(((XL * SLOTS + 1) * per, HD), F32)],
    )(
        *(notices, came, mine, other),
        *(codes, sib, near, two, three, near_x, two_x, three_x),
        *(swap(x, "core") for x in (near, two, three, near_x, two_x, three_x)),
    )
    parts = call(
        last_body,
        jax.ShapeDtypeStruct((XL * COLS, ROWS, HD), BF16),
        [smem()] + [vmem()] * 4,
        [pltpu.VMEM((COLS, XL * ROWS, HD), F32)],
    )(notices, rows, total, four, four_x)
    parts = exchange(parts, ("xl",) + tp_axes).reshape(XL * TP, OUT_COLS, ROWS, HD)
    return call(
        sum_body, jax.ShapeDtypeStruct((STEPS, SLOTS, OUT_COLS * HD), BF16), [vmem()]
    )(parts)


def solution(mesh):
    rep, tp = ("xl", "z", "core"), ("y", "xh")
    parts = Mesh(mesh.devices.reshape(XL, Z, CORE, 4, 2), rep + tp)
    placed = (
        P(rep, tp, None, None),
        P(rep),
        P(rep, None),
        P(rep, None),
        P(None, rep, tp, None),
        P(None, rep, tp, None),
        P(tp + rep, None, None),
        P(tp + rep),
        P(tp + rep),
    )
    return jax.shard_map(
        shards, mesh=parts, in_specs=placed, out_specs=P(None, rep, tp), check_vma=False
    )
```

```python
import math

import jax
import jax.numpy as jnp
from jax import lax
from jax.experimental import pallas as pl
from jax.experimental.pallas import tpu as pltpu
from jax.sharding import Mesh, PartitionSpec as P

BF16, F32, I32 = jnp.bfloat16, jnp.float32, jnp.int32

XL, Z, CORE, TP = 2, 8, 2, 8
REP = XL * Z * CORE

HD = 128
SLOTS = 16
STEPS = 2
HEADS = 8
CTX = 256
MOVE = 13
STAY = SLOTS - MOVE
COLS = 40
OUT_COLS = COLS // TP
OWN = 10
ROWS = SLOTS * STEPS
PACK = STEPS * HEADS + 2 * STEPS

ROUND, PAIR_ROUND, ME, HEAD, COL, SCALE, DEP, DEST, LEN = 0, 1, 2, 3, 13, 23, 33, 46, 59

VMEM_LIMIT = 16 * 1024 * 1024


def smem():
    return pl.BlockSpec(memory_space=pltpu.SMEM)


def vmem():
    return pl.BlockSpec(memory_space=pltpu.VMEM)


def hbm():
    return pl.BlockSpec(memory_space=pltpu.HBM)


def call(body, out_shape, in_specs, scratch=(), out_specs=None, **kw):
    single = not isinstance(out_shape, (list, tuple))
    return pl.pallas_call(
        body,
        out_shape=out_shape,
        in_specs=in_specs,
        out_specs=out_specs or (vmem() if single else [vmem()] * len(out_shape)),
        scratch_shapes=list(scratch),
        compiler_params=pltpu.CompilerParams(vmem_limit_bytes=VMEM_LIMIT),
        **kw,
    )


def copy_in(pairs, sems):
    copies = [pltpu.make_async_copy(a, b, sems.at[i]) for i, (a, b) in enumerate(pairs)]
    for c in copies:
        c.start()
    for c in copies:
        c.wait()


def notice_body(place, *refs):
    given, notice, held, sems = refs[:5], refs[5], refs[6:11], refs[11]
    copy_in(zip(given, held), sems)
    dep, dest, lengths, ids, scales = held
    row = lax.broadcasted_iota(I32, (REP, HD), 0)
    lane = lax.broadcasted_iota(I32, (REP, HD), 1)
    base = place[0]
    pair_row = lax.rem(row + REP // XL, REP)
    out = jnp.where(lane == ME, row, -1).astype(F32)
    for k in range(MOVE):
        out = jnp.where((lane == ROUND) & (row == dest[0, k]), float(k), out)
        out = jnp.where((lane == PAIR_ROUND) & (pair_row == dest[0, k]), float(k), out)
        out = jnp.where(lane == DEP + k, dep[0, k].astype(F32), out)
        out = jnp.where(lane == DEST + k, dest[0, k].astype(F32), out)
    for n in range(OWN):
        place_n = ids[n] - base
        head = lax.div(place_n, COLS)
        out = jnp.where(lane == HEAD + n, head.astype(F32), out)
        out = jnp.where(lane == COL + n, (place_n - head * COLS).astype(F32), out)
        out = jnp.where(lane == SCALE + n, scales[n], out)
    for s in range(SLOTS):
        out = jnp.where(lane == LEN + s, lengths[s].astype(F32), out)
    notice[:, 0, :] = out


def at(notices, rep, lane):
    return notices[rep, 0, lane].astype(I32)


def pull_body(notices, packs, out):
    me = at(notices, 0, ME)

    def one(peer, carry):
        turn = at(notices, peer, ROUND)
        out[peer] = packs[at(notices, me, DEP + jnp.maximum(turn, 0))]
        return carry

    lax.fori_loop(0, REP, one, 0, unroll=4)


def score(pack, keys, length):
    per = STEPS * HEADS
    sc = lax.dot_general(
        pack[:per], keys, (((1,), (1,)), ((), ())), preferred_element_type=F32
    )
    pos = lax.broadcasted_iota(I32, (per, CTX), 1)
    return jnp.where(pos < length, sc * (1.0 / math.sqrt(HD)), -jnp.inf)


def blend(pack, sc, values):
    per = STEPS * HEADS
    step = lax.broadcasted_iota(I32, (per, 1), 0) // HEADS
    top = jnp.max(sc, axis=1, keepdims=True)
    expo = jnp.exp(sc - top)
    total = jnp.sum(expo, axis=1, keepdims=True)
    carried = jnp.dot(expo.astype(BF16), values, preferred_element_type=F32)
    pack = pack.astype(F32)
    q = pack[:per]
    peak = top
    extra = []
    for u in range(STEPS):
        f = jnp.sum(q * pack[per + 2 * u : per + 2 * u + 1], axis=1, keepdims=True)
        f = jnp.where(step >= u, f * (1.0 / math.sqrt(HD)), -jnp.inf)
        extra.append(f)
        peak = jnp.maximum(peak, f)
    factor = jnp.exp(top - peak)
    denom = total * factor
    numer = carried * factor
    for u in range(STEPS):
        w = jnp.exp(extra[u] - peak)
        denom = denom + w
        numer = numer + w * pack[per + 2 * u + 1 : per + 2 * u + 2]
    return (numer / denom).astype(BF16)


def stay_body(dep_in, lengths_in, q_in, fresh_in, cache, out, packs, *scratch):
    dep, lengths, queries, fresh, held, leaves, sems = scratch
    copy_in(
        [(dep_in, dep), (lengths_in, lengths), (q_in, queries), (fresh_in, fresh)],
        sems.at[SLOTS:],
    )
    for s in range(SLOTS):
        leaves[s] = 0
    for k in range(MOVE):
        leaves[dep[0, k]] = 1

    def copy(s):
        return pltpu.make_async_copy(cache.at[s], held.at[s], sems.at[s])

    def start(s, carry):
        @pl.when(leaves[s] == 0)
        def _():
            copy(s).start()

        return carry

    def one(s, carry):
        @pl.when(leaves[s] == 0)
        def _():
            copy(s).wait()
            pack = packs[s]
            sc = score(pack, held[s, 0, :, :HD], lengths[s])
            out[s] = blend(pack, sc, held[s, 0, :, HD:])

        return carry

    lax.fori_loop(0, SLOTS, start, 0)
    for s in range(SLOTS):
        packs[s] = jnp.concatenate(
            [queries[t, s] for t in range(STEPS)]
            + [fresh[t, s : s + 1, j * HD : (j + 1) * HD] for t in range(STEPS) for j in range(2)],
            axis=0,
        )
    lax.fori_loop(0, SLOTS, one, 0)


def attend_body(notices, pulled, packs, cache, send, out, scores, held):
    per = STEPS * HEADS
    me = at(notices, 0, ME)
    for s in range(SLOTS):
        held[s] = packs[s]
    for k in range(MOVE):
        held[at(notices, me, DEP + k)] = pulled[at(notices, me, DEST + k)]
    for s in range(SLOTS):
        scores[s] = score(held[s], cache[s, 0, :, :HD], at(notices, me, LEN + s))
    for s in range(SLOTS):
        out[s] = blend(held[s], scores[s], cache[s, 0, :, HD:])
    for k in range(MOVE):
        goal = at(notices, me, DEST + k)
        rows = out[at(notices, me, DEP + k)]
        send[goal, :per, :] = rows
        send[lax.rem(goal + REP // XL, REP), per:, :] = rows


def add_blocks(notices, rows, total, blocks, line, step, origin):
    me = at(notices, 0, ME)
    xl, z = lax.div(me, Z * CORE), lax.rem(lax.div(me, CORE), Z)
    far = lax.rem(z - (1 - 2 * line) * step + Z, Z)
    src = (xl * Z + far) * CORE + origin
    for lo in range(0, OWN, 5):
        products = []
        for n in range(lo, lo + 5):
            products.append(
                jnp.dot(
                    rows[at(notices, src, HEAD + n)], blocks[n], preferred_element_type=F32
                )
                * notices[src, 0, SCALE + n]
            )
        for n in range(lo, lo + 5):
            total[at(notices, src, COL + n)] += products[n - lo]


def source_body(notices, out):
    me = at(notices, 0, ME)
    pair = lax.rem(me + REP // XL, REP)
    for side, owner, lane in ((0, me, ROUND), (1, pair, PAIR_ROUND)):
        for k in range(SLOTS):
            out[side, k] = 0
        for k in range(MOVE):
            out[XL + side, k] = at(notices, owner, DEP + k)
        for peer in range(REP):
            turn = at(notices, peer, lane)
            out[side, jnp.where(turn >= 0, turn, SLOTS - 1)] = peer


def project_body(notices, sources, came, mine, other, *rest):
    arrays, rows, total, slots = rest[:-3], rest[-3], rest[-2], rest[-1]
    per = STEPS * HEADS
    me = at(notices, 0, ME)
    xl, core = lax.div(me, Z * CORE), lax.rem(me, CORE)
    for side, here, start in ((0, mine, xl * SLOTS), (1, other, (1 - xl) * SLOTS)):
        for s in range(SLOTS):
            slots[pl.ds(pl.multiple_of((start + s) * per, per), per), :] = here[s].astype(F32)
        for k in range(MOVE):
            rows_k = came[sources[side, k], side * per : (side + 1) * per, :]
            goal = start + sources[XL + side, k]
            slots[pl.ds(pl.multiple_of(goal * per, per), per), :] = rows_k.astype(F32)
    for h in range(HEADS):
        for side in range(XL):
            for t in range(STEPS):
                lo = side * ROWS + t * SLOTS
                rows[h, lo : lo + SLOTS, :] = slots[
                    pl.ds(side * SLOTS * per + t * HEADS + h, SLOTS, stride=per), :
                ].astype(BF16)
    total[...] = jnp.zeros_like(total)
    half = Z // 2
    steps = [(0, core, core), (0, core, 1 - core)]
    steps += [(i, core, core) for i in range(1, half)]
    steps += [(i, core, 1 - core) for i in range(1, half)]
    steps += [(i, 1 - core, 1 - core) for i in range(1, half)]
    steps += [(i, 1 - core, core) for i in range(1, half)]
    for blocks, (step, line, origin) in zip(arrays, steps):
        add_blocks(notices, rows, total, blocks, line, step, origin)


def last_body(notices, rows, so_far, four, four_x, out, total):
    core = lax.rem(at(notices, 0, ME), CORE)
    total[...] = so_far[...]
    add_blocks(notices, rows, total, four, core, Z // 2, core)
    add_blocks(notices, rows, total, four_x, core, Z // 2, 1 - core)
    out[:COLS] = total[:, :ROWS, :].astype(BF16)
    out[COLS:] = total[:, ROWS:, :].astype(BF16)


def sum_body(parts, out):
    for c in range(OUT_COLS):
        acc = parts[0, c].astype(F32)
        for t in range(1, XL * TP):
            acc = acc + parts[t, c].astype(F32)
        acc = acc.astype(BF16)
        for t in range(STEPS):
            out[t, :, c * HD : (c + 1) * HD] = acc[t * SLOTS : (t + 1) * SLOTS, :]


def shards(kv_cache, lengths, departing, destination, queries, new_kv, codes, scales, block_slot):
    rep_axes, tp_axes = ("xl", "z", "core"), ("y", "xh")
    base = lax.axis_index(tp_axes) * (HEADS * COLS)
    per = STEPS * HEADS

    def in_hbm(x):
        return pltpu.with_memory_space_constraint(x, pltpu.HBM)

    def exchange(x, axes):
        return lax.all_to_all(x, axes, split_axis=0, concat_axis=0, tiled=True)

    def swap(x, axis):
        return lax.ppermute(x, axis, [(0, 1), (1, 0)])

    def around(x, cross=0):
        pairs = []
        for i in range(Z):
            for c in range(CORE):
                line = (c + cross) % CORE
                pairs.append((i * CORE + c, ((i + 1 - 2 * line) % Z) * CORE + line))
        return lax.ppermute(x, ("z", "core"), pairs)

    sib = swap(codes, "core")
    given = [departing, destination, lengths, block_slot, scales]
    notice = call(
        notice_body,
        jax.ShapeDtypeStruct((REP, 1, HD), F32),
        [smem()] + [hbm()] * len(given),
        [pltpu.SMEM(a.shape, a.dtype) for a in given] + [pltpu.SemaphoreType.DMA((len(given),))],
    )(base.astype(I32)[None], *(in_hbm(a) for a in given))
    cache = in_hbm(kv_cache)
    sib, notice = lax.optimization_barrier((sib, notice))
    near, near_x = around(codes), around(sib)
    notices = exchange(notice, rep_axes)
    fresh = new_kv.reshape(STEPS, SLOTS, 2 * HD)
    stays, packs = call(
        stay_body,
        [
            jax.ShapeDtypeStruct((SLOTS, per, HD), BF16),
            jax.ShapeDtypeStruct((SLOTS, PACK, HD), BF16),
        ],
        [hbm()] * 5,
        [
            pltpu.SMEM(departing.shape, I32),
            pltpu.SMEM(lengths.shape, I32),
            pltpu.VMEM(queries.shape, BF16),
            pltpu.VMEM(fresh.shape, BF16),
            pltpu.VMEM(kv_cache.shape, BF16),
            pltpu.SMEM((SLOTS,), I32),
            pltpu.SemaphoreType.DMA((SLOTS + 4,)),
        ],
    )(*(in_hbm(a) for a in (departing, lengths, queries, fresh)), cache)
    near, stays = lax.optimization_barrier((near, stays))
    near_x, notices = lax.optimization_barrier((near_x, notices))
    two, two_x = around(near), around(near_x)
    other = swap(stays, "xl")
    sources = call(
        source_body, jax.ShapeDtypeStruct((2 * XL, SLOTS), I32), [smem()], out_specs=smem()
    )(notices)
    to_pull = call(
        pull_body, jax.ShapeDtypeStruct((REP, PACK, HD), BF16), [smem(), vmem()]
    )(notices, packs)
    pulled = exchange(to_pull, rep_axes)
    three, three_x = around(two), around(two_x)
    send, mine = call(
        attend_body,
        [
            jax.ShapeDtypeStruct((REP, 2 * per, HD), BF16),
            jax.ShapeDtypeStruct((SLOTS, per, HD), BF16),
        ],
        [smem()] + [vmem()] * 3,
        [pltpu.VMEM((SLOTS, per, CTX), F32), pltpu.VMEM((SLOTS, PACK, HD), BF16)],
    )(notices, pulled, packs, kv_cache)
    came = exchange(send, rep_axes)
    four, four_x = around(three), around(three_x)
    rows, total = call(
        project_body,
        [
            jax.ShapeDtypeStruct((HEADS, XL * ROWS, HD), BF16),
            jax.ShapeDtypeStruct((COLS, XL * ROWS, HD), F32),
        ],
        [smem()] * 2 + [vmem()] * 17,
        [pltpu.VMEM((XL * SLOTS * per, HD), F32)],
    )(
        *(notices, sources, came, mine, other),
        *(codes, sib, near, two, three, near_x, two_x, three_x),
        *(swap(x, "core") for x in (near, two, three, near_x, two_x, three_x)),
    )
    parts = call(
        last_body,
        jax.ShapeDtypeStruct((XL * COLS, ROWS, HD), BF16),
        [smem()] + [vmem()] * 4,
        [pltpu.VMEM((COLS, XL * ROWS, HD), F32)],
    )(notices, rows, total, four, four_x)
    parts = exchange(parts, ("xl",) + tp_axes).reshape(XL * TP, OUT_COLS, ROWS, HD)
    return call(
        sum_body, jax.ShapeDtypeStruct((STEPS, SLOTS, OUT_COLS * HD), BF16), [vmem()]
    )(parts)


def solution(mesh):
    rep, tp = ("xl", "z", "core"), ("y", "xh")
    parts = Mesh(mesh.devices.reshape(XL, Z, CORE, 4, 2), rep + tp)
    placed = (
        P(rep, tp, None, None),
        P(rep),
        P(rep, None),
        P(rep, None),
        P(None, rep, tp, None),
        P(None, rep, tp, None),
        P(tp + rep, None, None),
        P(tp + rep),
        P(tp + rep),
    )
    return jax.shard_map(
        shards, mesh=parts, in_specs=placed, out_specs=P(None, rep, tp), check_vma=False
    )
```

```python
import math

import jax
import jax.numpy as jnp
from jax import lax
from jax.experimental import pallas as pl
from jax.experimental.pallas import tpu as pltpu
from jax.sharding import Mesh, PartitionSpec as P

BF16, F32, I32 = jnp.bfloat16, jnp.float32, jnp.int32

XL, Z, CORE, TP = 2, 8, 2, 8
REP = XL * Z * CORE

HD = 128
SLOTS = 16
STEPS = 2
HEADS = 8
CTX = 256
MOVE = 13
STAY = SLOTS - MOVE
COLS = 40
OUT_COLS = COLS // TP
OWN = 10
ROWS = SLOTS * STEPS
PACK = STEPS * HEADS + 2 * STEPS

ROUND, PAIR_ROUND, ME, HEAD, COL, SCALE, DEP, DEST, LEN = 0, 1, 2, 3, 13, 23, 33, 46, 59

SLOT_OF, PEER_OF, HEAD_OF = 0, 2 * SLOTS, 4 * SLOTS
COL_OF = HEAD_OF + 2 * Z * OWN
TABLE = COL_OF + 2 * Z * OWN

VMEM_LIMIT = 16 * 1024 * 1024


def smem():
    return pl.BlockSpec(memory_space=pltpu.SMEM)


def vmem():
    return pl.BlockSpec(memory_space=pltpu.VMEM)


def hbm():
    return pl.BlockSpec(memory_space=pltpu.HBM)


def call(body, out_shape, in_specs, scratch=(), out_specs=None, **kw):
    single = not isinstance(out_shape, (list, tuple))
    return pl.pallas_call(
        body,
        out_shape=out_shape,
        in_specs=in_specs,
        out_specs=out_specs or (vmem() if single else [vmem()] * len(out_shape)),
        scratch_shapes=list(scratch),
        compiler_params=pltpu.CompilerParams(vmem_limit_bytes=VMEM_LIMIT),
        **kw,
    )


def copy_in(pairs, sems):
    copies = [pltpu.make_async_copy(a, b, sems.at[i]) for i, (a, b) in enumerate(pairs)]
    for c in copies:
        c.start()
    for c in copies:
        c.wait()


def notice_body(place, *refs):
    given, notice, held, sems = refs[:5], refs[5], refs[6:11], refs[11]
    copy_in(zip(given, held), sems)
    dep, dest, lengths, ids, scales = held
    row = lax.broadcasted_iota(I32, (REP, HD), 0)
    lane = lax.broadcasted_iota(I32, (REP, HD), 1)
    base = place[0]
    pair_row = lax.rem(row + REP // XL, REP)
    out = jnp.where(lane == ME, row, -1).astype(F32)
    for k in range(MOVE):
        out = jnp.where((lane == ROUND) & (row == dest[0, k]), float(k), out)
        out = jnp.where((lane == PAIR_ROUND) & (pair_row == dest[0, k]), float(k), out)
        out = jnp.where(lane == DEP + k, dep[0, k].astype(F32), out)
        out = jnp.where(lane == DEST + k, dest[0, k].astype(F32), out)
    for n in range(OWN):
        place_n = ids[n] - base
        head = lax.div(place_n, COLS)
        out = jnp.where(lane == HEAD + n, head.astype(F32), out)
        out = jnp.where(lane == COL + n, (place_n - head * COLS).astype(F32), out)
        out = jnp.where(lane == SCALE + n, scales[n], out)
    for s in range(SLOTS):
        out = jnp.where(lane == LEN + s, lengths[s].astype(F32), out)
    notice[:, 0, :] = out


def at(notices, rep, lane):
    return notices[rep, 0, lane].astype(I32)


def pull_body(notices, packs, out):
    for peer in range(REP):
        out[peer] = packs[jnp.maximum(at(notices, peer, ROUND), 0)]


def score(pack, keys, length):
    per = STEPS * HEADS
    sc = lax.dot_general(
        pack[:per], keys, (((1,), (1,)), ((), ())), preferred_element_type=F32
    )
    pos = lax.broadcasted_iota(I32, (per, CTX), 1)
    return jnp.where(pos < length, sc * (1.0 / math.sqrt(HD)), -jnp.inf)


def blend(pack, sc, values):
    per = STEPS * HEADS
    step = lax.broadcasted_iota(I32, (per, 1), 0) // HEADS
    top = jnp.max(sc, axis=1, keepdims=True)
    expo = jnp.exp(sc - top)
    total = jnp.sum(expo, axis=1, keepdims=True)
    carried = jnp.dot(expo.astype(BF16), values, preferred_element_type=F32)
    pack = pack.astype(F32)
    q = pack[:per]
    peak = top
    extra = []
    for u in range(STEPS):
        f = jnp.sum(q * pack[per + 2 * u : per + 2 * u + 1], axis=1, keepdims=True)
        f = jnp.where(step >= u, f * (1.0 / math.sqrt(HD)), -jnp.inf)
        extra.append(f)
        peak = jnp.maximum(peak, f)
    factor = jnp.exp(top - peak)
    denom = total * factor
    numer = carried * factor
    for u in range(STEPS):
        w = jnp.exp(extra[u] - peak)
        denom = denom + w
        numer = numer + w * pack[per + 2 * u + 1 : per + 2 * u + 2]
    return (numer / denom).astype(BF16)


def stay_body(dep_in, lengths_in, q_in, fresh_in, cache, out, packs, *scratch):
    dep, lengths, queries, fresh, held, leaves, mine, sems = scratch
    copy_in(
        [(dep_in, dep), (lengths_in, lengths), (q_in, queries), (fresh_in, fresh)],
        sems.at[SLOTS:],
    )
    for s in range(SLOTS):
        leaves[s] = 0
    for k in range(MOVE):
        leaves[dep[0, k]] = 1

    def copy(s):
        return pltpu.make_async_copy(cache.at[s], held.at[s], sems.at[s])

    def start(s, carry):
        @pl.when(leaves[s] == 0)
        def _():
            copy(s).start()

        return carry

    def one(s, carry):
        @pl.when(leaves[s] == 0)
        def _():
            copy(s).wait()
            pack = mine[s]
            sc = score(pack, held[s, 0, :, :HD], lengths[s])
            out[s] = blend(pack, sc, held[s, 0, :, HD:])

        return carry

    lax.fori_loop(0, SLOTS, start, 0)
    for s in range(SLOTS):
        mine[s] = jnp.concatenate(
            [queries[t, s] for t in range(STEPS)]
            + [fresh[t, s : s + 1, j * HD : (j + 1) * HD] for t in range(STEPS) for j in range(2)],
            axis=0,
        )
    for k in range(MOVE):
        packs[k] = mine[dep[0, k]]
    lax.fori_loop(0, SLOTS, one, 0)


def attend_body(notices, pulled, cache, send, scores):
    per = STEPS * HEADS
    me = at(notices, 0, ME)
    slots = [at(notices, me, DEP + k) for k in range(MOVE)]
    goals = [at(notices, me, DEST + k) for k in range(MOVE)]
    for k in range(MOVE):
        length = at(notices, me, LEN + slots[k])
        scores[k] = score(pulled[goals[k]], cache[slots[k], 0, :, :HD], length)
    for k in range(MOVE):
        rows = blend(pulled[goals[k]], scores[k], cache[slots[k], 0, :, HD:])
        send[goals[k], :per, :] = rows
        send[lax.rem(goals[k] + REP // XL, REP), per:, :] = rows


def add_blocks(table, scales, rows, total, blocks, first):
    for lo in range(first, first + OWN, 5):
        products = [
            jnp.dot(rows[table[HEAD_OF + n]], blocks[n - first], preferred_element_type=F32)
            * scales[n]
            for n in range(lo, lo + 5)
        ]
        for n in range(lo, lo + 5):
            total[table[COL_OF + n]] += products[n - lo]


def table_body(notices, table, scales):
    me = at(notices, 0, ME)
    pair = lax.rem(me + REP // XL, REP)
    for side, owner, lane in ((0, me, ROUND), (1, pair, PAIR_ROUND)):
        for k in range(MOVE):
            table[SLOT_OF + side * SLOTS + k] = at(notices, owner, DEP + k)
        for peer in range(REP):
            turn = at(notices, peer, lane)
            table[PEER_OF + side * SLOTS + jnp.where(turn >= 0, turn, SLOTS - 1)] = peer
    xl, z, core = lax.div(me, Z * CORE), lax.rem(lax.div(me, CORE), Z), lax.rem(me, CORE)
    half = Z // 2
    for i, (step, line, cross) in enumerate(
        [(0, 0, 0), (0, 0, 1)]
        + [(j, 0, cross) for cross in (0, 1) for j in range(1, half)]
        + [(j, 1, cross) for cross in (0, 1) for j in range(1, half)]
        + [(half, 0, 0), (half, 0, 1)]
    ):
        on = core if line == 0 else 1 - core
        origin = on if cross == 0 else 1 - on
        far = lax.rem(z - (1 - 2 * on) * step + Z, Z)
        src = (xl * Z + far) * CORE + origin
        for n in range(OWN):
            table[HEAD_OF + i * OWN + n] = at(notices, src, HEAD + n)
            table[COL_OF + i * OWN + n] = at(notices, src, COL + n)
            scales[i * OWN + n] = notices[src, 0, SCALE + n]


def project_body(where, table, scales, came, mine, other, *rest):
    arrays, rows, total, slots = rest[:-3], rest[-3], rest[-2], rest[-1]
    per = STEPS * HEADS
    xl = where[0]
    for side, here, start in ((0, mine, xl * SLOTS), (1, other, (1 - xl) * SLOTS)):
        for s in range(SLOTS):
            slots[pl.ds(pl.multiple_of((start + s) * per, per), per), :] = here[s].astype(F32)
        for k in range(MOVE):
            rows_k = came[table[PEER_OF + side * SLOTS + k], side * per : (side + 1) * per, :]
            goal = start + table[SLOT_OF + side * SLOTS + k]
            slots[pl.ds(pl.multiple_of(goal * per, per), per), :] = rows_k.astype(F32)
    for h in range(HEADS):
        for side in range(XL):
            for t in range(STEPS):
                lo = side * ROWS + t * SLOTS
                rows[h, lo : lo + SLOTS, :] = slots[
                    pl.ds(side * SLOTS * per + t * HEADS + h, SLOTS, stride=per), :
                ].astype(BF16)
    total[...] = jnp.zeros_like(total)
    for i, blocks in enumerate(arrays):
        add_blocks(table, scales, rows, total, blocks, i * OWN)


def last_body(table, scales, rows, so_far, four, four_x, out, total):
    total[...] = so_far[...]
    add_blocks(table, scales, rows, total, four, (2 * Z - 2) * OWN)
    add_blocks(table, scales, rows, total, four_x, (2 * Z - 1) * OWN)
    out[:COLS] = total[:, :ROWS, :].astype(BF16)
    out[COLS:] = total[:, ROWS:, :].astype(BF16)


def sum_body(parts, out):
    for c in range(OUT_COLS):
        acc = parts[0, c].astype(F32)
        for t in range(1, XL * TP):
            acc = acc + parts[t, c].astype(F32)
        acc = acc.astype(BF16)
        for t in range(STEPS):
            out[t, :, c * HD : (c + 1) * HD] = acc[t * SLOTS : (t + 1) * SLOTS, :]


def shards(kv_cache, lengths, departing, destination, queries, new_kv, codes, scales, block_slot):
    rep_axes, tp_axes = ("xl", "z", "core"), ("y", "xh")
    base = lax.axis_index(tp_axes) * (HEADS * COLS)
    xl = lax.axis_index("xl").astype(I32)
    per = STEPS * HEADS

    def in_hbm(x):
        return pltpu.with_memory_space_constraint(x, pltpu.HBM)

    def exchange(x, axes):
        return lax.all_to_all(x, axes, split_axis=0, concat_axis=0, tiled=True)

    def swap(x, axis):
        return lax.ppermute(x, axis, [(0, 1), (1, 0)])

    def around(x, cross=0):
        pairs = []
        for i in range(Z):
            for c in range(CORE):
                line = (c + cross) % CORE
                pairs.append((i * CORE + c, ((i + 1 - 2 * line) % Z) * CORE + line))
        return lax.ppermute(x, ("z", "core"), pairs)

    sib = swap(codes, "core")
    given = [departing, destination, lengths, block_slot, scales]
    notice = call(
        notice_body,
        jax.ShapeDtypeStruct((REP, 1, HD), F32),
        [smem()] + [hbm()] * len(given),
        [pltpu.SMEM(a.shape, a.dtype) for a in given] + [pltpu.SemaphoreType.DMA((len(given),))],
    )(base.astype(I32)[None], *(in_hbm(a) for a in given))
    cache = in_hbm(kv_cache)
    sib, notice = lax.optimization_barrier((sib, notice))
    near, near_x = around(codes), around(sib)
    notices = exchange(notice, rep_axes)
    fresh = new_kv.reshape(STEPS, SLOTS, 2 * HD)
    stays, packs = call(
        stay_body,
        [
            jax.ShapeDtypeStruct((SLOTS, per, HD), BF16),
            jax.ShapeDtypeStruct((MOVE, PACK, HD), BF16),
        ],
        [hbm()] * 5,
        [
            pltpu.SMEM(departing.shape, I32),
            pltpu.SMEM(lengths.shape, I32),
            pltpu.VMEM(queries.shape, BF16),
            pltpu.VMEM(fresh.shape, BF16),
            pltpu.VMEM(kv_cache.shape, BF16),
            pltpu.SMEM((SLOTS,), I32),
            pltpu.VMEM((SLOTS, PACK, HD), BF16),
            pltpu.SemaphoreType.DMA((SLOTS + 4,)),
        ],
    )(*(in_hbm(a) for a in (departing, lengths, queries, fresh)), cache)
    near, stays = lax.optimization_barrier((near, stays))
    near_x, notices = lax.optimization_barrier((near_x, notices))
    two, two_x = around(near), around(near_x)
    other = swap(stays, "xl")
    table, factors = call(
        table_body,
        [jax.ShapeDtypeStruct((TABLE,), I32), jax.ShapeDtypeStruct((2 * Z * OWN,), F32)],
        [smem()],
        out_specs=[smem(), smem()],
    )(notices)
    to_pull = call(
        pull_body, jax.ShapeDtypeStruct((REP, PACK, HD), BF16), [smem(), vmem()]
    )(notices, packs)
    pulled = exchange(to_pull, rep_axes)
    three, three_x = around(two), around(two_x)
    send = call(
        attend_body,
        jax.ShapeDtypeStruct((REP, 2 * per, HD), BF16),
        [smem()] + [vmem()] * 2,
        [pltpu.VMEM((MOVE, per, CTX), F32)],
    )(notices, pulled, kv_cache)
    came = exchange(send, rep_axes)
    four, four_x = around(three), around(three_x)
    rows, total = call(
        project_body,
        [
            jax.ShapeDtypeStruct((HEADS, XL * ROWS, HD), BF16),
            jax.ShapeDtypeStruct((COLS, XL * ROWS, HD), F32),
        ],
        [smem()] * 3 + [vmem()] * 17,
        [pltpu.VMEM((XL * SLOTS * per, HD), F32)],
    )(
        *(xl[None], table, factors, came, stays, other),
        *(codes, sib, near, two, three, near_x, two_x, three_x),
        *(swap(x, "core") for x in (near, two, three, near_x, two_x, three_x)),
    )
    parts = call(
        last_body,
        jax.ShapeDtypeStruct((XL * COLS, ROWS, HD), BF16),
        [smem()] * 2 + [vmem()] * 4,
        [pltpu.VMEM((COLS, XL * ROWS, HD), F32)],
    )(table, factors, rows, total, four, four_x)
    parts = exchange(parts, ("xl",) + tp_axes).reshape(XL * TP, OUT_COLS, ROWS, HD)
    return call(
        sum_body, jax.ShapeDtypeStruct((STEPS, SLOTS, OUT_COLS * HD), BF16), [vmem()]
    )(parts)


def solution(mesh):
    rep, tp = ("xl", "z", "core"), ("y", "xh")
    parts = Mesh(mesh.devices.reshape(XL, Z, CORE, 4, 2), rep + tp)
    placed = (
        P(rep, tp, None, None),
        P(rep),
        P(rep, None),
        P(rep, None),
        P(None, rep, tp, None),
        P(None, rep, tp, None),
        P(tp + rep, None, None),
        P(tp + rep),
        P(tp + rep),
    )
    return jax.shard_map(
        shards, mesh=parts, in_specs=placed, out_specs=P(None, rep, tp), check_vma=False
    )
```

```python
import math

import jax
import jax.numpy as jnp
from jax import lax
from jax.experimental import pallas as pl
from jax.experimental.pallas import tpu as pltpu
from jax.sharding import Mesh, PartitionSpec as P

BF16, F32, I32 = jnp.bfloat16, jnp.float32, jnp.int32

XL, Z, CORE, TP = 2, 8, 2, 8
REP = XL * Z * CORE

HD = 128
SLOTS = 16
STEPS = 2
HEADS = 8
CTX = 256
MOVE = 13
STAY = SLOTS - MOVE
COLS = 40
OUT_COLS = COLS // TP
OWN = 10
ROWS = SLOTS * STEPS
PACK = STEPS * HEADS + 2 * STEPS

ROUND, PAIR_ROUND, ME, HEAD, COL, SCALE, DEP, DEST, LEN = 0, 1, 2, 3, 13, 23, 33, 46, 59

SLOT_OF, PEER_OF, HEAD_OF = 0, 2 * SLOTS, 4 * SLOTS
COL_OF = HEAD_OF + 2 * Z * OWN
TABLE = COL_OF + 2 * Z * OWN

VMEM_LIMIT = 16 * 1024 * 1024


def smem():
    return pl.BlockSpec(memory_space=pltpu.SMEM)


def vmem():
    return pl.BlockSpec(memory_space=pltpu.VMEM)


def hbm():
    return pl.BlockSpec(memory_space=pltpu.HBM)


def call(body, out_shape, in_specs, scratch=(), out_specs=None, **kw):
    single = not isinstance(out_shape, (list, tuple))
    return pl.pallas_call(
        body,
        out_shape=out_shape,
        in_specs=in_specs,
        out_specs=out_specs or (vmem() if single else [vmem()] * len(out_shape)),
        scratch_shapes=list(scratch),
        compiler_params=pltpu.CompilerParams(vmem_limit_bytes=VMEM_LIMIT),
        **kw,
    )


def copy_in(pairs, sems):
    copies = [pltpu.make_async_copy(a, b, sems.at[i]) for i, (a, b) in enumerate(pairs)]
    for c in copies:
        c.start()
    for c in copies:
        c.wait()


def notice_body(place, *refs):
    given, notice, held, sems = refs[:5], refs[5], refs[6:11], refs[11]
    copy_in(zip(given, held), sems)
    dep, dest, lengths, ids, scales = held
    row = lax.broadcasted_iota(I32, (REP, HD), 0)
    lane = lax.broadcasted_iota(I32, (REP, HD), 1)
    base = place[0]
    pair_row = lax.rem(row + REP // XL, REP)
    out = jnp.where(lane == ME, row, -1).astype(F32)
    for k in range(MOVE):
        out = jnp.where((lane == ROUND) & (row == dest[0, k]), float(k), out)
        out = jnp.where((lane == PAIR_ROUND) & (pair_row == dest[0, k]), float(k), out)
        out = jnp.where(lane == DEP + k, dep[0, k].astype(F32), out)
        out = jnp.where(lane == DEST + k, dest[0, k].astype(F32), out)
    for n in range(OWN):
        place_n = ids[n] - base
        head = lax.div(place_n, COLS)
        out = jnp.where(lane == HEAD + n, head.astype(F32), out)
        out = jnp.where(lane == COL + n, (place_n - head * COLS).astype(F32), out)
        out = jnp.where(lane == SCALE + n, scales[n], out)
    for s in range(SLOTS):
        out = jnp.where(lane == LEN + s, lengths[s].astype(F32), out)
    notice[:, 0, :] = out


def at(notices, rep, lane):
    return notices[rep, 0, lane].astype(I32)


def pull_body(notices, packs, out):
    for peer in range(REP):
        out[peer] = packs[jnp.maximum(at(notices, peer, ROUND), 0)]


def score(pack, keys, length):
    per = STEPS * HEADS
    sc = lax.dot_general(
        pack[:per], keys, (((1,), (1,)), ((), ())), preferred_element_type=F32
    )
    pos = lax.broadcasted_iota(I32, (per, CTX), 1)
    return jnp.where(pos < length, sc * (1.0 / math.sqrt(HD)), -jnp.inf)


def blend(pack, sc, values):
    per = STEPS * HEADS
    step = lax.broadcasted_iota(I32, (per, 1), 0) // HEADS
    top = jnp.max(sc, axis=1, keepdims=True)
    expo = jnp.exp(sc - top)
    total = jnp.sum(expo, axis=1, keepdims=True)
    carried = jnp.dot(expo.astype(BF16), values, preferred_element_type=F32)
    pack = pack.astype(F32)
    q = pack[:per]
    peak = top
    extra = []
    for u in range(STEPS):
        f = jnp.sum(q * pack[per + 2 * u : per + 2 * u + 1], axis=1, keepdims=True)
        f = jnp.where(step >= u, f * (1.0 / math.sqrt(HD)), -jnp.inf)
        extra.append(f)
        peak = jnp.maximum(peak, f)
    factor = jnp.exp(top - peak)
    denom = total * factor
    numer = carried * factor
    for u in range(STEPS):
        w = jnp.exp(extra[u] - peak)
        denom = denom + w
        numer = numer + w * pack[per + 2 * u + 1 : per + 2 * u + 2]
    return (numer / denom).astype(BF16)


def stay_body(dep_in, lengths_in, q_in, fresh_in, cache, out, packs, *scratch):
    dep, lengths, queries, fresh, held, leaves, mine, sems = scratch
    copy_in(
        [(dep_in, dep), (lengths_in, lengths), (q_in, queries), (fresh_in, fresh)],
        sems.at[SLOTS:],
    )
    for s in range(SLOTS):
        leaves[s] = 0
    for k in range(MOVE):
        leaves[dep[0, k]] = 1

    def copy(s):
        return pltpu.make_async_copy(cache.at[s], held.at[s], sems.at[s])

    def start(s, carry):
        @pl.when(leaves[s] == 0)
        def _():
            copy(s).start()

        return carry

    def one(s, carry):
        @pl.when(leaves[s] == 0)
        def _():
            copy(s).wait()
            pack = mine[s]
            sc = score(pack, held[s, 0, :, :HD], lengths[s])
            out[s] = blend(pack, sc, held[s, 0, :, HD:])

        return carry

    lax.fori_loop(0, SLOTS, start, 0)
    for s in range(SLOTS):
        mine[s] = jnp.concatenate(
            [queries[t, s] for t in range(STEPS)]
            + [fresh[t, s : s + 1, j * HD : (j + 1) * HD] for t in range(STEPS) for j in range(2)],
            axis=0,
        )
    for k in range(MOVE):
        packs[k] = mine[dep[0, k]]
    lax.fori_loop(0, SLOTS, one, 0)


def attend_body(notices, pulled, cache, send, scores):
    per = STEPS * HEADS
    me = at(notices, 0, ME)
    slots = [at(notices, me, DEP + k) for k in range(MOVE)]
    goals = [at(notices, me, DEST + k) for k in range(MOVE)]
    for k in range(MOVE):
        length = at(notices, me, LEN + slots[k])
        scores[k] = score(pulled[goals[k]], cache[slots[k], 0, :, :HD], length)
    for k in range(MOVE):
        rows = blend(pulled[goals[k]], scores[k], cache[slots[k], 0, :, HD:])
        send[goals[k], :per, :] = rows
        send[lax.rem(goals[k] + REP // XL, REP), per:, :] = rows


def add_blocks(table, scales, rows, total, blocks, first):
    for lo in range(first, first + OWN, 5):
        products = [
            jnp.dot(rows[table[HEAD_OF + n]], blocks[n - first], preferred_element_type=F32)
            * scales[n]
            for n in range(lo, lo + 5)
        ]
        for n in range(lo, lo + 5):
            total[table[COL_OF + n]] += products[n - lo]


def table_body(notices, table, scales):
    me = at(notices, 0, ME)
    pair = lax.rem(me + REP // XL, REP)
    for side, owner, lane in ((0, me, ROUND), (1, pair, PAIR_ROUND)):
        for k in range(MOVE):
            table[SLOT_OF + side * SLOTS + k] = at(notices, owner, DEP + k)
        for peer in range(REP):
            turn = at(notices, peer, lane)
            table[PEER_OF + side * SLOTS + jnp.where(turn >= 0, turn, SLOTS - 1)] = peer
    xl, z, core = lax.div(me, Z * CORE), lax.rem(lax.div(me, CORE), Z), lax.rem(me, CORE)
    half = Z // 2
    for i, (step, line, cross) in enumerate(
        [(0, 0, 0), (0, 0, 1)]
        + [(j, 0, cross) for cross in (0, 1) for j in range(1, half)]
        + [(j, 1, cross) for cross in (0, 1) for j in range(1, half)]
        + [(half, 0, 0), (half, 0, 1)]
    ):
        on = core if line == 0 else 1 - core
        origin = on if cross == 0 else 1 - on
        far = lax.rem(z - (1 - 2 * on) * step + Z, Z)
        src = (xl * Z + far) * CORE + origin
        for n in range(OWN):
            table[HEAD_OF + i * OWN + n] = at(notices, src, HEAD + n)
            table[COL_OF + i * OWN + n] = at(notices, src, COL + n)
            scales[i * OWN + n] = notices[src, 0, SCALE + n]


def project_body(where, table, scales, came, mine, other, *rest):
    arrays, rows, total, slots = rest[:-3], rest[-3], rest[-2], rest[-1]
    per = STEPS * HEADS
    xl = where[0]
    for side, here, start in ((0, mine, xl * SLOTS), (1, other, (1 - xl) * SLOTS)):
        for s in range(SLOTS):
            slots[pl.ds(pl.multiple_of((start + s) * per, per), per), :] = here[s].astype(F32)
        for k in range(MOVE):
            rows_k = came[table[PEER_OF + side * SLOTS + k], side * per : (side + 1) * per, :]
            goal = start + table[SLOT_OF + side * SLOTS + k]
            slots[pl.ds(pl.multiple_of(goal * per, per), per), :] = rows_k.astype(F32)
    for h in range(HEADS):
        for side in range(XL):
            for t in range(STEPS):
                lo = side * ROWS + t * SLOTS
                rows[h, lo : lo + SLOTS, :] = slots[
                    pl.ds(side * SLOTS * per + t * HEADS + h, SLOTS, stride=per), :
                ].astype(BF16)
    total[...] = jnp.zeros_like(total)
    for i, blocks in enumerate(arrays):
        add_blocks(table, scales, rows, total, blocks, i * OWN)


def last_body(table, scales, rows, so_far, four, four_x, out, total):
    total[...] = so_far[...]
    add_blocks(table, scales, rows, total, four, (2 * Z - 2) * OWN)
    add_blocks(table, scales, rows, total, four_x, (2 * Z - 1) * OWN)
    out[:COLS] = total[:, :ROWS, :].astype(BF16)
    out[COLS:] = total[:, ROWS:, :].astype(BF16)


def sum_body(parts, out):
    for c in range(OUT_COLS):
        acc = parts[0, c].astype(F32)
        for t in range(1, XL * TP):
            acc = acc + parts[t, c].astype(F32)
        acc = acc.astype(BF16)
        for t in range(STEPS):
            out[t, :, c * HD : (c + 1) * HD] = acc[t * SLOTS : (t + 1) * SLOTS, :]


def shards(kv_cache, lengths, departing, destination, queries, new_kv, codes, scales, block_slot):
    rep_axes, tp_axes = ("xl", "z", "core"), ("y", "xh")
    base = lax.axis_index(tp_axes) * (HEADS * COLS)
    xl = lax.axis_index("xl").astype(I32)
    per = STEPS * HEADS

    def in_hbm(x):
        return pltpu.with_memory_space_constraint(x, pltpu.HBM)

    def exchange(x, axes):
        return lax.all_to_all(x, axes, split_axis=0, concat_axis=0, tiled=True)

    def swap(x, axis):
        return lax.ppermute(x, axis, [(0, 1), (1, 0)])

    def around(x, cross=0):
        pairs = []
        for i in range(Z):
            for c in range(CORE):
                line = (c + cross) % CORE
                pairs.append((i * CORE + c, ((i + 1 - 2 * line) % Z) * CORE + line))
        return lax.ppermute(x, ("z", "core"), pairs)

    sib = swap(codes, "core")
    given = [departing, destination, lengths, block_slot, scales]
    notice = call(
        notice_body,
        jax.ShapeDtypeStruct((REP, 1, HD), F32),
        [smem()] + [hbm()] * len(given),
        [pltpu.SMEM(a.shape, a.dtype) for a in given] + [pltpu.SemaphoreType.DMA((len(given),))],
    )(base.astype(I32)[None], *(in_hbm(a) for a in given))
    cache = in_hbm(kv_cache)
    near, near_x = around(codes), around(codes, 1)
    notices = exchange(notice, rep_axes)
    fresh = new_kv.reshape(STEPS, SLOTS, 2 * HD)
    stays, packs = call(
        stay_body,
        [
            jax.ShapeDtypeStruct((SLOTS, per, HD), BF16),
            jax.ShapeDtypeStruct((MOVE, PACK, HD), BF16),
        ],
        [hbm()] * 5,
        [
            pltpu.SMEM(departing.shape, I32),
            pltpu.SMEM(lengths.shape, I32),
            pltpu.VMEM(queries.shape, BF16),
            pltpu.VMEM(fresh.shape, BF16),
            pltpu.VMEM(kv_cache.shape, BF16),
            pltpu.SMEM((SLOTS,), I32),
            pltpu.VMEM((SLOTS, PACK, HD), BF16),
            pltpu.SemaphoreType.DMA((SLOTS + 4,)),
        ],
    )(*(in_hbm(a) for a in (departing, lengths, queries, fresh)), cache)
    near, stays = lax.optimization_barrier((near, stays))
    near_x, notices, stays = lax.optimization_barrier((near_x, notices, stays))
    two, two_x = around(near), around(near_x)
    other = swap(stays, "xl")
    table, factors = call(
        table_body,
        [jax.ShapeDtypeStruct((TABLE,), I32), jax.ShapeDtypeStruct((2 * Z * OWN,), F32)],
        [smem()],
        out_specs=[smem(), smem()],
    )(notices)
    to_pull = call(
        pull_body, jax.ShapeDtypeStruct((REP, PACK, HD), BF16), [smem(), vmem()]
    )(notices, packs)
    pulled = exchange(to_pull, rep_axes)
    three, three_x = around(two), around(two_x)
    send = call(
        attend_body,
        jax.ShapeDtypeStruct((REP, 2 * per, HD), BF16),
        [smem()] + [vmem()] * 2,
        [pltpu.VMEM((MOVE, per, CTX), F32)],
    )(notices, pulled, kv_cache)
    came = exchange(send, rep_axes)
    four, four_x = around(three), around(three_x)
    rows, total = call(
        project_body,
        [
            jax.ShapeDtypeStruct((HEADS, XL * ROWS, HD), BF16),
            jax.ShapeDtypeStruct((COLS, XL * ROWS, HD), F32),
        ],
        [smem()] * 3 + [vmem()] * 17,
        [pltpu.VMEM((XL * SLOTS * per, HD), F32)],
    )(
        *(xl[None], table, factors, came, stays, other),
        *(codes, sib, near, two, three, near_x, two_x, three_x),
        *(swap(x, "core") for x in (near, two, three, near_x, two_x, three_x)),
    )
    parts = call(
        last_body,
        jax.ShapeDtypeStruct((XL * COLS, ROWS, HD), BF16),
        [smem()] * 2 + [vmem()] * 4,
        [pltpu.VMEM((COLS, XL * ROWS, HD), F32)],
    )(table, factors, rows, total, four, four_x)
    parts = exchange(parts, ("xl",) + tp_axes).reshape(XL * TP, OUT_COLS, ROWS, HD)
    return call(
        sum_body, jax.ShapeDtypeStruct((STEPS, SLOTS, OUT_COLS * HD), BF16), [vmem()]
    )(parts)


def solution(mesh):
    rep, tp = ("xl", "z", "core"), ("y", "xh")
    parts = Mesh(mesh.devices.reshape(XL, Z, CORE, 4, 2), rep + tp)
    placed = (
        P(rep, tp, None, None),
        P(rep),
        P(rep, None),
        P(rep, None),
        P(None, rep, tp, None),
        P(None, rep, tp, None),
        P(tp + rep, None, None),
        P(tp + rep),
        P(tp + rep),
    )
    return jax.shard_map(
        shards, mesh=parts, in_specs=placed, out_specs=P(None, rep, tp), check_vma=False
    )
```

```python
import math

import jax
import jax.numpy as jnp
from jax import lax
from jax.experimental import pallas as pl
from jax.experimental.pallas import tpu as pltpu
from jax.sharding import Mesh, PartitionSpec as P

BF16, F32, I32 = jnp.bfloat16, jnp.float32, jnp.int32

XL, Z, CORE, TP = 2, 8, 2, 8
REP = XL * Z * CORE

HD = 128
SLOTS = 16
STEPS = 2
HEADS = 8
CTX = 256
MOVE = 13
STAY = SLOTS - MOVE
COLS = 40
OUT_COLS = COLS // TP
OWN = 10
ROWS = SLOTS * STEPS
PACK = STEPS * HEADS + 2 * STEPS

ROUND, PAIR_ROUND, ME, HEAD, COL, SCALE, DEP, DEST, LEN = 0, 1, 2, 3, 13, 23, 33, 46, 59

SLOT_OF, PEER_OF, HEAD_OF = 0, 2 * SLOTS, 4 * SLOTS
COL_OF = HEAD_OF + 2 * Z * OWN
TABLE = COL_OF + 2 * Z * OWN

VMEM_LIMIT = 16 * 1024 * 1024


def smem():
    return pl.BlockSpec(memory_space=pltpu.SMEM)


def vmem():
    return pl.BlockSpec(memory_space=pltpu.VMEM)


def hbm():
    return pl.BlockSpec(memory_space=pltpu.HBM)


def call(body, out_shape, in_specs, scratch=(), out_specs=None, **kw):
    single = not isinstance(out_shape, (list, tuple))
    return pl.pallas_call(
        body,
        out_shape=out_shape,
        in_specs=in_specs,
        out_specs=out_specs or (vmem() if single else [vmem()] * len(out_shape)),
        scratch_shapes=list(scratch),
        compiler_params=pltpu.CompilerParams(vmem_limit_bytes=VMEM_LIMIT),
        **kw,
    )


def copy_in(pairs, sems):
    copies = [pltpu.make_async_copy(a, b, sems.at[i]) for i, (a, b) in enumerate(pairs)]
    for c in copies:
        c.start()
    for c in copies:
        c.wait()


def notice_body(place, *refs):
    given, notice, held, sems = refs[:5], refs[5], refs[6:11], refs[11]
    copy_in(zip(given, held), sems)
    dep, dest, lengths, ids, scales = held
    row = lax.broadcasted_iota(I32, (REP, HD), 0)
    lane = lax.broadcasted_iota(I32, (REP, HD), 1)
    base = place[0]
    pair_row = lax.rem(row + REP // XL, REP)
    out = jnp.where(lane == ME, row, -1).astype(F32)
    for k in range(MOVE):
        out = jnp.where((lane == ROUND) & (row == dest[0, k]), float(k), out)
        out = jnp.where((lane == PAIR_ROUND) & (pair_row == dest[0, k]), float(k), out)
        out = jnp.where(lane == DEP + k, dep[0, k].astype(F32), out)
        out = jnp.where(lane == DEST + k, dest[0, k].astype(F32), out)
    for n in range(OWN):
        place_n = ids[n] - base
        head = lax.div(place_n, COLS)
        out = jnp.where(lane == HEAD + n, head.astype(F32), out)
        out = jnp.where(lane == COL + n, (place_n - head * COLS).astype(F32), out)
        out = jnp.where(lane == SCALE + n, scales[n], out)
    for s in range(SLOTS):
        out = jnp.where(lane == LEN + s, lengths[s].astype(F32), out)
    notice[:, 0, :] = out


def at(notices, rep, lane):
    return notices[rep, 0, lane].astype(I32)


def pull_body(notices, packs, out):
    for peer in range(REP):
        out[peer] = packs[jnp.maximum(at(notices, peer, ROUND), 0)]


def score(pack, keys, length):
    per = STEPS * HEADS
    sc = lax.dot_general(
        pack[:per], keys, (((1,), (1,)), ((), ())), preferred_element_type=F32
    )
    pos = lax.broadcasted_iota(I32, (per, CTX), 1)
    return jnp.where(pos < length, sc * (1.0 / math.sqrt(HD)), -jnp.inf)


def blend(pack, sc, values):
    per = STEPS * HEADS
    step = lax.broadcasted_iota(I32, (per, 1), 0) // HEADS
    top = jnp.max(sc, axis=1, keepdims=True)
    expo = jnp.exp(sc - top)
    total = jnp.sum(expo, axis=1, keepdims=True)
    carried = jnp.dot(expo.astype(BF16), values, preferred_element_type=F32)
    pack = pack.astype(F32)
    q = pack[:per]
    peak = top
    extra = []
    for u in range(STEPS):
        f = jnp.sum(q * pack[per + 2 * u : per + 2 * u + 1], axis=1, keepdims=True)
        f = jnp.where(step >= u, f * (1.0 / math.sqrt(HD)), -jnp.inf)
        extra.append(f)
        peak = jnp.maximum(peak, f)
    factor = jnp.exp(top - peak)
    denom = total * factor
    numer = carried * factor
    for u in range(STEPS):
        w = jnp.exp(extra[u] - peak)
        denom = denom + w
        numer = numer + w * pack[per + 2 * u + 1 : per + 2 * u + 2]
    return (numer / denom).astype(BF16)


def stay_body(dep_in, lengths_in, q_in, fresh_in, cache, out, packs, *scratch):
    dep, lengths, queries, fresh, held, leaves, mine, sems = scratch
    copy_in(
        [(dep_in, dep), (lengths_in, lengths), (q_in, queries), (fresh_in, fresh)],
        sems.at[SLOTS:],
    )
    for s in range(SLOTS):
        leaves[s] = 0
    for k in range(MOVE):
        leaves[dep[0, k]] = 1

    def copy(s):
        return pltpu.make_async_copy(cache.at[s], held.at[s], sems.at[s])

    def start(s, carry):
        @pl.when(leaves[s] == 0)
        def _():
            copy(s).start()

        return carry

    def one(s, carry):
        @pl.when(leaves[s] == 0)
        def _():
            copy(s).wait()
            pack = mine[s]
            sc = score(pack, held[s, 0, :, :HD], lengths[s])
            out[s] = blend(pack, sc, held[s, 0, :, HD:])

        return carry

    lax.fori_loop(0, SLOTS, start, 0)
    for s in range(SLOTS):
        mine[s] = jnp.concatenate(
            [queries[t, s] for t in range(STEPS)]
            + [fresh[t, s : s + 1, j * HD : (j + 1) * HD] for t in range(STEPS) for j in range(2)],
            axis=0,
        )
    for k in range(MOVE):
        packs[k] = mine[dep[0, k]]
    lax.fori_loop(0, SLOTS, one, 0)


def attend_body(notices, pulled, cache, send, scores):
    per = STEPS * HEADS
    me = at(notices, 0, ME)
    slots = [at(notices, me, DEP + k) for k in range(MOVE)]
    goals = [at(notices, me, DEST + k) for k in range(MOVE)]
    for k in range(MOVE):
        length = at(notices, me, LEN + slots[k])
        scores[k] = score(pulled[goals[k]], cache[slots[k], 0, :, :HD], length)
    for k in range(MOVE):
        rows = blend(pulled[goals[k]], scores[k], cache[slots[k], 0, :, HD:])
        send[goals[k], :per, :] = rows
        send[lax.rem(goals[k] + REP // XL, REP), per:, :] = rows


def add_blocks(table, scales, rows, total, blocks, first):
    for lo in range(first, first + OWN, 5):
        products = [
            jnp.dot(rows[table[HEAD_OF + n]], blocks[n - first], preferred_element_type=F32)
            * scales[n]
            for n in range(lo, lo + 5)
        ]
        for n in range(lo, lo + 5):
            total[table[COL_OF + n]] += products[n - lo]


def table_body(notices, table, scales):
    me = at(notices, 0, ME)
    pair = lax.rem(me + REP // XL, REP)
    for side, owner, lane in ((0, me, ROUND), (1, pair, PAIR_ROUND)):
        for k in range(MOVE):
            table[SLOT_OF + side * SLOTS + k] = at(notices, owner, DEP + k)
        for peer in range(REP):
            turn = at(notices, peer, lane)
            table[PEER_OF + side * SLOTS + jnp.where(turn >= 0, turn, SLOTS - 1)] = peer
    xl, z, core = lax.div(me, Z * CORE), lax.rem(lax.div(me, CORE), Z), lax.rem(me, CORE)
    half = Z // 2
    for i, (step, line, cross) in enumerate(
        [(0, 0, 0), (0, 0, 1)]
        + [(j, 0, cross) for cross in (0, 1) for j in range(1, half)]
        + [(j, 1, cross) for cross in (0, 1) for j in range(1, half)]
        + [(half, 0, 0), (half, 0, 1)]
    ):
        on = core if line == 0 else 1 - core
        origin = on if cross == 0 else 1 - on
        far = lax.rem(z - (1 - 2 * on) * step + Z, Z)
        src = (xl * Z + far) * CORE + origin
        for n in range(OWN):
            table[HEAD_OF + i * OWN + n] = at(notices, src, HEAD + n)
            table[COL_OF + i * OWN + n] = at(notices, src, COL + n)
            scales[i * OWN + n] = notices[src, 0, SCALE + n]


def project_body(where, table, scales, came, mine, other, *rest):
    arrays, rows, total, slots = rest[:-3], rest[-3], rest[-2], rest[-1]
    per = STEPS * HEADS
    xl = where[0]
    for side, here, start in ((0, mine, xl * SLOTS), (1, other, (1 - xl) * SLOTS)):
        for s in range(SLOTS):
            slots[pl.ds(pl.multiple_of((start + s) * per, per), per), :] = here[s].astype(F32)
        for k in range(MOVE):
            rows_k = came[table[PEER_OF + side * SLOTS + k], side * per : (side + 1) * per, :]
            goal = start + table[SLOT_OF + side * SLOTS + k]
            slots[pl.ds(pl.multiple_of(goal * per, per), per), :] = rows_k.astype(F32)
    for h in range(HEADS):
        for side in range(XL):
            for t in range(STEPS):
                lo = side * ROWS + t * SLOTS
                rows[h, lo : lo + SLOTS, :] = slots[
                    pl.ds(side * SLOTS * per + t * HEADS + h, SLOTS, stride=per), :
                ].astype(BF16)
    total[...] = jnp.zeros_like(total)
    for i, blocks in enumerate(arrays):
        add_blocks(table, scales, rows, total, blocks, i * OWN)


def last_body(table, scales, rows, so_far, four, four_x, out, total):
    total[...] = so_far[...]
    add_blocks(table, scales, rows, total, four, (2 * Z - 2) * OWN)
    add_blocks(table, scales, rows, total, four_x, (2 * Z - 1) * OWN)
    out[:COLS] = total[:, :ROWS, :].astype(BF16)
    out[COLS:] = total[:, ROWS:, :].astype(BF16)


def sum_body(parts, out):
    for c in range(OUT_COLS):
        acc = parts[0, c].astype(F32)
        for t in range(1, XL * TP):
            acc = acc + parts[t, c].astype(F32)
        acc = acc.astype(BF16)
        for t in range(STEPS):
            out[t, :, c * HD : (c + 1) * HD] = acc[t * SLOTS : (t + 1) * SLOTS, :]


def shards(kv_cache, lengths, departing, destination, queries, new_kv, codes, scales, block_slot):
    rep_axes, tp_axes = ("xl", "z", "core"), ("y", "xh")
    base = lax.axis_index(tp_axes) * (HEADS * COLS)
    xl = lax.axis_index("xl").astype(I32)
    per = STEPS * HEADS

    def in_hbm(x):
        return pltpu.with_memory_space_constraint(x, pltpu.HBM)

    def exchange(x, axes):
        return lax.all_to_all(x, axes, split_axis=0, concat_axis=0, tiled=True)

    def swap(x, axis):
        return lax.ppermute(x, axis, [(0, 1), (1, 0)])

    def around(x, cross=0):
        pairs = []
        for i in range(Z):
            for c in range(CORE):
                line = (c + cross) % CORE
                pairs.append((i * CORE + c, ((i + 1 - 2 * line) % Z) * CORE + line))
        return lax.ppermute(x, ("z", "core"), pairs)

    sib = swap(codes, "core")
    given = [departing, destination, lengths, block_slot, scales]
    notice = call(
        notice_body,
        jax.ShapeDtypeStruct((REP, 1, HD), F32),
        [smem()] + [hbm()] * len(given),
        [pltpu.SMEM(a.shape, a.dtype) for a in given] + [pltpu.SemaphoreType.DMA((len(given),))],
    )(base.astype(I32)[None], *(in_hbm(a) for a in given))
    cache = in_hbm(kv_cache)
    sib, notice = lax.optimization_barrier((sib, notice))
    near, near_x = around(codes), around(sib)
    notices = exchange(notice, rep_axes)
    fresh = new_kv.reshape(STEPS, SLOTS, 2 * HD)
    stays, packs = call(
        stay_body,
        [
            jax.ShapeDtypeStruct((SLOTS, per, HD), BF16),
            jax.ShapeDtypeStruct((MOVE, PACK, HD), BF16),
        ],
        [hbm()] * 5,
        [
            pltpu.SMEM(departing.shape, I32),
            pltpu.SMEM(lengths.shape, I32),
            pltpu.VMEM(queries.shape, BF16),
            pltpu.VMEM(fresh.shape, BF16),
            pltpu.VMEM(kv_cache.shape, BF16),
            pltpu.SMEM((SLOTS,), I32),
            pltpu.VMEM((SLOTS, PACK, HD), BF16),
            pltpu.SemaphoreType.DMA((SLOTS + 4,)),
        ],
    )(*(in_hbm(a) for a in (departing, lengths, queries, fresh)), cache)
    near, stays = lax.optimization_barrier((near, stays))
    near_x, notices = lax.optimization_barrier((near_x, notices))
    two, two_x = around(near), around(near_x)
    other = swap(stays, "xl")
    table, factors = call(
        table_body,
        [jax.ShapeDtypeStruct((TABLE,), I32), jax.ShapeDtypeStruct((2 * Z * OWN,), F32)],
        [smem()],
        out_specs=[smem(), smem()],
    )(notices)
    to_pull = call(
        pull_body, jax.ShapeDtypeStruct((REP, PACK, HD), BF16), [smem(), vmem()]
    )(notices, packs)
    pulled = exchange(to_pull, rep_axes)
    other, pulled = lax.optimization_barrier((other, pulled))
    three, three_x = around(two), around(two_x)
    send = call(
        attend_body,
        jax.ShapeDtypeStruct((REP, 2 * per, HD), BF16),
        [smem()] + [vmem()] * 2,
        [pltpu.VMEM((MOVE, per, CTX), F32)],
    )(notices, pulled, kv_cache)
    came = exchange(send, rep_axes)
    four = around(three)
    four_x = swap(four, "core")
    rows, total = call(
        project_body,
        [
            jax.ShapeDtypeStruct((HEADS, XL * ROWS, HD), BF16),
            jax.ShapeDtypeStruct((COLS, XL * ROWS, HD), F32),
        ],
        [smem()] * 3 + [vmem()] * 17,
        [pltpu.VMEM((XL * SLOTS * per, HD), F32)],
        cost_estimate=pl.CostEstimate(flops=5000000000, bytes_accessed=15000000, transcendentals=0),
    )(
        *(xl[None], table, factors, came, stays, other),
        *(codes, sib, near, two, three, near_x, two_x, three_x),
        *(swap(x, "core") for x in (near, two, three, near_x, two_x, three_x)),
    )
    parts = call(
        last_body,
        jax.ShapeDtypeStruct((XL * COLS, ROWS, HD), BF16),
        [smem()] * 2 + [vmem()] * 4,
        [pltpu.VMEM((COLS, XL * ROWS, HD), F32)],
    )(table, factors, rows, total, four, four_x)
    parts = exchange(parts, ("xl",) + tp_axes).reshape(XL * TP, OUT_COLS, ROWS, HD)
    return call(
        sum_body, jax.ShapeDtypeStruct((STEPS, SLOTS, OUT_COLS * HD), BF16), [vmem()]
    )(parts)


def solution(mesh):
    rep, tp = ("xl", "z", "core"), ("y", "xh")
    parts = Mesh(mesh.devices.reshape(XL, Z, CORE, 4, 2), rep + tp)
    placed = (
        P(rep, tp, None, None),
        P(rep),
        P(rep, None),
        P(rep, None),
        P(None, rep, tp, None),
        P(None, rep, tp, None),
        P(tp + rep, None, None),
        P(tp + rep),
        P(tp + rep),
    )
    return jax.shard_map(
        shards, mesh=parts, in_specs=placed, out_specs=P(None, rep, tp), check_vma=False
    )
```

```python
import math

import jax
import jax.numpy as jnp
from jax import lax
from jax.experimental import pallas as pl
from jax.experimental.pallas import tpu as pltpu
from jax.sharding import Mesh, PartitionSpec as P

BF16, F32, I32 = jnp.bfloat16, jnp.float32, jnp.int32

XL, Z, CORE, TP = 2, 8, 2, 8
REP = XL * Z * CORE

HD = 128
SLOTS = 16
STEPS = 2
HEADS = 8
CTX = 256
MOVE = 13
STAY = SLOTS - MOVE
COLS = 40
OUT_COLS = COLS // TP
OWN = 10
ROWS = SLOTS * STEPS
PACK = STEPS * HEADS + 2 * STEPS

ROUND, PAIR_ROUND, ME, HEAD, COL, SCALE, DEP = 0, 1, 2, 3, 13, 23, 33

SLOT_OF, PEER_OF, HEAD_OF = 0, 2 * SLOTS, 4 * SLOTS
COL_OF = HEAD_OF + 2 * Z * OWN
TABLE = COL_OF + 2 * Z * OWN

VMEM_LIMIT = 16 * 1024 * 1024


def smem():
    return pl.BlockSpec(memory_space=pltpu.SMEM)


def vmem():
    return pl.BlockSpec(memory_space=pltpu.VMEM)


def hbm():
    return pl.BlockSpec(memory_space=pltpu.HBM)


def call(body, out_shape, in_specs, scratch=(), out_specs=None, **kw):
    single = not isinstance(out_shape, (list, tuple))
    return pl.pallas_call(
        body,
        out_shape=out_shape,
        in_specs=in_specs,
        out_specs=out_specs or (vmem() if single else [vmem()] * len(out_shape)),
        scratch_shapes=list(scratch),
        compiler_params=pltpu.CompilerParams(vmem_limit_bytes=VMEM_LIMIT),
        **kw,
    )


def copy_in(pairs, sems):
    copies = [pltpu.make_async_copy(a, b, sems.at[i]) for i, (a, b) in enumerate(pairs)]
    for c in copies:
        c.start()
    for c in copies:
        c.wait()


def notice_body(place, *refs):
    given, notice, held, sems = refs[:4], refs[4], refs[5:9], refs[9]
    copy_in(zip(given, held), sems)
    dep, dest, ids, scales = held
    row = lax.broadcasted_iota(I32, (REP, HD), 0)
    lane = lax.broadcasted_iota(I32, (REP, HD), 1)
    base = place[0]
    pair_row = lax.rem(row + REP // XL, REP)
    out = jnp.where(lane == ME, row, -1).astype(F32)
    for k in range(MOVE):
        out = jnp.where((lane == ROUND) & (row == dest[0, k]), float(k), out)
        out = jnp.where((lane == PAIR_ROUND) & (pair_row == dest[0, k]), float(k), out)
        out = jnp.where(lane == DEP + k, dep[0, k].astype(F32), out)
    for n in range(OWN):
        place_n = ids[n] - base
        head = lax.div(place_n, COLS)
        out = jnp.where(lane == HEAD + n, head.astype(F32), out)
        out = jnp.where(lane == COL + n, (place_n - head * COLS).astype(F32), out)
        out = jnp.where(lane == SCALE + n, scales[n], out)
    notice[:, 0, :] = out


def at(notices, rep, lane):
    return notices[rep, 0, lane].astype(I32)


def pull_body(notices, packs, out):
    for peer in range(REP):
        out[peer] = packs[jnp.maximum(at(notices, peer, ROUND), 0)]


def score(pack, keys, length):
    per = STEPS * HEADS
    sc = lax.dot_general(
        pack[:per], keys, (((1,), (1,)), ((), ())), preferred_element_type=F32
    )
    pos = lax.broadcasted_iota(I32, (per, CTX), 1)
    return jnp.where(pos < length, sc * (1.0 / math.sqrt(HD)), -jnp.inf)


def blend(pack, sc, values):
    per = STEPS * HEADS
    step = lax.broadcasted_iota(I32, (per, 1), 0) // HEADS
    top = jnp.max(sc, axis=1, keepdims=True)
    expo = jnp.exp(sc - top)
    total = jnp.sum(expo, axis=1, keepdims=True)
    carried = jnp.dot(expo.astype(BF16), values, preferred_element_type=F32)
    pack = pack.astype(F32)
    q = pack[:per]
    peak = top
    extra = []
    for u in range(STEPS):
        f = jnp.sum(q * pack[per + 2 * u : per + 2 * u + 1], axis=1, keepdims=True)
        f = jnp.where(step >= u, f * (1.0 / math.sqrt(HD)), -jnp.inf)
        extra.append(f)
        peak = jnp.maximum(peak, f)
    factor = jnp.exp(top - peak)
    denom = total * factor
    numer = carried * factor
    for u in range(STEPS):
        w = jnp.exp(extra[u] - peak)
        denom = denom + w
        numer = numer + w * pack[per + 2 * u + 1 : per + 2 * u + 2]
    return (numer / denom).astype(BF16)


def stay_body(dep_in, dest_in, lengths_in, q_in, fresh_in, cache, out, packs, lists, *scratch):
    dep, dest, lengths, queries, fresh, held, leaves, mine, sems = scratch
    given = zip((dep_in, dest_in, lengths_in, q_in, fresh_in), (dep, dest, lengths, queries, fresh))
    copy_in(given, sems.at[SLOTS:])
    for k in range(MOVE):
        lists[k] = dep[0, k]
        lists[SLOTS + k] = dest[0, k]
        lists[2 * SLOTS + k] = lengths[dep[0, k]]
    for s in range(SLOTS):
        leaves[s] = 0
    for k in range(MOVE):
        leaves[dep[0, k]] = 1

    def copy(s):
        return pltpu.make_async_copy(cache.at[s], held.at[s], sems.at[s])

    def start(s, carry):
        @pl.when(leaves[s] == 0)
        def _():
            copy(s).start()

        return carry

    def one(s, carry):
        @pl.when(leaves[s] == 0)
        def _():
            copy(s).wait()
            pack = mine[s]
            sc = score(pack, held[s, 0, :, :HD], lengths[s])
            out[s] = blend(pack, sc, held[s, 0, :, HD:])

        return carry

    lax.fori_loop(0, SLOTS, start, 0)
    for s in range(SLOTS):
        mine[s] = jnp.concatenate(
            [queries[t, s] for t in range(STEPS)]
            + [fresh[t, s : s + 1, j * HD : (j + 1) * HD] for t in range(STEPS) for j in range(2)],
            axis=0,
        )
    for k in range(MOVE):
        packs[k] = mine[dep[0, k]]
    lax.fori_loop(0, SLOTS, one, 0)


def attend_body(lists, pulled, cache, send, scores):
    per = STEPS * HEADS
    slots = [lists[k] for k in range(MOVE)]
    goals = [lists[SLOTS + k] for k in range(MOVE)]
    for k in range(MOVE):
        length = lists[2 * SLOTS + k]
        scores[k] = score(pulled[goals[k]], cache[slots[k], 0, :, :HD], length)
    for k in range(MOVE):
        rows = blend(pulled[goals[k]], scores[k], cache[slots[k], 0, :, HD:])
        send[goals[k], :per, :] = rows
        send[lax.rem(goals[k] + REP // XL, REP), per:, :] = rows


def add_blocks(table, scales, rows, total, blocks, first):
    for lo in range(first, first + OWN, 5):
        products = [
            jnp.dot(rows[table[HEAD_OF + n]], blocks[n - first], preferred_element_type=F32)
            * scales[n]
            for n in range(lo, lo + 5)
        ]
        for n in range(lo, lo + 5):
            total[table[COL_OF + n]] += products[n - lo]


def table_body(notices, table, scales):
    me = at(notices, 0, ME)
    pair = lax.rem(me + REP // XL, REP)
    for side, owner, lane in ((0, me, ROUND), (1, pair, PAIR_ROUND)):
        for k in range(MOVE):
            table[SLOT_OF + side * SLOTS + k] = at(notices, owner, DEP + k)
        for peer in range(REP):
            turn = at(notices, peer, lane)
            table[PEER_OF + side * SLOTS + jnp.where(turn >= 0, turn, SLOTS - 1)] = peer
    xl, z, core = lax.div(me, Z * CORE), lax.rem(lax.div(me, CORE), Z), lax.rem(me, CORE)
    half = Z // 2
    for i, (step, line, cross) in enumerate(
        [(0, 0, 0), (0, 0, 1)]
        + [(j, 0, cross) for cross in (0, 1) for j in range(1, half)]
        + [(j, 1, cross) for cross in (0, 1) for j in range(1, half)]
        + [(half, 0, 0), (half, 0, 1)]
    ):
        on = core if line == 0 else 1 - core
        origin = on if cross == 0 else 1 - on
        far = lax.rem(z - (1 - 2 * on) * step + Z, Z)
        src = (xl * Z + far) * CORE + origin
        for n in range(OWN):
            table[HEAD_OF + i * OWN + n] = at(notices, src, HEAD + n)
            table[COL_OF + i * OWN + n] = at(notices, src, COL + n)
            scales[i * OWN + n] = notices[src, 0, SCALE + n]


def project_body(where, table, scales, came, mine, other, *rest):
    arrays, rows, total, slots = rest[:-3], rest[-3], rest[-2], rest[-1]
    per = STEPS * HEADS
    xl = where[0]
    for side, here, start in ((0, mine, xl * SLOTS), (1, other, (1 - xl) * SLOTS)):
        for s in range(SLOTS):
            slots[pl.ds(pl.multiple_of((start + s) * per, per), per), :] = here[s].astype(F32)
        for k in range(MOVE):
            rows_k = came[table[PEER_OF + side * SLOTS + k], side * per : (side + 1) * per, :]
            goal = start + table[SLOT_OF + side * SLOTS + k]
            slots[pl.ds(pl.multiple_of(goal * per, per), per), :] = rows_k.astype(F32)
    for h in range(HEADS):
        for side in range(XL):
            for t in range(STEPS):
                lo = side * ROWS + t * SLOTS
                rows[h, lo : lo + SLOTS, :] = slots[
                    pl.ds(side * SLOTS * per + t * HEADS + h, SLOTS, stride=per), :
                ].astype(BF16)
    total[...] = jnp.zeros_like(total)
    for i, blocks in enumerate(arrays):
        add_blocks(table, scales, rows, total, blocks, i * OWN)


def last_body(table, scales, rows, so_far, four, four_x, out, total):
    total[...] = so_far[...]
    add_blocks(table, scales, rows, total, four, (2 * Z - 2) * OWN)
    add_blocks(table, scales, rows, total, four_x, (2 * Z - 1) * OWN)
    out[:COLS] = total[:, :ROWS, :].astype(BF16)
    out[COLS:] = total[:, ROWS:, :].astype(BF16)


def sum_body(parts, out):
    for c in range(OUT_COLS):
        acc = parts[0, c].astype(F32)
        for t in range(1, XL * TP):
            acc = acc + parts[t, c].astype(F32)
        acc = acc.astype(BF16)
        for t in range(STEPS):
            out[t, :, c * HD : (c + 1) * HD] = acc[t * SLOTS : (t + 1) * SLOTS, :]


def shards(kv_cache, lengths, departing, destination, queries, new_kv, codes, scales, block_slot):
    rep_axes, tp_axes = ("xl", "z", "core"), ("y", "xh")
    base = lax.axis_index(tp_axes) * (HEADS * COLS)
    xl = lax.axis_index("xl").astype(I32)
    per = STEPS * HEADS

    def in_hbm(x):
        return pltpu.with_memory_space_constraint(x, pltpu.HBM)

    def exchange(x, axes):
        return lax.all_to_all(x, axes, split_axis=0, concat_axis=0, tiled=True)

    def swap(x, axis):
        return lax.ppermute(x, axis, [(0, 1), (1, 0)])

    def around(x, cross=0):
        pairs = []
        for i in range(Z):
            for c in range(CORE):
                line = (c + cross) % CORE
                pairs.append((i * CORE + c, ((i + 1 - 2 * line) % Z) * CORE + line))
        return lax.ppermute(x, ("z", "core"), pairs)

    sib = swap(codes, "core")
    given = [departing, destination, block_slot, scales]
    notice = call(
        notice_body,
        jax.ShapeDtypeStruct((REP, 1, HD), F32),
        [smem()] + [hbm()] * len(given),
        [pltpu.SMEM(a.shape, a.dtype) for a in given] + [pltpu.SemaphoreType.DMA((len(given),))],
    )(base.astype(I32)[None], *(in_hbm(a) for a in given))
    cache = in_hbm(kv_cache)
    sib, notice = lax.optimization_barrier((sib, notice))
    near, near_x = around(codes), around(sib)
    notices = exchange(notice, rep_axes)
    fresh = new_kv.reshape(STEPS, SLOTS, 2 * HD)
    stays, packs, lists = call(
        stay_body,
        [
            jax.ShapeDtypeStruct((SLOTS, per, HD), BF16),
            jax.ShapeDtypeStruct((MOVE, PACK, HD), BF16),
            jax.ShapeDtypeStruct((3 * SLOTS,), I32),
        ],
        [hbm()] * 6,
        [
            pltpu.SMEM(departing.shape, I32),
            pltpu.SMEM(destination.shape, I32),
            pltpu.SMEM(lengths.shape, I32),
            pltpu.VMEM(queries.shape, BF16),
            pltpu.VMEM(fresh.shape, BF16),
            pltpu.VMEM(kv_cache.shape, BF16),
            pltpu.SMEM((SLOTS,), I32),
            pltpu.VMEM((SLOTS, PACK, HD), BF16),
            pltpu.SemaphoreType.DMA((SLOTS + 5,)),
        ],
        out_specs=[vmem(), vmem(), smem()],
    )(*(in_hbm(a) for a in (departing, destination, lengths, queries, fresh)), cache)
    near, stays = lax.optimization_barrier((near, stays))
    near_x, notices = lax.optimization_barrier((near_x, notices))
    two, two_x = around(near), around(near_x)
    other = swap(stays, "xl")
    table, factors = call(
        table_body,
        [jax.ShapeDtypeStruct((TABLE,), I32), jax.ShapeDtypeStruct((2 * Z * OWN,), F32)],
        [smem()],
        out_specs=[smem(), smem()],
    )(notices)
    to_pull = call(
        pull_body, jax.ShapeDtypeStruct((REP, PACK, HD), BF16), [smem(), vmem()]
    )(notices, packs)
    pulled = exchange(to_pull, rep_axes)
    three, three_x = around(two), around(two_x)
    send = call(
        attend_body,
        jax.ShapeDtypeStruct((REP, 2 * per, HD), BF16),
        [smem()] + [vmem()] * 2,
        [pltpu.VMEM((MOVE, per, CTX), F32)],
    )(lists, pulled, kv_cache)
    came = exchange(send, rep_axes)
    four, four_x = around(three), around(three_x)
    rows, total = call(
        project_body,
        [
            jax.ShapeDtypeStruct((HEADS, XL * ROWS, HD), BF16),
            jax.ShapeDtypeStruct((COLS, XL * ROWS, HD), F32),
        ],
        [smem()] * 3 + [vmem()] * 17,
        [pltpu.VMEM((XL * SLOTS * per, HD), F32)],
    )(
        *(xl[None], table, factors, came, stays, other),
        *(codes, sib, near, two, three, near_x, two_x, three_x),
        *(swap(x, "core") for x in (near, two, three, near_x, two_x, three_x)),
    )
    parts = call(
        last_body,
        jax.ShapeDtypeStruct((XL * COLS, ROWS, HD), BF16),
        [smem()] * 2 + [vmem()] * 4,
        [pltpu.VMEM((COLS, XL * ROWS, HD), F32)],
    )(table, factors, rows, total, four, four_x)
    parts = exchange(parts, ("xl",) + tp_axes).reshape(XL * TP, OUT_COLS, ROWS, HD)
    return call(
        sum_body, jax.ShapeDtypeStruct((STEPS, SLOTS, OUT_COLS * HD), BF16), [vmem()]
    )(parts)


def solution(mesh):
    rep, tp = ("xl", "z", "core"), ("y", "xh")
    parts = Mesh(mesh.devices.reshape(XL, Z, CORE, 4, 2), rep + tp)
    placed = (
        P(rep, tp, None, None),
        P(rep),
        P(rep, None),
        P(rep, None),
        P(None, rep, tp, None),
        P(None, rep, tp, None),
        P(tp + rep, None, None),
        P(tp + rep),
        P(tp + rep),
    )
    return jax.shard_map(
        shards, mesh=parts, in_specs=placed, out_specs=P(None, rep, tp), check_vma=False
    )
```

```python
import math

import jax
import jax.numpy as jnp
from jax import lax
from jax.experimental import pallas as pl
from jax.experimental.pallas import tpu as pltpu
from jax.sharding import Mesh, PartitionSpec as P

BF16, F32, I32 = jnp.bfloat16, jnp.float32, jnp.int32

XL, Z, CORE, TP = 2, 8, 2, 8
REP = XL * Z * CORE

HD = 128
SLOTS = 16
STEPS = 2
HEADS = 8
CTX = 256
MOVE = 13
STAY = SLOTS - MOVE
COLS = 40
OUT_COLS = COLS // TP
OWN = 10
ROWS = SLOTS * STEPS
PACK = STEPS * HEADS + 2 * STEPS

ROUND, PAIR_ROUND, ME, HEAD, COL, SCALE, DEP = 0, 1, 2, 3, 13, 23, 33

SLOT_OF, PEER_OF, HEAD_OF = 0, 2 * SLOTS, 4 * SLOTS
COL_OF = HEAD_OF + 2 * Z * OWN
TABLE = COL_OF + 2 * Z * OWN

VMEM_LIMIT = 16 * 1024 * 1024


def smem():
    return pl.BlockSpec(memory_space=pltpu.SMEM)


def vmem():
    return pl.BlockSpec(memory_space=pltpu.VMEM)


def hbm():
    return pl.BlockSpec(memory_space=pltpu.HBM)


def call(body, out_shape, in_specs, scratch=(), out_specs=None, **kw):
    single = not isinstance(out_shape, (list, tuple))
    return pl.pallas_call(
        body,
        out_shape=out_shape,
        in_specs=in_specs,
        out_specs=out_specs or (vmem() if single else [vmem()] * len(out_shape)),
        scratch_shapes=list(scratch),
        compiler_params=pltpu.CompilerParams(vmem_limit_bytes=VMEM_LIMIT),
        **kw,
    )


def copy_in(pairs, sems):
    copies = [pltpu.make_async_copy(a, b, sems.at[i]) for i, (a, b) in enumerate(pairs)]
    for c in copies:
        c.start()
    for c in copies:
        c.wait()


def notice_body(place, *refs):
    given, notice, held, sems = refs[:4], refs[4], refs[5:9], refs[9]
    copy_in(zip(given, held), sems)
    dep, dest, ids, scales = held
    row = lax.broadcasted_iota(I32, (REP, HD), 0)
    lane = lax.broadcasted_iota(I32, (REP, HD), 1)
    base = place[0]
    pair_row = lax.rem(row + REP // XL, REP)
    out = jnp.where(lane == ME, row, -1).astype(F32)
    for k in range(MOVE):
        out = jnp.where((lane == ROUND) & (row == dest[0, k]), float(k), out)
        out = jnp.where((lane == PAIR_ROUND) & (pair_row == dest[0, k]), float(k), out)
        out = jnp.where(lane == DEP + k, dep[0, k].astype(F32), out)
    for n in range(OWN):
        place_n = ids[n] - base
        head = lax.div(place_n, COLS)
        out = jnp.where(lane == HEAD + n, head.astype(F32), out)
        out = jnp.where(lane == COL + n, (place_n - head * COLS).astype(F32), out)
        out = jnp.where(lane == SCALE + n, scales[n], out)
    notice[:, 0, :] = out


def at(notices, rep, lane):
    return notices[rep, 0, lane].astype(I32)


def pull_body(notices, packs, out):
    for peer in range(REP):
        out[peer] = packs[jnp.maximum(at(notices, peer, ROUND), 0)]


def score(pack, keys, length):
    per = STEPS * HEADS
    sc = lax.dot_general(
        pack[:per], keys, (((1,), (1,)), ((), ())), preferred_element_type=F32
    )
    pos = lax.broadcasted_iota(I32, (per, CTX), 1)
    return jnp.where(pos < length, sc * (1.0 / math.sqrt(HD)), -jnp.inf)


def blend(pack, sc, values):
    per = STEPS * HEADS
    step = lax.broadcasted_iota(I32, (per, 1), 0) // HEADS
    top = jnp.max(sc, axis=1, keepdims=True)
    expo = jnp.exp(sc - top)
    total = jnp.sum(expo, axis=1, keepdims=True)
    carried = jnp.dot(expo.astype(BF16), values, preferred_element_type=F32)
    pack = pack.astype(F32)
    q = pack[:per]
    peak = top
    extra = []
    for u in range(STEPS):
        f = jnp.sum(q * pack[per + 2 * u : per + 2 * u + 1], axis=1, keepdims=True)
        f = jnp.where(step >= u, f * (1.0 / math.sqrt(HD)), -jnp.inf)
        extra.append(f)
        peak = jnp.maximum(peak, f)
    factor = jnp.exp(top - peak)
    denom = total * factor
    numer = carried * factor
    for u in range(STEPS):
        w = jnp.exp(extra[u] - peak)
        denom = denom + w
        numer = numer + w * pack[per + 2 * u + 1 : per + 2 * u + 2]
    return (numer / denom).astype(BF16)


def stay_body(dep_in, dest_in, lengths_in, q_in, fresh_in, cache, out, packs, lists, *scratch):
    dep, dest, lengths, queries, fresh, held, leaves, mine, sems = scratch
    given = zip((dep_in, dest_in, lengths_in, q_in, fresh_in), (dep, dest, lengths, queries, fresh))
    copy_in(given, sems.at[SLOTS:])
    for k in range(MOVE):
        lists[k] = dep[0, k]
        lists[SLOTS + k] = dest[0, k]
        lists[2 * SLOTS + k] = lengths[dep[0, k]]
    for s in range(SLOTS):
        leaves[s] = 0
    for k in range(MOVE):
        leaves[dep[0, k]] = 1

    def copy(s):
        return pltpu.make_async_copy(cache.at[s], held.at[s], sems.at[s])

    def start(s, carry):
        @pl.when(leaves[s] == 0)
        def _():
            copy(s).start()

        return carry

    def one(s, carry):
        @pl.when(leaves[s] == 0)
        def _():
            copy(s).wait()
            pack = mine[s]
            sc = score(pack, held[s, 0, :, :HD], lengths[s])
            out[s] = blend(pack, sc, held[s, 0, :, HD:])

        return carry

    lax.fori_loop(0, SLOTS, start, 0)
    for s in range(SLOTS):
        mine[s] = jnp.concatenate(
            [queries[t, s] for t in range(STEPS)]
            + [fresh[t, s : s + 1, j * HD : (j + 1) * HD] for t in range(STEPS) for j in range(2)],
            axis=0,
        )
    for k in range(MOVE):
        packs[k] = mine[dep[0, k]]
    lax.fori_loop(0, SLOTS, one, 0)


def attend_body(lists, pulled, cache, send, scores):
    per = STEPS * HEADS
    slots = [lists[k] for k in range(MOVE)]
    goals = [lists[SLOTS + k] for k in range(MOVE)]
    for k in range(MOVE):
        length = lists[2 * SLOTS + k]
        scores[k] = score(pulled[goals[k]], cache[slots[k], 0, :, :HD], length)
    for k in range(MOVE):
        rows = blend(pulled[goals[k]], scores[k], cache[slots[k], 0, :, HD:])
        send[goals[k], :per, :] = rows
        send[lax.rem(goals[k] + REP // XL, REP), per:, :] = rows


def add_blocks(table, scales, rows, total, blocks, first):
    for lo in range(first, first + OWN, 5):
        products = [
            jnp.dot(rows[table[HEAD_OF + n]], blocks[n - first], preferred_element_type=F32)
            * scales[n]
            for n in range(lo, lo + 5)
        ]
        for n in range(lo, lo + 5):
            total[table[COL_OF + n]] += products[n - lo]


def table_body(notices, table, scales):
    me = at(notices, 0, ME)
    pair = lax.rem(me + REP // XL, REP)
    for side, owner, lane in ((0, me, ROUND), (1, pair, PAIR_ROUND)):
        for k in range(MOVE):
            table[SLOT_OF + side * SLOTS + k] = at(notices, owner, DEP + k)
        for peer in range(REP):
            turn = at(notices, peer, lane)
            table[PEER_OF + side * SLOTS + jnp.where(turn >= 0, turn, SLOTS - 1)] = peer
    xl, z, core = lax.div(me, Z * CORE), lax.rem(lax.div(me, CORE), Z), lax.rem(me, CORE)
    half = Z // 2
    for i, (step, line, cross) in enumerate(
        [(0, 0, 0), (0, 0, 1)]
        + [(j, 0, cross) for cross in (0, 1) for j in range(1, half)]
        + [(j, 1, cross) for cross in (0, 1) for j in range(1, half)]
        + [(half, 0, 0), (half, 0, 1)]
    ):
        on = core if line == 0 else 1 - core
        origin = on if cross == 0 else 1 - on
        far = lax.rem(z - (1 - 2 * on) * step + Z, Z)
        src = (xl * Z + far) * CORE + origin
        for n in range(OWN):
            table[HEAD_OF + i * OWN + n] = at(notices, src, HEAD + n)
            table[COL_OF + i * OWN + n] = at(notices, src, COL + n)
            scales[i * OWN + n] = notices[src, 0, SCALE + n]


def project_body(where, table, scales, came, mine, other, *rest):
    arrays, rows, total, slots = rest[:-3], rest[-3], rest[-2], rest[-1]
    per = STEPS * HEADS
    xl = where[0]
    for side, here, start in ((0, mine, xl * SLOTS), (1, other, (1 - xl) * SLOTS)):
        for s in range(SLOTS):
            slots[pl.ds(pl.multiple_of((start + s) * per, per), per), :] = here[s].astype(F32)
        for k in range(MOVE):
            rows_k = came[table[PEER_OF + side * SLOTS + k], side * per : (side + 1) * per, :]
            goal = start + table[SLOT_OF + side * SLOTS + k]
            slots[pl.ds(pl.multiple_of(goal * per, per), per), :] = rows_k.astype(F32)
    for h in range(HEADS):
        for side in range(XL):
            for t in range(STEPS):
                lo = side * ROWS + t * SLOTS
                rows[h, lo : lo + SLOTS, :] = slots[
                    pl.ds(side * SLOTS * per + t * HEADS + h, SLOTS, stride=per), :
                ].astype(BF16)
    total[...] = jnp.zeros_like(total)
    for i, blocks in enumerate(arrays):
        add_blocks(table, scales, rows, total, blocks, i * OWN)


def last_body(table, scales, rows, so_far, four, four_x, out, total):
    total[...] = so_far[...]
    add_blocks(table, scales, rows, total, four, (2 * Z - 2) * OWN)
    add_blocks(table, scales, rows, total, four_x, (2 * Z - 1) * OWN)
    out[:COLS] = total[:, :ROWS, :].astype(BF16)
    out[COLS:] = total[:, ROWS:, :].astype(BF16)


def sum_body(parts, out):
    for c in range(OUT_COLS):
        acc = parts[0, c].astype(F32)
        for t in range(1, XL * TP):
            acc = acc + parts[t, c].astype(F32)
        acc = acc.astype(BF16)
        for t in range(STEPS):
            out[t, :, c * HD : (c + 1) * HD] = acc[t * SLOTS : (t + 1) * SLOTS, :]


def shards(kv_cache, lengths, departing, destination, queries, new_kv, codes, scales, block_slot):
    rep_axes, tp_axes = ("xl", "z", "core"), ("y", "xh")
    base = lax.axis_index(tp_axes) * (HEADS * COLS)
    xl = lax.axis_index("xl").astype(I32)
    per = STEPS * HEADS

    def in_hbm(x):
        return pltpu.with_memory_space_constraint(x, pltpu.HBM)

    def exchange(x, axes):
        return lax.all_to_all(x, axes, split_axis=0, concat_axis=0, tiled=True)

    def swap(x, axis):
        return lax.ppermute(x, axis, [(0, 1), (1, 0)])

    def around(x, cross=0):
        pairs = []
        for i in range(Z):
            for c in range(CORE):
                line = (c + cross) % CORE
                pairs.append((i * CORE + c, ((i + 1 - 2 * line) % Z) * CORE + line))
        return lax.ppermute(x, ("z", "core"), pairs)

    sib = swap(codes, "core")
    given = [departing, destination, block_slot, scales]
    notice = call(
        notice_body,
        jax.ShapeDtypeStruct((REP, 1, HD), F32),
        [smem()] + [hbm()] * len(given),
        [pltpu.SMEM(a.shape, a.dtype) for a in given] + [pltpu.SemaphoreType.DMA((len(given),))],
    )(base.astype(I32)[None], *(in_hbm(a) for a in given))
    cache = in_hbm(kv_cache)
    sib, notice = lax.optimization_barrier((sib, notice))
    near, near_x = around(codes), around(sib)
    notices = exchange(notice, rep_axes)
    fresh = new_kv.reshape(STEPS, SLOTS, 2 * HD)
    stays, packs, lists = call(
        stay_body,
        [
            jax.ShapeDtypeStruct((SLOTS, per, HD), BF16),
            jax.ShapeDtypeStruct((MOVE, PACK, HD), BF16),
            jax.ShapeDtypeStruct((3 * SLOTS,), I32),
        ],
        [hbm()] * 6,
        [
            pltpu.SMEM(departing.shape, I32),
            pltpu.SMEM(destination.shape, I32),
            pltpu.SMEM(lengths.shape, I32),
            pltpu.VMEM(queries.shape, BF16),
            pltpu.VMEM(fresh.shape, BF16),
            pltpu.VMEM(kv_cache.shape, BF16),
            pltpu.SMEM((SLOTS,), I32),
            pltpu.VMEM((SLOTS, PACK, HD), BF16),
            pltpu.SemaphoreType.DMA((SLOTS + 5,)),
        ],
        out_specs=[vmem(), vmem(), smem()],
    )(*(in_hbm(a) for a in (departing, destination, lengths, queries, fresh)), cache)
    near, stays = lax.optimization_barrier((near, stays))
    near_x, notices = lax.optimization_barrier((near_x, notices))
    two, two_x = around(near), around(near_x)
    other = swap(stays, "xl")
    table, factors = call(
        table_body,
        [jax.ShapeDtypeStruct((TABLE,), I32), jax.ShapeDtypeStruct((2 * Z * OWN,), F32)],
        [smem()],
        out_specs=[smem(), smem()],
    )(notices)
    to_pull = call(
        pull_body, jax.ShapeDtypeStruct((REP, PACK, HD), BF16), [smem(), vmem()]
    )(notices, packs)
    pulled = exchange(to_pull, rep_axes)
    other, pulled = lax.optimization_barrier((other, pulled))
    three, three_x = around(two), around(two_x)
    send = call(
        attend_body,
        jax.ShapeDtypeStruct((REP, 2 * per, HD), BF16),
        [smem()] + [vmem()] * 2,
        [pltpu.VMEM((MOVE, per, CTX), F32)],
    )(lists, pulled, kv_cache)
    came = exchange(send, rep_axes)
    four = around(three)
    rows, total = call(
        project_body,
        [
            jax.ShapeDtypeStruct((HEADS, XL * ROWS, HD), BF16),
            jax.ShapeDtypeStruct((COLS, XL * ROWS, HD), F32),
        ],
        [smem()] * 3 + [vmem()] * 17,
        [pltpu.VMEM((XL * SLOTS * per, HD), F32)],
    )(
        *(xl[None], table, factors, came, stays, other),
        *(codes, sib, near, two, three, near_x, two_x, three_x),
        *(swap(x, "core") for x in (near, two, three, near_x, two_x, three_x)),
    )
    four, rows = lax.optimization_barrier((four, rows))
    four_x = swap(four, "core")
    parts = call(
        last_body,
        jax.ShapeDtypeStruct((XL * COLS, ROWS, HD), BF16),
        [smem()] * 2 + [vmem()] * 4,
        [pltpu.VMEM((COLS, XL * ROWS, HD), F32)],
    )(table, factors, rows, total, four, four_x)
    parts = exchange(parts, ("xl",) + tp_axes).reshape(XL * TP, OUT_COLS, ROWS, HD)
    return call(
        sum_body, jax.ShapeDtypeStruct((STEPS, SLOTS, OUT_COLS * HD), BF16), [vmem()]
    )(parts)


def solution(mesh):
    rep, tp = ("xl", "z", "core"), ("y", "xh")
    parts = Mesh(mesh.devices.reshape(XL, Z, CORE, 4, 2), rep + tp)
    placed = (
        P(rep, tp, None, None),
        P(rep),
        P(rep, None),
        P(rep, None),
        P(None, rep, tp, None),
        P(None, rep, tp, None),
        P(tp + rep, None, None),
        P(tp + rep),
        P(tp + rep),
    )
    return jax.shard_map(
        shards, mesh=parts, in_specs=placed, out_specs=P(None, rep, tp), check_vma=False
    )
```

```python
import math

import jax
import jax.numpy as jnp
from jax import lax
from jax.experimental import pallas as pl
from jax.experimental.pallas import tpu as pltpu
from jax.sharding import Mesh, PartitionSpec as P

BF16, F32, I32 = jnp.bfloat16, jnp.float32, jnp.int32

XL, Z, CORE, TP = 2, 8, 2, 8
REP = XL * Z * CORE

HD = 128
SLOTS = 16
STEPS = 2
HEADS = 8
CTX = 256
MOVE = 13
STAY = SLOTS - MOVE
COLS = 40
OUT_COLS = COLS // TP
OWN = 10
ROWS = SLOTS * STEPS
PACK = STEPS * HEADS + 2 * STEPS

ROUND, PAIR_ROUND, ME, HEAD, COL, SCALE, DEP = 0, 1, 2, 3, 13, 23, 33

SLOT_OF, PEER_OF, HEAD_OF = 0, 2 * SLOTS, 4 * SLOTS
COL_OF = HEAD_OF + 2 * Z * OWN
TABLE = COL_OF + 2 * Z * OWN

VMEM_LIMIT = 10 * 1024 * 1024


def smem():
    return pl.BlockSpec(memory_space=pltpu.SMEM)


def vmem():
    return pl.BlockSpec(memory_space=pltpu.VMEM)


def hbm():
    return pl.BlockSpec(memory_space=pltpu.HBM)


def call(body, out_shape, in_specs, scratch=(), out_specs=None, **kw):
    single = not isinstance(out_shape, (list, tuple))
    return pl.pallas_call(
        body,
        out_shape=out_shape,
        in_specs=in_specs,
        out_specs=out_specs or (vmem() if single else [vmem()] * len(out_shape)),
        scratch_shapes=list(scratch),
        compiler_params=pltpu.CompilerParams(vmem_limit_bytes=VMEM_LIMIT),
        **kw,
    )


def copy_in(pairs, sems):
    copies = [pltpu.make_async_copy(a, b, sems.at[i]) for i, (a, b) in enumerate(pairs)]
    for c in copies:
        c.start()
    for c in copies:
        c.wait()


def notice_body(place, *refs):
    given, notice, held, sems = refs[:4], refs[4], refs[5:9], refs[9]
    copy_in(zip(given, held), sems)
    dep, dest, ids, scales = held
    row = lax.broadcasted_iota(I32, (REP, HD), 0)
    lane = lax.broadcasted_iota(I32, (REP, HD), 1)
    base = place[0]
    pair_row = lax.rem(row + REP // XL, REP)
    out = jnp.where(lane == ME, row, -1).astype(F32)
    for k in range(MOVE):
        out = jnp.where((lane == ROUND) & (row == dest[0, k]), float(k), out)
        out = jnp.where((lane == PAIR_ROUND) & (pair_row == dest[0, k]), float(k), out)
        out = jnp.where(lane == DEP + k, dep[0, k].astype(F32), out)
    for n in range(OWN):
        place_n = ids[n] - base
        head = lax.div(place_n, COLS)
        out = jnp.where(lane == HEAD + n, head.astype(F32), out)
        out = jnp.where(lane == COL + n, (place_n - head * COLS).astype(F32), out)
        out = jnp.where(lane == SCALE + n, scales[n], out)
    notice[:, 0, :] = out


def at(notices, rep, lane):
    return notices[rep, 0, lane].astype(I32)


def pull_body(notices, packs, out):
    for peer in range(REP):
        out[peer] = packs[jnp.maximum(at(notices, peer, ROUND), 0)]


def score(pack, keys, length):
    per = STEPS * HEADS
    sc = lax.dot_general(
        pack[:per], keys, (((1,), (1,)), ((), ())), preferred_element_type=F32
    )
    pos = lax.broadcasted_iota(I32, (per, CTX), 1)
    return jnp.where(pos < length, sc * (1.0 / math.sqrt(HD)), -jnp.inf)


def blend(pack, sc, values):
    per = STEPS * HEADS
    step = lax.broadcasted_iota(I32, (per, 1), 0) // HEADS
    top = jnp.max(sc, axis=1, keepdims=True)
    expo = jnp.exp(sc - top)
    total = jnp.sum(expo, axis=1, keepdims=True)
    carried = jnp.dot(expo.astype(BF16), values, preferred_element_type=F32)
    pack = pack.astype(F32)
    q = pack[:per]
    peak = top
    extra = []
    for u in range(STEPS):
        f = jnp.sum(q * pack[per + 2 * u : per + 2 * u + 1], axis=1, keepdims=True)
        f = jnp.where(step >= u, f * (1.0 / math.sqrt(HD)), -jnp.inf)
        extra.append(f)
        peak = jnp.maximum(peak, f)
    factor = jnp.exp(top - peak)
    denom = total * factor
    numer = carried * factor
    for u in range(STEPS):
        w = jnp.exp(extra[u] - peak)
        denom = denom + w
        numer = numer + w * pack[per + 2 * u + 1 : per + 2 * u + 2]
    return (numer / denom).astype(BF16)


def stay_body(dep_in, dest_in, lengths_in, q_in, fresh_in, cache, out, packs, lists, *scratch):
    dep, dest, lengths, queries, fresh, held, leaves, mine, sems = scratch
    given = zip((dep_in, dest_in, lengths_in, q_in, fresh_in), (dep, dest, lengths, queries, fresh))
    copy_in(given, sems.at[SLOTS:])
    for k in range(MOVE):
        lists[k] = dep[0, k]
        lists[SLOTS + k] = dest[0, k]
        lists[2 * SLOTS + k] = lengths[dep[0, k]]
    for s in range(SLOTS):
        leaves[s] = 0
    for k in range(MOVE):
        leaves[dep[0, k]] = 1

    def copy(s):
        return pltpu.make_async_copy(cache.at[s], held.at[s], sems.at[s])

    def start(s, carry):
        @pl.when(leaves[s] == 0)
        def _():
            copy(s).start()

        return carry

    def one(s, carry):
        @pl.when(leaves[s] == 0)
        def _():
            copy(s).wait()
            pack = mine[s]
            sc = score(pack, held[s, 0, :, :HD], lengths[s])
            out[s] = blend(pack, sc, held[s, 0, :, HD:])

        return carry

    lax.fori_loop(0, SLOTS, start, 0)
    for s in range(SLOTS):
        mine[s] = jnp.concatenate(
            [queries[t, s] for t in range(STEPS)]
            + [fresh[t, s : s + 1, j * HD : (j + 1) * HD] for t in range(STEPS) for j in range(2)],
            axis=0,
        )
    for k in range(MOVE):
        packs[k] = mine[dep[0, k]]
    lax.fori_loop(0, SLOTS, one, 0)


def attend_body(lists, pulled, cache, send, scores):
    per = STEPS * HEADS
    slots = [lists[k] for k in range(MOVE)]
    goals = [lists[SLOTS + k] for k in range(MOVE)]
    for k in range(MOVE):
        length = lists[2 * SLOTS + k]
        scores[k] = score(pulled[goals[k]], cache[slots[k], 0, :, :HD], length)
    for k in range(MOVE):
        rows = blend(pulled[goals[k]], scores[k], cache[slots[k], 0, :, HD:])
        send[goals[k], :per, :] = rows
        send[lax.rem(goals[k] + REP // XL, REP), per:, :] = rows


def add_blocks(table, scales, rows, total, blocks, first):
    for lo in range(first, first + OWN, 5):
        products = [
            jnp.dot(rows[table[HEAD_OF + n]], blocks[n - first], preferred_element_type=F32)
            * scales[n]
            for n in range(lo, lo + 5)
        ]
        for n in range(lo, lo + 5):
            total[table[COL_OF + n]] += products[n - lo]


def table_body(notices, table, scales):
    me = at(notices, 0, ME)
    pair = lax.rem(me + REP // XL, REP)
    for side, owner, lane in ((0, me, ROUND), (1, pair, PAIR_ROUND)):
        for k in range(MOVE):
            table[SLOT_OF + side * SLOTS + k] = at(notices, owner, DEP + k)
        for peer in range(REP):
            turn = at(notices, peer, lane)
            table[PEER_OF + side * SLOTS + jnp.where(turn >= 0, turn, SLOTS - 1)] = peer
    xl, z, core = lax.div(me, Z * CORE), lax.rem(lax.div(me, CORE), Z), lax.rem(me, CORE)
    half = Z // 2
    for i, (step, line, cross) in enumerate(
        [(0, 0, 0), (0, 0, 1)]
        + [(j, 0, cross) for cross in (0, 1) for j in range(1, half)]
        + [(j, 1, cross) for cross in (0, 1) for j in range(1, half)]
        + [(half, 0, 0), (half, 0, 1)]
    ):
        on = core if line == 0 else 1 - core
        origin = on if cross == 0 else 1 - on
        far = lax.rem(z - (1 - 2 * on) * step + Z, Z)
        src = (xl * Z + far) * CORE + origin
        for n in range(OWN):
            table[HEAD_OF + i * OWN + n] = at(notices, src, HEAD + n)
            table[COL_OF + i * OWN + n] = at(notices, src, COL + n)
            scales[i * OWN + n] = notices[src, 0, SCALE + n]


def project_body(where, table, scales, came, mine, other, *rest):
    arrays, rows, total, slots = rest[:-3], rest[-3], rest[-2], rest[-1]
    per = STEPS * HEADS
    xl = where[0]
    for side, here, start in ((0, mine, xl * SLOTS), (1, other, (1 - xl) * SLOTS)):
        for s in range(SLOTS):
            slots[pl.ds(pl.multiple_of((start + s) * per, per), per), :] = here[s].astype(F32)
        for k in range(MOVE):
            rows_k = came[table[PEER_OF + side * SLOTS + k], side * per : (side + 1) * per, :]
            goal = start + table[SLOT_OF + side * SLOTS + k]
            slots[pl.ds(pl.multiple_of(goal * per, per), per), :] = rows_k.astype(F32)
    for h in range(HEADS):
        for side in range(XL):
            for t in range(STEPS):
                lo = side * ROWS + t * SLOTS
                rows[h, lo : lo + SLOTS, :] = slots[
                    pl.ds(side * SLOTS * per + t * HEADS + h, SLOTS, stride=per), :
                ].astype(BF16)
    total[...] = jnp.zeros_like(total)
    for i, blocks in enumerate(arrays):
        add_blocks(table, scales, rows, total, blocks, i * OWN)


def last_body(table, scales, rows, so_far, four, four_x, out, total):
    total[...] = so_far[...]
    add_blocks(table, scales, rows, total, four, (2 * Z - 2) * OWN)
    add_blocks(table, scales, rows, total, four_x, (2 * Z - 1) * OWN)
    out[:COLS] = total[:, :ROWS, :].astype(BF16)
    out[COLS:] = total[:, ROWS:, :].astype(BF16)


def sum_body(parts, out):
    for c in range(OUT_COLS):
        acc = parts[0, c].astype(F32)
        for t in range(1, XL * TP):
            acc = acc + parts[t, c].astype(F32)
        acc = acc.astype(BF16)
        for t in range(STEPS):
            out[t, :, c * HD : (c + 1) * HD] = acc[t * SLOTS : (t + 1) * SLOTS, :]


def shards(kv_cache, lengths, departing, destination, queries, new_kv, codes, scales, block_slot):
    rep_axes, tp_axes = ("xl", "z", "core"), ("y", "xh")
    base = lax.axis_index(tp_axes) * (HEADS * COLS)
    xl = lax.axis_index("xl").astype(I32)
    per = STEPS * HEADS

    def in_hbm(x):
        return pltpu.with_memory_space_constraint(x, pltpu.HBM)

    def exchange(x, axes):
        return lax.all_to_all(x, axes, split_axis=0, concat_axis=0, tiled=True)

    def swap(x, axis):
        return lax.ppermute(x, axis, [(0, 1), (1, 0)])

    def around(x, cross=0):
        pairs = []
        for i in range(Z):
            for c in range(CORE):
                line = (c + cross) % CORE
                pairs.append((i * CORE + c, ((i + 1 - 2 * line) % Z) * CORE + line))
        return lax.ppermute(x, ("z", "core"), pairs)

    sib = swap(codes, "core")
    given = [departing, destination, block_slot, scales]
    notice = call(
        notice_body,
        jax.ShapeDtypeStruct((REP, 1, HD), F32),
        [smem()] + [hbm()] * len(given),
        [pltpu.SMEM(a.shape, a.dtype) for a in given] + [pltpu.SemaphoreType.DMA((len(given),))],
    )(base.astype(I32)[None], *(in_hbm(a) for a in given))
    cache = in_hbm(kv_cache)
    sib, notice = lax.optimization_barrier((sib, notice))
    near, near_x = around(codes), around(sib)
    notices = exchange(notice, rep_axes)
    fresh = new_kv.reshape(STEPS, SLOTS, 2 * HD)
    stays, packs, lists = call(
        stay_body,
        [
            jax.ShapeDtypeStruct((SLOTS, per, HD), BF16),
            jax.ShapeDtypeStruct((MOVE, PACK, HD), BF16),
            jax.ShapeDtypeStruct((3 * SLOTS,), I32),
        ],
        [hbm()] * 6,
        [
            pltpu.SMEM(departing.shape, I32),
            pltpu.SMEM(destination.shape, I32),
            pltpu.SMEM(lengths.shape, I32),
            pltpu.VMEM(queries.shape, BF16),
            pltpu.VMEM(fresh.shape, BF16),
            pltpu.VMEM(kv_cache.shape, BF16),
            pltpu.SMEM((SLOTS,), I32),
            pltpu.VMEM((SLOTS, PACK, HD), BF16),
            pltpu.SemaphoreType.DMA((SLOTS + 5,)),
        ],
        out_specs=[vmem(), vmem(), smem()],
    )(*(in_hbm(a) for a in (departing, destination, lengths, queries, fresh)), cache)
    near, stays = lax.optimization_barrier((near, stays))
    near_x, notices = lax.optimization_barrier((near_x, notices))
    two, two_x = around(near), around(near_x)
    other = swap(stays, "xl")
    table, factors = call(
        table_body,
        [jax.ShapeDtypeStruct((TABLE,), I32), jax.ShapeDtypeStruct((2 * Z * OWN,), F32)],
        [smem()],
        out_specs=[smem(), smem()],
    )(notices)
    to_pull = call(
        pull_body, jax.ShapeDtypeStruct((REP, PACK, HD), BF16), [smem(), vmem()]
    )(notices, packs)
    pulled = exchange(to_pull, rep_axes)
    three, three_x = around(two), around(two_x)
    send = call(
        attend_body,
        jax.ShapeDtypeStruct((REP, 2 * per, HD), BF16),
        [smem()] + [vmem()] * 2,
        [pltpu.VMEM((MOVE, per, CTX), F32)],
    )(lists, pulled, kv_cache)
    came = exchange(send, rep_axes)
    four, four_x = around(three), around(three_x)
    rows, total = call(
        project_body,
        [
            jax.ShapeDtypeStruct((HEADS, XL * ROWS, HD), BF16),
            jax.ShapeDtypeStruct((COLS, XL * ROWS, HD), F32),
        ],
        [smem()] * 3 + [vmem()] * 17,
        [pltpu.VMEM((XL * SLOTS * per, HD), F32)],
    )(
        *(xl[None], table, factors, came, stays, other),
        *(codes, sib, near, two, three, near_x, two_x, three_x),
        *(swap(x, "core") for x in (near, two, three, near_x, two_x, three_x)),
    )
    parts = call(
        last_body,
        jax.ShapeDtypeStruct((XL * COLS, ROWS, HD), BF16),
        [smem()] * 2 + [vmem()] * 4,
        [pltpu.VMEM((COLS, XL * ROWS, HD), F32)],
    )(table, factors, rows, total, four, four_x)
    parts = exchange(parts, ("xl",) + tp_axes).reshape(XL * TP, OUT_COLS, ROWS, HD)
    return call(
        sum_body, jax.ShapeDtypeStruct((STEPS, SLOTS, OUT_COLS * HD), BF16), [vmem()]
    )(parts)


def solution(mesh):
    rep, tp = ("xl", "z", "core"), ("y", "xh")
    parts = Mesh(mesh.devices.reshape(XL, Z, CORE, 4, 2), rep + tp)
    placed = (
        P(rep, tp, None, None),
        P(rep),
        P(rep, None),
        P(rep, None),
        P(None, rep, tp, None),
        P(None, rep, tp, None),
        P(tp + rep, None, None),
        P(tp + rep),
        P(tp + rep),
    )
    return jax.shard_map(
        shards, mesh=parts, in_specs=placed, out_specs=P(None, rep, tp), check_vma=False
    )
```
